128 devices in a mesh: dp: 16 (over y_hi, x, core), tensor: 8 (over y_lo, z).
Axes of the slice: x: 4, y: 4 (y_hi: 2, y_lo: 2; y = y_hi * 2 + y_lo), z: 4, core: 2. Of those that a mesh axis runs over, the one named last changes fastest.
Arguments:
- tokens: bfloat16 [16, 1024, 2048], P('dp', 'tensor'), may hold values from -6 to 6
- lengths: int32 [16], P('dp'), may hold values from 897 to 1024, as said below
- w_query: bfloat16 [2048, 2048], P('dp', 'tensor'), may hold values from -0.125 to 0.125
- w_key: bfloat16 [2048, 2048], P('dp', 'tensor'), may hold values from -0.125 to 0.125
- w_value: bfloat16 [2048, 2048], P('dp', 'tensor'), may hold values from -0.125 to 0.125
- w_out: bfloat16 [2048, 2048], P('tensor', 'dp'), may hold values from -0.125 to 0.125
- w_gate: bfloat16 [2048, 8192], P('dp', 'tensor'), may hold values from -0.125 to 0.125
- w_up: bfloat16 [2048, 8192], P('dp', 'tensor'), may hold values from -0.125 to 0.125
- w_down: bfloat16 [8192, 2048], P('tensor', 'dp'), may hold values from -0.0625 to 0.0625
- q_gain: float32 [2048], replicated, may hold values from 0.25 to 1.75
- k_gain: float32 [2048], replicated, may hold values from 0.25 to 1.75
- attn_gain: float32 [2048], replicated, may hold values from 0.25 to 1.75
- mlp_gain: float32 [2048], replicated, may hold values from 0.25 to 1.75
- cotangent: bfloat16 [16, 1024, 2048], P('dp', 'tensor'), may hold values from -6 to 6
Outputs:
- activations: bfloat16 [16, 1024, 2048], P('dp', 'tensor')
- input_grad: float32 [16, 1024, 2048], P('dp', 'tensor')
- w_query_grad: float32 [2048, 2048], P('dp', 'tensor')
- w_key_grad: float32 [2048, 2048], P('dp', 'tensor')
- w_value_grad: float32 [2048, 2048], P('dp', 'tensor')
- w_out_grad: float32 [2048, 2048], P('tensor', 'dp')
- w_gate_grad: float32 [2048, 8192], P('dp', 'tensor')
- w_up_grad: float32 [2048, 8192], P('dp', 'tensor')
- w_down_grad: float32 [8192, 2048], P('tensor', 'dp')
- q_gain_grad: float32 [2048], replicated
- k_gain_grad: float32 [2048], replicated
- attn_gain_grad: float32 [2048], replicated
- mlp_gain_grad: float32 [2048], replicated
The draws below stay inside these ranges and needn't reach their ends.
Inputs may be any that keep to these rules, and one draw needn't show every extreme that they name: `lengths`: one sequence of the batch, drawn from the seed, has length 1024; every other sequence is shorter.
All inputs are finite; a program needn't handle non-finite values.
Results may differ from the reference program's by a relative error of at most 0.024.
Values may be sent and summed in bfloat16 or wider, within the bound.
A program may use at most 192 MiB of HBM per device.

```python
import jax
import jax.numpy as jnp
from jax import lax

MODEL_WIDTH = 2048
HEADS = 16
HEAD_DIM = 128
FF = 8192
LEN = 1024
BATCH = 16
SHORTEST = 897


def draw_lengths(key, part):
    key = jax.random.fold_in(key, 11)
    first_key, second_key = jax.random.split(key)
    base_len = jax.random.randint(first_key, (BATCH,), SHORTEST, LEN)
    chosen_row = jax.random.randint(second_key, (), 0, BATCH)
    longest = jnp.arange(BATCH) == chosen_row
    return jnp.where(longest, LEN, base_len).astype(jnp.int32)


def shard_levels(stream_key, dims, cuts, least, largest):
    loudness = 1.0
    for dim, blocks in cuts:
        heights = jax.random.uniform(jax.random.fold_in(jax.random.fold_in(stream_key, 6), dim), (blocks,), jnp.float32, least / len(cuts), largest / len(cuts))
        loudness = loudness * jnp.repeat(jnp.exp(heights), dims[dim] // blocks).reshape((-1,) + (1,) * (len(dims) - 1 - dim))
    return loudness


def gaussian(own_key, extent, scale, most, cuts=(), kind=jnp.bfloat16):
    result = scale * jax.random.normal(own_key, extent, jnp.float32)
    if cuts:
        result = result * shard_levels(own_key, extent, cuts, -0.22, 0.18)
    return jnp.clip(result, -most, most).astype(kind)


def setup_inputs(seed: int = 0) -> dict:
    arg_keys = jax.random.split(jax.random.key(seed), 15)
    tokens = gaussian(arg_keys[0], (BATCH, LEN, MODEL_WIDTH), 1.0, 6.0, ((0, 16), (1, 8)))
    lengths = draw_lengths(jax.random.fold_in(arg_keys[14], 71), 0)
    w_query = gaussian(arg_keys[2], (MODEL_WIDTH, MODEL_WIDTH), MODEL_WIDTH ** -0.5, 0.125, ((0, 16), (1, 8)))
    w_key = gaussian(arg_keys[3], (MODEL_WIDTH, MODEL_WIDTH), MODEL_WIDTH ** -0.5, 0.125, ((0, 16), (1, 8)))
    w_value = gaussian(arg_keys[4], (MODEL_WIDTH, MODEL_WIDTH), MODEL_WIDTH ** -0.5, 0.125, ((0, 16), (1, 8)))
    w_out = gaussian(arg_keys[5], (MODEL_WIDTH, MODEL_WIDTH), MODEL_WIDTH ** -0.5, 0.125, ((0, 8), (1, 16)))
    w_gate = gaussian(arg_keys[6], (MODEL_WIDTH, FF), MODEL_WIDTH ** -0.5, 0.125, ((0, 16), (1, 8)))
    w_up = gaussian(arg_keys[7], (MODEL_WIDTH, FF), MODEL_WIDTH ** -0.5, 0.125, ((0, 16), (1, 8)))
    w_down = gaussian(arg_keys[8], (FF, MODEL_WIDTH), FF ** -0.5, 0.0625, ((0, 8), (1, 16)))
    q_gain = jnp.clip(1.0 + 0.15 * jax.random.normal(arg_keys[9], (MODEL_WIDTH,), jnp.float32), 0.25, 1.75)
    k_gain = jnp.clip(1.0 + 0.15 * jax.random.normal(arg_keys[10], (MODEL_WIDTH,), jnp.float32), 0.25, 1.75)
    attn_gain = jnp.clip(1.0 + 0.15 * jax.random.normal(arg_keys[11], (MODEL_WIDTH,), jnp.float32), 0.25, 1.75)
    mlp_gain = jnp.clip(1.0 + 0.15 * jax.random.normal(arg_keys[12], (MODEL_WIDTH,), jnp.float32), 0.25, 1.75)
    cotangent = gaussian(arg_keys[13], (BATCH, LEN, MODEL_WIDTH), 1.0, 6.0, ((0, 16), (1, 8)))
    return dict(tokens=tokens, lengths=lengths, w_query=w_query, w_key=w_key, w_value=w_value, w_out=w_out, w_gate=w_gate, w_up=w_up, w_down=w_down, q_gain=q_gain, k_gain=k_gain, attn_gain=attn_gain, mlp_gain=mlp_gain, cotangent=cotangent)


EPS = 1e-06
THETA = 500000.0
HIGH_PRECISION = lax.Precision.HIGHEST

@jax.custom_vjp
def lower_precision(v):
    return lax.optimization_barrier(v.astype(jnp.bfloat16)).astype(jnp.float32)

@jax.custom_vjp
def lower_precision_backward(v):
    return v

def low_keep(v):
    return (lower_precision(v), None)

def low_pass(kept, grad):
    return (grad,)

def back_keep(v):
    return (v, None)

def back_low(kept, grad):
    return (lower_precision(grad),)
lower_precision.defvjp(low_keep, low_pass)
lower_precision_backward.defvjp(back_keep, back_low)

def matmul(left, right):
    return jnp.dot(left, right, precision=HIGH_PRECISION, preferred_element_type=jnp.float32)

def rope_tables(count, size):
    half_size = size // 2
    frequency = THETA ** (-(jnp.arange(half_size, dtype=jnp.float32) * 2.0 / size))
    angles = jnp.arange(count, dtype=jnp.float32)[:, None] * frequency[None, :]
    return (jnp.cos(angles), jnp.sin(angles))

def rotate(values, cosine, sine_table):
    half_size = values.shape[-1] // 2
    first_half = values[..., :half_size]
    second_half = values[..., half_size:]
    cos_b = cosine[:, None, :]
    sin_b = sine_table[:, None, :]
    return jnp.concatenate([first_half * cos_b - second_half * sin_b, second_half * cos_b + first_half * sin_b], -1)

def rms_scale(values):
    return lax.rsqrt(lax.optimization_barrier(jnp.mean(values * values, -1, keepdims=True)) + EPS)

def forward_one(x_val, param_set, length):
    w_query, w_key, w_value, w_out, w_gate, w_up, w_down, q_gain, k_gain, attn_gain, mlp_gain = param_set
    sequence_length = x_val.shape[0]
    q_raw = lower_precision_backward(matmul(x_val, w_query))
    k_raw = lower_precision_backward(matmul(x_val, w_key))
    v_raw = lower_precision_backward(matmul(x_val, w_value))
    q_norm = q_raw * rms_scale(q_raw) * q_gain
    k_norm = k_raw * rms_scale(k_raw) * k_gain
    cosine, sine_table = rope_tables(sequence_length, HEAD_DIM)
    rotated_queries = lower_precision(rotate(q_norm.reshape(sequence_length, HEADS, HEAD_DIM), cosine, sine_table) * HEAD_DIM ** (-0.5))
    rotated_keys = lower_precision(rotate(k_norm.reshape(sequence_length, HEADS, HEAD_DIM), cosine, sine_table))
    value_lower_precision = lower_precision(v_raw).reshape(sequence_length, HEADS, HEAD_DIM)
    score_matrix = lower_precision_backward(jnp.einsum('euk,zuk->uez', rotated_queries, rotated_keys, precision=HIGH_PRECISION))
    row_pos = jnp.arange(sequence_length)[:, None]
    col_pos = jnp.arange(sequence_length)[None, :]
    allowed = (col_pos <= row_pos) & (col_pos < length)
    score_matrix = jnp.where(allowed[None], score_matrix, -1e+30)
    attention_probability = jax.nn.softmax(score_matrix, axis=-1)
    mixed_value_rows = lower_precision(lower_precision_backward(jnp.einsum('gqk,kgf->qgf', lower_precision(attention_probability), value_lower_precision, precision=HIGH_PRECISION))).reshape(sequence_length, MODEL_WIDTH)
    branch = lower_precision_backward(matmul(mixed_value_rows, w_out))
    residual = x_val + branch * rms_scale(branch) * attn_gain
    res_low = lower_precision(residual)
    gate_value = lower_precision_backward(matmul(res_low, w_gate))
    up_value = lower_precision_backward(matmul(res_low, w_up))
    inner = lower_precision(jax.nn.silu(gate_value) * up_value)
    down_value = lower_precision_backward(matmul(inner, w_down))
    valid_rows = (jnp.arange(sequence_length) < length)[:, None]
    return jnp.where(valid_rows, residual + down_value * rms_scale(down_value) * mlp_gain, 0.0)

def reference(tokens, lengths, w_query, w_key, w_value, w_out, w_gate, w_up, w_down, q_gain, k_gain, attn_gain, mlp_gain, cotangent):
    params = tuple((value_in.astype(jnp.float32) for value_in in (w_query, w_key, w_value, w_out, w_gate, w_up, w_down, q_gain, k_gain, attn_gain, mlp_gain)))

    def seq_step(totals, operands):
        row_tokens, length, row_cot = operands

        def forward_fn(x_val, param_set):
            return forward_one(x_val, param_set, length)
        result_rows, pullback = jax.vjp(forward_fn, row_tokens.astype(jnp.float32), params)
        grad_x, grad_params = pullback(row_cot.astype(jnp.float32))
        summed = tuple((left_term + right_term for left_term, right_term in zip(totals, grad_params)))
        return (summed, (result_rows.astype(jnp.bfloat16), grad_x))
    start = tuple((jnp.zeros_like(value_in) for value_in in params))
    totals, outputs = lax.scan(seq_step, start, (tokens, lengths, cotangent))
    activations, input_grad = outputs
    return (activations, input_grad, totals[0], totals[1], totals[2], totals[3], totals[4], totals[5], totals[6], totals[7], totals[8], totals[9], totals[10])
```

```python
import functools
import jax
import jax.numpy as jnp
from jax import lax
from jax.experimental import pallas as pl
from jax.experimental.pallas import tpu as pltpu
from jax.sharding import PartitionSpec as P

HEAD_DIM = 128
EPS = 1e-06
THETA = 500000.0
MESH = pl.DeviceIdType.MESH
BF16 = jnp.bfloat16
F32 = jnp.float32
ANY = pl.BlockSpec(memory_space=pl.ANY)
VM = pl.BlockSpec(memory_space=pltpu.VMEM)
CUT = 80


def place():
    d = lax.axis_index("dp")
    t = lax.axis_index("tensor")
    return d // 8, lax.rem(d // 2, 4), lax.rem(d, 2), t // 4, lax.rem(t, 4)


def other(dyh=0, dx=0, dc=0, dyl=0, dz=0):
    yh, x, c, yl, z = place()
    return (
        lax.rem(yh + dyh, 2) * 8 + lax.rem(x + dx, 4) * 2 + lax.rem(c + dc, 2),
        lax.rem(yl + dyl, 2) * 4 + lax.rem(z + dz, 4),
    )


TENSOR_PEERS = (dict(dz=1), dict(dz=2), dict(dz=3), dict(dyl=1))
DP_PEERS = (dict(dx=1), dict(dx=2), dict(dx=3), dict(dyh=1), dict(dc=1))


def greet(peers):
    barrier = pltpu.get_barrier_semaphore()
    for peer in peers:
        pl.semaphore_signal(barrier, 1, device_id=other(**peer), device_id_type=MESH)
    pl.semaphore_wait(barrier, len(peers))


def remote(src, dst, ssem, rsem, peer):
    return pltpu.make_async_remote_copy(
        src_ref=src,
        dst_ref=dst,
        send_sem=ssem,
        recv_sem=rsem,
        device_id=other(**peer),
        device_id_type=MESH,
    )


class GatherTensor:
    COPIES = 10

    def __init__(self, buf, ssem, rsem):
        yh, x, c, yl, z = place()
        me = yl * 4 + z
        pair = (1 - yl) * 4 + z
        self.own = [
            remote(buf.at[me], buf.at[me], ssem.at[i], rsem.at[i], dict(dz=i + 1)) for i in range(3)
        ]
        self.own_pair = remote(buf.at[me], buf.at[me], ssem.at[3], rsem.at[3], dict(dyl=1))
        low = pl.ds(0, CUT)
        high = pl.ds(CUT, 128 - CUT)
        self.to_pair = []
        for i in range(3):
            slot = yl * 4 + lax.rem(z + 3 - i, 4)
            block = buf.at[slot, low]
            self.to_pair.append(remote(block, block, ssem.at[4 + i], rsem.at[4 + i], dict(dyl=1)))
        block = buf.at[pair, high]
        self.from_pair = [
            remote(block, block, ssem.at[7 + i], rsem.at[7 + i], dict(dz=i + 1)) for i in range(3)
        ]

    def start(self):
        self.own_pair.start()
        for i in (0, 2, 1):
            self.own[i].start()

    def forward(self):
        self.own_pair.wait_recv()
        for copy in self.from_pair:
            copy.start()
        for i in (0, 2, 1):
            self.own[i].wait_recv()
            self.to_pair[i].start()

    def finish(self):
        for copy in self.from_pair + self.to_pair:
            copy.wait_recv()
        for copy in [self.own_pair] + self.own + self.to_pair + self.from_pair:
            copy.wait_send()


class ScatterTensor:
    COPIES = 14

    @staticmethod
    def scratch(n):
        return [
            pltpu.VMEM((4, CUT, n), BF16),
            pltpu.VMEM((3, 2, 128 - CUT, n), BF16),
            pltpu.VMEM((3, CUT, n), BF16),
            pltpu.VMEM((128 - CUT, n), BF16),
            pltpu.SemaphoreType.DMA((14,)),
            pltpu.SemaphoreType.DMA((14,)),
        ]

    def __init__(self, part, from_pair, from_z, total_z, total_pair, ssem, rsem):
        self.part, self.bufs = part, (from_pair, from_z, total_z, total_pair)
        yh, x, c, yl, z = place()
        self.yl, self.z = yl, z
        low = pl.ds(0, CUT)
        high = pl.ds(CUT, 128 - CUT)
        self.first_pair = []
        for i in range(4):
            q = lax.rem(z + i, 4)
            self.first_pair.append(
                remote(part.at[(1 - yl) * 4 + q, low], from_pair.at[i], ssem.at[i], rsem.at[i], dict(dyl=1))
            )
        self.first_z = []
        for i in range(3):
            for k in range(2):
                n = 4 + 2 * i + k
                row = lax.rem(yl + k, 2) * 4 + lax.rem(z + i + 1, 4)
                self.first_z.append(
                    remote(part.at[row, high], from_z.at[i, k], ssem.at[n], rsem.at[n], dict(dz=i + 1))
                )
        self.second_z = [
            remote(
                part.at[yl * 4 + lax.rem(z + i + 1, 4), low],
                total_z.at[i],
                ssem.at[10 + i],
                rsem.at[10 + i],
                dict(dz=i + 1),
            )
            for i in range(3)
        ]
        self.second_pair = remote(
            part.at[(1 - yl) * 4 + z, high], total_pair, ssem.at[13], rsem.at[13], dict(dyl=1)
        )

    def start(self):
        for i in (1, 3, 2, 0):
            self.first_pair[i].start()
        for k in (1, 0):
            for i in (0, 2, 1):
                self.first_z[2 * i + k].start()

    def middle(self):
        from_pair, from_z, _, _ = self.bufs
        yl, z, part = self.yl, self.z, self.part
        low = pl.ds(0, CUT)
        high = pl.ds(CUT, 128 - CUT)
        for i in (1, 3, 2, 0):
            self.first_pair[i].wait_recv()
            slot = yl * 4 + lax.rem(z + i, 4)
            part[slot, low] = (part[slot, low].astype(F32) + from_pair[i].astype(F32)).astype(BF16)
            if i:
                self.second_z[i - 1].start()
        for k in (1, 0):
            slot = lax.rem(yl + k, 2) * 4 + z
            for i in range(3):
                self.first_z[2 * i + k].wait_recv()
            total = part[slot, high].astype(F32)
            for i in range(3):
                total += from_z[i, k].astype(F32)
            part[slot, high] = total.astype(BF16)
            if k:
                self.second_pair.start()

    def finish(self, out):
        _, _, total_z, total_pair = self.bufs
        part, me = self.part, self.yl * 4 + self.z
        for copy in self.second_z:
            copy.wait_recv()
        total = part[me, 0:CUT].astype(F32)
        for i in range(3):
            total += total_z[i].astype(F32)
        out[0:CUT] = total.astype(out.dtype)
        self.second_pair.wait_recv()
        out[CUT:128] = (part[me, CUT:128].astype(F32) + total_pair[...].astype(F32)).astype(out.dtype)
        for copy in self.first_pair + self.first_z + self.second_z + [self.second_pair]:
            copy.wait_send()


def block_of(ref, kind, slot):
    if kind == "slot":
        return ref.at[slot]
    size = ref.shape[1] // 16
    return ref.at[:, pl.ds(pl.multiple_of(slot * size, size), size)]


class GatherDp:
    COPIES = 15

    def __init__(self, shard, out, kind, ssem, rsem, lsem):
        yh, x, c, yl, z = place()
        slot = lambda a, b, d: a * 8 + b * 2 + d
        mine = block_of(out, kind, slot(yh, x, c))
        self.local = pltpu.make_async_copy(shard, mine, lsem)
        self.own = [remote(shard, mine, ssem.at[i], rsem.at[i], dict(dx=i + 1)) for i in range(3)]
        self.own_y = remote(shard, mine, ssem.at[3], rsem.at[3], dict(dyh=1))
        far = block_of(out, kind, slot(1 - yh, x, c))
        self.far = [remote(far, far, ssem.at[4 + i], rsem.at[4 + i], dict(dx=i + 1)) for i in range(3)]
        self.core = [remote(shard, mine, ssem.at[7], rsem.at[7], dict(dc=1))]
        for k in range(2):
            for i in range(4):
                if k == 0 and i == 0:
                    continue
                n = 7 + 4 * k + i
                block = block_of(out, kind, slot(lax.rem(yh + k, 2), lax.rem(x + 4 - i, 4), c))
                self.core.append(remote(block, block, ssem.at[n], rsem.at[n], dict(dc=1)))

    def start(self):
        self.own_y.start()
        for i in (0, 2, 1):
            self.own[i].start()
        self.core[0].start()
        self.local.start()

    def forward(self):
        self.own_y.wait_recv()
        for i in (0, 2, 1):
            self.far[i].start()
        self.core[4].start()

    def share(self):
        for i in (0, 2, 1):
            self.own[i].wait_recv()
            self.core[1 + i].start()
        for i in (0, 2, 1):
            self.far[i].wait_recv()
            self.core[5 + i].start()

    def finish(self):
        for copy in self.core:
            copy.wait_recv()
        self.local.wait()
        for copy in self.own + [self.own_y] + self.far + self.core:
            copy.wait_send()


class ScatterDp:
    COPIES = 8 + 6 + 1

    @staticmethod
    def scratch(block):
        return [
            pltpu.VMEM((8,) + block, BF16),
            pltpu.VMEM((3, 2) + block, BF16),
            pltpu.VMEM(block, BF16),
            pltpu.SemaphoreType.DMA((15,)),
            pltpu.SemaphoreType.DMA((15,)),
        ]

    def __init__(self, part, kind, from_core, from_x, from_y, ssem, rsem):
        yh, x, c, yl, z = place()
        self.from_core, self.from_x, self.from_y = from_core, from_x, from_y
        self.block = lambda k, i, d: block_of(
            part, kind, lax.rem(yh + k, 2) * 8 + lax.rem(x + i, 4) * 2 + d
        )
        self.c = c
        self.core, self.along = [], []
        for k in range(2):
            for i in range(4):
                n = k * 4 + i
                self.core.append(
                    remote(self.block(k, i, 1 - c), from_core.at[n], ssem.at[n], rsem.at[n], dict(dc=1))
                )
        for k in range(2):
            for i in range(3):
                n = 8 + k * 3 + i
                self.along.append(
                    remote(self.block(k, i + 1, c), from_x.at[i, k], ssem.at[n], rsem.at[n], dict(dx=i + 1))
                )
        self.last = remote(self.block(1, 0, c), from_y, ssem.at[14], rsem.at[14], dict(dyh=1))

    def start(self):
        for k in (1, 0):
            for i in (1, 3, 2, 0):
                self.core[k * 4 + i].start()

    def along_x(self):
        for k in (1, 0):
            for i in (1, 3, 2, 0):
                n = k * 4 + i
                self.core[n].wait_recv()
                ref = self.block(k, i, self.c)
                ref[...] = (ref[...].astype(F32) + self.from_core[n].astype(F32)).astype(BF16)
                if i:
                    self.along[k * 3 + i - 1].start()

    def along_y(self):
        for i in (0, 2, 1):
            self.along[3 + i].wait_recv()
        ref = self.block(1, 0, self.c)
        total = ref[...].astype(F32)
        for i in range(3):
            total += self.from_x[i, 1].astype(F32)
        ref[...] = total.astype(BF16)
        self.last.start()

    def finish(self, out):
        for i in (0, 2, 1):
            self.along[i].wait_recv()
        total = self.block(0, 0, self.c)[...].astype(F32)
        for i in range(3):
            total += self.from_x[i, 0].astype(F32)
        self.last.wait_recv()
        out[...] = total + self.from_y[...].astype(F32)
        for copy in self.core + self.along + [self.last]:
            copy.wait_send()


def params(cid, vmem=60):
    return pltpu.CompilerParams(
        collective_id=cid, has_side_effects=True, vmem_limit_bytes=vmem << 20
    )


def gather_tensor(shard, cid):
    n = shard.shape[1]

    def gather_rows(shard_ref, out_ref, ssem, rsem, lsem):
        yh, x, c, yl, z = place()
        local = pltpu.make_async_copy(shard_ref, out_ref.at[yl * 4 + z], lsem)
        local.start()
        greet(TENSOR_PEERS)
        local.wait()
        gather = GatherTensor(out_ref, ssem, rsem)
        gather.start()
        gather.forward()
        gather.finish()

    out = pl.pallas_call(
        gather_rows,
        out_shape=jax.ShapeDtypeStruct((8, 128, n), shard.dtype),
        in_specs=[ANY],
        out_specs=ANY,
        scratch_shapes=[
            pltpu.SemaphoreType.DMA((10,)),
            pltpu.SemaphoreType.DMA((10,)),
            pltpu.SemaphoreType.DMA,
        ],
        compiler_params=params(cid, 16),
        name="gather_rows_%d" % cid,
    )(shard)
    return out.reshape(1024, n)


def scatter_tensor(part, cid):
    n = part.shape[1]

    def scatter_rows(part_ref, out_ref, mine, b0, b1, b2, b3, ssem, rsem, lsem):
        local = pltpu.make_async_copy(part_ref, mine, lsem)
        local.start()
        greet(TENSOR_PEERS)
        local.wait()
        scatter = ScatterTensor(mine, b0, b1, b2, b3, ssem, rsem)
        scatter.start()
        scatter.middle()
        scatter.finish(out_ref)

    return pl.pallas_call(
        scatter_rows,
        out_shape=jax.ShapeDtypeStruct((128, n), F32),
        in_specs=[ANY],
        out_specs=VM,
        scratch_shapes=[pltpu.VMEM((8, 128, n), BF16)]
        + ScatterTensor.scratch(n)
        + [pltpu.SemaphoreType.DMA],
        compiler_params=params(cid, 40),
        name="scatter_rows_%d" % cid,
    )(part.reshape(8, 128, n))


def gather_dp(shards, kinds, cid):
    outs = []
    for shard, kind in zip(shards, kinds):
        a, b = shard.shape
        outs.append(
            jax.ShapeDtypeStruct((16, a, b) if kind == "slot" else (a, 16 * b), shard.dtype)
        )
    n = len(shards)

    def gather_weights(*refs):
        ins, outs, (ssem, rsem, lsem) = refs[:n], refs[n : 2 * n], refs[2 * n :]
        greet(DP_PEERS)
        items = [
            GatherDp(ins[i], outs[i], kinds[i], ssem.at[i], rsem.at[i], lsem.at[i])
            for i in range(n)
        ]
        for item in items:
            item.start()
        for item in items:
            item.forward()
        for item in items:
            item.share()
        for item in items:
            item.finish()

    full = pl.pallas_call(
        gather_weights,
        out_shape=outs,
        in_specs=[ANY] * n,
        out_specs=[ANY] * n,
        scratch_shapes=[
            pltpu.SemaphoreType.DMA((n, 15)),
            pltpu.SemaphoreType.DMA((n, 15)),
            pltpu.SemaphoreType.DMA((n,)),
        ],
        compiler_params=params(cid, 16),
        name="gather_weights_%d" % cid,
    )(*shards)
    return [
        f.reshape(16 * f.shape[1], f.shape[2]) if kind == "slot" else f
        for f, kind in zip(full, kinds)
    ]


def scatter_dp(parts, kinds, cid):
    n = len(parts)
    shapes, ins = [], []
    for part, kind in zip(parts, kinds):
        a, b = part.shape
        shapes.append((a // 16, b) if kind == "slot" else (a, b // 16))
        ins.append(part.reshape(16, a // 16, b) if kind == "slot" else part)
    scratch = []
    for array, shape in zip(ins, shapes):
        scratch += [pltpu.VMEM(array.shape, BF16)] + ScatterDp.scratch(shape)
    scratch.append(pltpu.SemaphoreType.DMA((n,)))

    def scatter_grads(*refs):
        parts, outs, rest = refs[:n], refs[n : 2 * n], refs[2 * n :]
        lsem = rest[-1]
        local = [
            pltpu.make_async_copy(parts[i], rest[6 * i], lsem.at[i]) for i in range(n)
        ]
        for copy in local:
            copy.start()
        greet(DP_PEERS)
        items = [ScatterDp(rest[6 * i], kinds[i], *rest[6 * i + 1 : 6 * i + 6]) for i in range(n)]
        for copy, item in zip(local, items):
            copy.wait()
            item.start()
        for item in items:
            item.along_x()
        for item in items:
            item.along_y()
        for item, out in zip(items, outs):
            item.finish(out)

    return pl.pallas_call(
        scatter_grads,
        out_shape=[jax.ShapeDtypeStruct(s, F32) for s in shapes],
        in_specs=[ANY] * n,
        out_specs=[VM] * n,
        scratch_shapes=scratch,
        compiler_params=params(cid, 60),
        name="scatter_grads_%d" % cid,
    )(*ins)


def rope_tables(count, size):
    half_size = size // 2
    frequency = THETA ** (-(jnp.arange(half_size, dtype=jnp.float32) * 2.0 / size))
    angles = jnp.arange(count, dtype=jnp.float32)[:, None] * frequency[None, :]
    return (jnp.cos(angles), jnp.sin(angles))


def rotate(values, cosine, sine_table, direction):
    half_size = values.shape[-1] // 2
    first_half = values[..., :half_size]
    second_half = values[..., half_size:]
    cos_b = cosine[:, None, :]
    sin_b = direction * sine_table[:, None, :]
    return jnp.concatenate(
        [first_half * cos_b - second_half * sin_b, second_half * cos_b + first_half * sin_b], -1
    )


def dot_last(left, right):
    return lax.dot_general(
        left, right, (((1,), (1,)), ((), ())), preferred_element_type=jnp.float32
    )


def dot_first(left, right):
    return lax.dot_general(
        left, right, (((0,), (0,)), ((), ())), preferred_element_type=jnp.float32
    )


def rms_scale(values):
    return lax.rsqrt(jnp.mean(values * values, -1, keepdims=True) + EPS)


def norm_back(values, scale_rows, gain, grad_rows):
    weighted = gain * grad_rows
    mean_term = jnp.mean(values * weighted, -1, keepdims=True)
    return scale_rows * weighted - values * scale_rows**3 * mean_term


def masked_scores(rotated_queries, rotated_keys, length):
    unscaled_scores = jnp.einsum(
        "euk,zuk->uez", rotated_queries, rotated_keys, preferred_element_type=jnp.float32
    )
    count = rotated_queries.shape[0]
    row_pos = lax.broadcasted_iota(jnp.int32, (count, count), 0)
    col_pos = lax.broadcasted_iota(jnp.int32, (count, count), 1)
    allowed = (col_pos <= row_pos) & (col_pos < length)
    return jnp.where(allowed[None], unscaled_scores, -1e30)


def attend(operands):
    rotated_queries, rotated_keys, value_lower_precision, length = operands
    score_matrix = masked_scores(rotated_queries, rotated_keys, length)
    row_peak = jnp.max(score_matrix, -1, keepdims=True)
    exp_terms = jnp.exp(score_matrix - row_peak)
    row_total = jnp.sum(exp_terms, -1, keepdims=True)
    attention_probability = exp_terms / row_total
    lse_rows = row_peak[..., 0] + jnp.log(row_total[..., 0])
    mixed_heads = jnp.einsum(
        "gqk,kgf->qgf",
        attention_probability.astype(jnp.bfloat16),
        value_lower_precision,
        preferred_element_type=jnp.float32,
    )
    return (mixed_heads.astype(jnp.bfloat16), lse_rows)


def attend_back(operands):
    rotated_queries, rotated_keys, value_lower_precision, mixed_value_gradient, lse_rows, length = (
        operands
    )
    score_matrix = masked_scores(rotated_queries, rotated_keys, length)
    attention_probability = jnp.exp(score_matrix - lse_rows[..., None])
    probability_gradient = jnp.einsum(
        "euk,zuk->uez",
        mixed_value_gradient,
        value_lower_precision,
        preferred_element_type=jnp.float32,
    )
    delta_rows = jnp.sum(attention_probability * probability_gradient, -1, keepdims=True)
    score_gradient = (attention_probability * (probability_gradient - delta_rows)).astype(
        jnp.bfloat16
    )
    rotated_query_gradient = jnp.einsum(
        "gqk,kgf->qgf", score_gradient, rotated_keys, preferred_element_type=jnp.float32
    )
    rotated_key_gradient = jnp.einsum(
        "jkt,kji->tji", score_gradient, rotated_queries, preferred_element_type=jnp.float32
    )
    d_vlow = jnp.einsum(
        "jkt,kji->tji",
        attention_probability.astype(jnp.bfloat16),
        mixed_value_gradient,
        preferred_element_type=jnp.float32,
    )
    return (rotated_query_gradient, rotated_key_gradient, d_vlow.astype(jnp.bfloat16))


def local(
    tokens,
    lengths,
    w_query,
    w_key,
    w_value,
    w_out,
    w_gate,
    w_up,
    w_down,
    q_gain,
    k_gain,
    attn_gain,
    mlp_gain,
    cotangent,
):
    sequences, part_len, width = tokens.shape
    tp_count = lax.axis_size("tensor")
    tp_index = lax.axis_index("tensor")
    full_len = part_len * tp_count
    columns = w_query.shape[1]
    heads_dev = columns // HEAD_DIM
    kinds = ("slot", "slot", "slot", "col", "slot", "slot", "col")
    gathered = gather_dp((w_query, w_key, w_value, w_out, w_gate, w_up, w_down), kinds, 1)
    wq_full, wk_full, wv_full, wo_full, wg_full, wu_full, wd_full = gathered
    q_gain_dev = lax.dynamic_slice_in_dim(q_gain, tp_index * columns, columns)
    k_gain_dev = lax.dynamic_slice_in_dim(k_gain, tp_index * columns, columns)
    positions = tp_index * part_len + lax.broadcasted_iota(jnp.int32, (sequences, part_len), 1)
    valid_rows = (positions < lengths[:, None])[..., None]
    whole_rows = gather_tensor(tokens[0], 2)
    q_raw = jnp.dot(whole_rows, wq_full, preferred_element_type=jnp.float32)
    k_raw = jnp.dot(whole_rows, wk_full, preferred_element_type=jnp.float32)
    v_raw = jnp.dot(whole_rows, wv_full, preferred_element_type=jnp.float32)
    q_sums, k_sums = lax.psum((jnp.sum(q_raw * q_raw, -1), jnp.sum(k_raw * k_raw, -1)), "tensor")
    q_scale = lax.rsqrt(q_sums / width + EPS)[:, None]
    k_scale = lax.rsqrt(k_sums / width + EPS)[:, None]
    q_norm = q_raw * q_scale * q_gain_dev
    k_norm = k_raw * k_scale * k_gain_dev
    cosine, sine_table = rope_tables(full_len, HEAD_DIM)
    head_shape = (sequences, full_len, heads_dev, HEAD_DIM)
    score_scale = HEAD_DIM ** (-0.5)
    rotated_queries = (
        rotate(q_norm.reshape(head_shape), cosine, sine_table, 1.0) * score_scale
    ).astype(jnp.bfloat16)
    rotated_keys = rotate(k_norm.reshape(head_shape), cosine, sine_table, 1.0).astype(jnp.bfloat16)
    value_lower_precision = v_raw.astype(jnp.bfloat16).reshape(head_shape)
    mixed_heads, lse_all = lax.map(
        attend, (rotated_queries, rotated_keys, value_lower_precision, lengths)
    )
    mixed_flat = mixed_heads.reshape(sequences * full_len, columns)
    branch_part = jnp.dot(mixed_flat, wo_full, preferred_element_type=jnp.float32).reshape(
        sequences, full_len, width
    )
    branch = scatter_tensor(branch_part.astype(jnp.bfloat16)[0], 10)[None]
    b_scale = rms_scale(branch)
    residual = tokens.astype(jnp.float32) + branch * b_scale * attn_gain
    res_low = residual.astype(jnp.bfloat16)
    res_whole = gather_tensor(res_low[0], 3)
    gate_value = jnp.dot(res_whole, wg_full, preferred_element_type=jnp.float32)
    up_value = jnp.dot(res_whole, wu_full, preferred_element_type=jnp.float32)
    sigmoid_gate = jax.nn.sigmoid(gate_value)
    silu_gate = gate_value * sigmoid_gate
    inner_act = (silu_gate * up_value).astype(jnp.bfloat16)
    down_part = jnp.dot(inner_act, wd_full, preferred_element_type=jnp.float32).reshape(
        sequences, full_len, width
    )
    down_value = scatter_tensor(down_part.astype(jnp.bfloat16)[0], 11)[None]
    d_scale = rms_scale(down_value)
    activations = jnp.where(valid_rows, residual + down_value * d_scale * mlp_gain, 0.0).astype(
        jnp.bfloat16
    )
    back_weights = gathered
    wq_back, wk_back, wv_back, wo_back, wg_back, wu_back, wd_back = back_weights
    grad_out = jnp.where(valid_rows, cotangent.astype(jnp.float32), 0.0)
    mlp_gain_part = jnp.sum(grad_out * down_value * d_scale, (0, 1))
    d_down = norm_back(down_value, d_scale, mlp_gain, grad_out).astype(jnp.bfloat16)
    d_down_whole = gather_tensor(d_down[0], 4)
    d_inner = dot_last(d_down_whole, wd_back)
    w_down_part = dot_first(inner_act, d_down_whole)
    d_gate = (d_inner * up_value * sigmoid_gate * (1.0 + gate_value * (1.0 - sigmoid_gate))).astype(
        jnp.bfloat16
    )
    d_up = (d_inner * silu_gate).astype(jnp.bfloat16)
    w_gate_part = dot_first(res_whole, d_gate)
    w_up_part = dot_first(res_whole, d_up)
    d_res_part = (dot_last(d_gate, wg_back) + dot_last(d_up, wu_back)).reshape(
        sequences, full_len, width
    )
    d_res = grad_out + scatter_tensor(d_res_part.astype(jnp.bfloat16)[0], 12)[None]
    attn_gain_part = jnp.sum(d_res * branch * b_scale, (0, 1))
    d_branch = norm_back(branch, b_scale, attn_gain, d_res).astype(jnp.bfloat16)
    d_branch_whole = gather_tensor(d_branch[0], 5)
    w_out_part = dot_first(mixed_flat, d_branch_whole)
    mixed_value_gradient = (
        dot_last(d_branch_whole, wo_back).astype(jnp.bfloat16).reshape(head_shape)
    )
    rotated_query_gradient, rotated_key_gradient, d_vlow = lax.map(
        attend_back,
        (
            rotated_queries,
            rotated_keys,
            value_lower_precision,
            mixed_value_gradient,
            lse_all,
            lengths,
        ),
    )
    d_qnorm = rotate(rotated_query_gradient * score_scale, cosine, sine_table, -1.0).reshape(
        sequences * full_len, columns
    )
    d_knorm = rotate(rotated_key_gradient, cosine, sine_table, -1.0).reshape(
        sequences * full_len, columns
    )
    q_weighted = d_qnorm * q_gain_dev
    k_weighted = d_knorm * k_gain_dev
    q_inner, k_inner = lax.psum(
        (jnp.sum(q_raw * q_weighted, -1), jnp.sum(k_raw * k_weighted, -1)), "tensor"
    )
    d_qraw = (q_scale * q_weighted - q_raw * q_scale**3 * (q_inner / width)[:, None]).astype(
        jnp.bfloat16
    )
    d_kraw = (k_scale * k_weighted - k_raw * k_scale**3 * (k_inner / width)[:, None]).astype(
        jnp.bfloat16
    )
    d_vflat = d_vlow.reshape(sequences * full_len, columns)
    q_gain_part = jnp.sum(d_qnorm * q_raw * q_scale, 0)
    k_gain_part = jnp.sum(d_knorm * k_raw * k_scale, 0)
    w_query_part = dot_first(whole_rows, d_qraw)
    w_key_part = dot_first(whole_rows, d_kraw)
    w_value_part = dot_first(whole_rows, d_vflat)
    d_input_part = (
        dot_last(d_qraw, wq_back) + dot_last(d_kraw, wk_back) + dot_last(d_vflat, wv_back)
    ).reshape(sequences, full_len, width)
    input_grad = d_res + scatter_tensor(d_input_part.astype(jnp.bfloat16)[0], 13)[None]
    parts = (w_query_part, w_key_part, w_value_part, w_out_part, w_gate_part, w_up_part, w_down_part)
    grads_owned = scatter_dp([part.astype(jnp.bfloat16) for part in parts], kinds, 14)
    empty_gain = jnp.zeros((width,), jnp.float32)
    q_gain_full = lax.dynamic_update_slice_in_dim(empty_gain, q_gain_part, tp_index * columns, 0)
    k_gain_full = lax.dynamic_update_slice_in_dim(empty_gain, k_gain_part, tp_index * columns, 0)
    gain_totals = lax.psum(
        (q_gain_full, k_gain_full, attn_gain_part, mlp_gain_part), ("dp", "tensor")
    )
    return (
        activations,
        input_grad,
        grads_owned[0],
        grads_owned[1],
        grads_owned[2],
        grads_owned[3],
        grads_owned[4],
        grads_owned[5],
        grads_owned[6],
        gain_totals[0],
        gain_totals[1],
        gain_totals[2],
        gain_totals[3],
    )


def solution(mesh):
    return jax.shard_map(
        local,
        mesh=mesh,
        in_specs=(
            P("dp", "tensor", None),
            P("dp"),
            P("dp", "tensor"),
            P("dp", "tensor"),
            P("dp", "tensor"),
            P("tensor", "dp"),
            P("dp", "tensor"),
            P("dp", "tensor"),
            P("tensor", "dp"),
            P(),
            P(),
            P(),
            P(),
            P("dp", "tensor", None),
        ),
        out_specs=(
            P("dp", "tensor", None),
            P("dp", "tensor", None),
            P("dp", "tensor"),
            P("dp", "tensor"),
            P("dp", "tensor"),
            P("tensor", "dp"),
            P("dp", "tensor"),
            P("dp", "tensor"),
            P("tensor", "dp"),
            P(),
            P(),
            P(),
            P(),
        ),
        check_vma=False,
    )
```

```python
import jax
import jax.numpy as jnp
import numpy as np
from jax import lax
from jax.experimental import pallas as pl
from jax.experimental.pallas import tpu as pltpu
from jax.sharding import PartitionSpec as P

HEAD_DIM = 128
EPS = 1e-06
THETA = 500000.0
MESH = pl.DeviceIdType.MESH
BF16 = jnp.bfloat16
F32 = jnp.float32
ANY = pl.BlockSpec(memory_space=pl.ANY)
VM = pl.BlockSpec(memory_space=pltpu.VMEM)
DMA = pltpu.SemaphoreType.DMA
CUT = 896
WIDTH = 2048


def place():
    d = lax.axis_index("dp")
    t = lax.axis_index("tensor")
    return d // 8, lax.rem(d // 2, 4), lax.rem(d, 2), t // 4, lax.rem(t, 4)


def other(dyh=0, dx=0, dc=0, dyl=0, dz=0):
    yh, x, c, yl, z = place()
    return (
        lax.rem(yh + dyh, 2) * 8 + lax.rem(x + dx, 4) * 2 + lax.rem(c + dc, 2),
        lax.rem(yl + dyl, 2) * 4 + lax.rem(z + dz, 4),
    )


TENSOR_PEERS = (dict(dz=1), dict(dz=3), dict(dyl=1))
DP_PEERS = (dict(dx=1), dict(dx=2), dict(dx=3), dict(dyh=1), dict(dc=1))
SMEM = pl.BlockSpec(memory_space=pltpu.SMEM)


def greet(peers):
    barrier = pltpu.get_barrier_semaphore()
    for peer in peers:
        pl.semaphore_signal(barrier, 1, device_id=other(**peer), device_id_type=MESH)
    pl.semaphore_wait(barrier, len(peers))


def remote(src, dst, sems, index, peer):
    ssem, rsem = sems
    return pltpu.make_async_remote_copy(
        src_ref=src,
        dst_ref=dst,
        send_sem=ssem.at[index],
        recv_sem=rsem.at[index],
        device_id=other(**peer),
        device_id_type=MESH,
    )


def rows(ref, slot):
    return ref.at[pl.ds(pl.multiple_of(slot * 128, 128), 128)]


def halves(ref):
    half = ref.shape[0] // 2
    return ref.at[pl.ds(0, half)], ref.at[pl.ds(half, half)]


def add_into(out, *terms):
    @pl.loop(0, out.shape[0] // 16)
    def _(i):
        r = pl.ds(pl.multiple_of(i * 16, 16), 16)
        if len(terms) == 2 and out.dtype == BF16:
            out[r, :] = terms[0][r, :] + terms[1][r, :]
        else:
            total = terms[0][r, :].astype(F32)
            for term in terms[1:]:
                total += term[r, :].astype(F32)
            out[r, :] = total.astype(out.dtype)


class RingGather:
    COPIES = 6

    def __init__(self, block, axis, sems, base, source=None):
        up, down = {axis: 1}, {axis: 3}
        src = halves(block(0) if source is None else source)
        own, behind, ahead = halves(block(0)), halves(block(3)), halves(block(1))
        self.copies = [
            remote(src[0], own[0], sems, base, up),
            remote(src[1], own[1], sems, base + 1, down),
            remote(src[1], own[1], sems, base + 2, up),
            remote(src[0], own[0], sems, base + 3, down),
            remote(behind[0], behind[0], sems, base + 4, up),
            remote(ahead[1], ahead[1], sems, base + 5, down),
        ]

    def start(self):
        for copy in self.copies[:4]:
            copy.start()

    def forward(self):
        for i in range(2):
            self.copies[i].wait_recv()
            self.copies[4 + i].start()

    def behind(self):
        self.copies[2].wait_recv()

    def ahead(self):
        self.copies[3].wait_recv()

    def far(self):
        for copy in self.copies[4:]:
            copy.wait_recv()

    def drain(self):
        for copy in self.copies:
            copy.wait_send()


class RingReduce:
    COPIES = 6

    @staticmethod
    def scratch(n, m):
        return [pltpu.VMEM((2, n // 2, m), BF16), pltpu.VMEM((2, n, m), BF16)]

    def __init__(self, block, axis, part, full, sems, base):
        up, down = {axis: 1}, {axis: 3}
        one, two, three = halves(block(1)), halves(block(2)), halves(block(3))
        from_behind, from_ahead = halves(full.at[0]), halves(full.at[1])
        self.adds = ((one[0], part.at[0]), (three[1], part.at[1]))
        self.terms = (block(0), full.at[0], full.at[1])
        self.copies = [
            remote(two[0], part.at[0], sems, base, up),
            remote(two[1], part.at[1], sems, base + 1, down),
            remote(one[1], from_behind[1], sems, base + 2, up),
            remote(three[0], from_ahead[0], sems, base + 3, down),
            remote(one[0], from_behind[0], sems, base + 4, up),
            remote(three[1], from_ahead[1], sems, base + 5, down),
        ]

    def start(self):
        for copy in self.copies[:4]:
            copy.start()

    def forward(self):
        for i in range(2):
            self.copies[i].wait_recv()
            add_into(self.adds[i][0], *self.adds[i])
            self.copies[4 + i].start()

    def arrive(self):
        for copy in self.copies[2:]:
            copy.wait_recv()

    def drain(self):
        for copy in self.copies:
            copy.wait_send()


class GatherTensor:
    COPIES = 17

    def __init__(self, buf, ssem, rsem):
        yh, x, c, yl, z = place()
        self.yl, self.z = yl, z
        sems = (ssem, rsem)
        slot = lambda k, i: rows(buf, lax.rem(yl + k, 2) * 4 + lax.rem(z + i, 4))
        low = lambda ref: ref.at[:, pl.ds(0, CUT)]
        high = lambda ref: ref.at[:, pl.ds(CUT, WIDTH - CUT)]
        self.ring = RingGather(lambda i: slot(0, i), "dz", sems, 0)
        self.pair_ring = RingGather(lambda i: high(slot(1, i)), "dz", sems, 6)
        own = slot(0, 0)
        pair = dict(dyl=1)
        self.high = remote(high(own), high(own), sems, 12, pair)
        self.low = [
            remote(low(slot(0, i)), low(slot(0, i)), sems, 13 + i, pair) for i in range(4)
        ]

    def start(self):
        self.high.start()
        self.ring.start()
        self.low[0].start()

    def run(self, process, spare=None):
        yl, z = self.yl, self.z

        @pl.loop(0, 2)
        def _(k):
            @pl.when(k == 1)
            def _():
                self.ring.forward()
                self.high.wait_recv()
                self.pair_ring.start()
                self.low[0].wait_recv()

            process(lax.rem(yl + k, 2) * 4 + z)

        if spare is not None:
            spare(0)

        @pl.loop(0, 6)
        def _(j):
            @pl.when(j == 0)
            def _():
                self.ring.behind()
                self.low[3].start()
                self.ring.ahead()
                self.low[1].start()

            @pl.when(j == 2)
            def _():
                self.ring.far()
                self.low[2].start()
                self.pair_ring.forward()

            @pl.when(j == 3)
            def _():
                if spare is not None:
                    spare(1)
                self.pair_ring.behind()
                self.low[3].wait_recv()

            @pl.when(j == 4)
            def _():
                self.pair_ring.ahead()
                self.low[1].wait_recv()

            @pl.when(j == 5)
            def _():
                self.pair_ring.far()
                self.low[2].wait_recv()

            i = lax.rem(j, 3)
            step = (3 * i * i - 7 * i + 6) // 2
            process(lax.rem(yl + j // 3, 2) * 4 + lax.rem(z + step, 4))

        self.ring.drain()
        self.pair_ring.drain()
        for copy in [self.high] + self.low:
            copy.wait_send()


class ScatterTensor:
    COPIES = 23

    @staticmethod
    def scratch():
        return (
            [pltpu.VMEM((4, 128, CUT), BF16), pltpu.VMEM((128, WIDTH - CUT), BF16)]
            + RingReduce.scratch(128, CUT)
            + RingReduce.scratch(128, WIDTH - CUT) * 2
        )

    def __init__(self, part, bufs, ssem, rsem):
        yh, x, c, yl, z = place()
        self.yl = yl
        self.from_pair, self.last = bufs[0], bufs[1]
        sems = (ssem, rsem)
        slot = lambda k, i: rows(part, lax.rem(yl + k, 2) * 4 + lax.rem(z + i, 4))
        low = lambda k, i: slot(k, i).at[:, pl.ds(0, CUT)]
        high = lambda k, i: slot(k, i).at[:, pl.ds(CUT, WIDTH - CUT)]
        pair = dict(dyl=1)
        self.low = lambda i: low(0, i)
        self.low_ring = RingReduce(lambda i: low(0, i), "dz", bufs[2], bufs[3], sems, 0)
        self.pair_ring = RingReduce(lambda i: high(1, i), "dz", bufs[4], bufs[5], sems, 6)
        self.own_ring = RingReduce(lambda i: high(0, i), "dz", bufs[6], bufs[7], sems, 12)
        self.first = [remote(low(1, i), bufs[0].at[i], sems, 18 + i, pair) for i in range(4)]
        self.second = remote(high(1, 0), bufs[1], sems, 22, pair)

    def run(self, process):
        @pl.loop(0, 2)
        def _(k):
            process(lax.rem(self.yl + 1 + k, 2))

            @pl.when(k == 0)
            def _():
                for i in (2, 1, 3, 0):
                    self.first[i].start()
                self.pair_ring.start()

            @pl.when(k == 1)
            def _():
                self.own_ring.start()

    def add_first(self, i):
        self.first[i].wait_recv()
        add_into(self.low(i), self.low(i), self.from_pair.at[i])

    def middle(self):
        self.pair_ring.forward()
        for i in (2, 1, 3):
            self.add_first(i)
        self.low_ring.start()
        self.own_ring.forward()

    def later(self):
        self.pair_ring.arrive()
        add_into(self.pair_ring.terms[0], *self.pair_ring.terms)
        self.second.start()
        self.low_ring.forward()
        self.add_first(0)

    def finish(self, out):
        self.own_ring.arrive()
        self.second.wait_recv()
        add_into(out.at[:, pl.ds(CUT, WIDTH - CUT)], *self.own_ring.terms, self.last)
        self.low_ring.arrive()
        add_into(out.at[:, pl.ds(0, CUT)], *self.low_ring.terms)
        for ring in (self.low_ring, self.pair_ring, self.own_ring):
            ring.drain()
        for copy in self.first + [self.second]:
            copy.wait_send()


def block_of(ref, kind, slot):
    if kind == "row":
        size = ref.shape[0] // 16
        return ref.at[pl.ds(pl.multiple_of(slot * size, size), size)]
    size = ref.shape[1] // 16
    return ref.at[:, pl.ds(pl.multiple_of(slot * size, size), size)]


class GatherDp:
    COPIES = 21

    def __init__(self, shard, out, kind, ssem, rsem, lsem, pair=None):
        yh, x, c, yl, z = place()
        sems = (ssem, rsem)
        self.pair = pair
        block = lambda k, i: block_of(
            out, kind, lax.rem(yh + k, 2) * 8 + lax.rem(x + i, 4) * 2 + c
        )
        self.local = [pltpu.make_async_copy(shard, block(0, 0), lsem.at[0])]
        if pair is not None:
            self.local.append(pltpu.make_async_copy(pair, block(1, 0), lsem.at[1]))
        self.ring = RingGather(lambda i: block(0, i), "dx", sems, 0, shard)
        self.far_ring = RingGather(lambda i: block(1, i), "dx", sems, 6, pair)
        if pair is None:
            self.own_y = remote(shard, block(0, 0), sems, 12, dict(dyh=1))
        core = dict(dc=1)
        self.core = [remote(shard, block(0, 0), sems, 13, core)]
        for n in range(1, 8):
            ref = block(n // 4, n % 4)
            source = pair if n == 4 and pair is not None else ref
            self.core.append(remote(source, ref, sems, 13 + n, core))

    def start(self):
        if self.pair is None:
            self.own_y.start()
        self.ring.start()
        self.core[0].start()
        for copy in self.local:
            copy.start()
        if self.pair is not None:
            self.far_ring.start()
            self.core[4].start()

    def forward(self):
        self.ring.forward()

    def forward_y(self):
        self.own_y.wait_recv()
        self.far_ring.start()
        self.core[4].start()

    def share(self):
        self.ring.behind()
        self.core[3].start()
        self.ring.ahead()
        self.core[1].start()
        self.ring.far()
        self.core[2].start()

    def forward_far(self):
        self.far_ring.forward()

    def share_far(self):
        self.far_ring.behind()
        self.core[7].start()
        self.far_ring.ahead()
        self.core[5].start()
        self.far_ring.far()
        self.core[6].start()

    def finish(self):
        for copy in self.core:
            copy.wait_recv()
        for copy in self.local:
            copy.wait()
        self.ring.drain()
        self.far_ring.drain()
        for copy in self.core if self.pair is not None else [self.own_y] + self.core:
            copy.wait_send()


class ScatterDp:
    COPIES = 21

    @staticmethod
    def scratch(block):
        return (
            [pltpu.VMEM((8,) + block, BF16), pltpu.VMEM(block, BF16)]
            + RingReduce.scratch(*block) * 2
            + [DMA((21,)), DMA((21,))]
        )

    def __init__(self, part, kind, from_core, from_y, h0, f0, h1, f1, ssem, rsem):
        yh, x, c, yl, z = place()
        sems = (ssem, rsem)
        self.from_core, self.from_y = from_core, from_y
        block = lambda k, i, d: block_of(
            part, kind, lax.rem(yh + k, 2) * 8 + lax.rem(x + i, 4) * 2 + d
        )
        self.block = lambda k, i: block(k, i, c)
        self.core = [
            remote(block(n // 4, n % 4, 1 - c), from_core.at[n], sems, n, dict(dc=1))
            for n in range(8)
        ]
        self.ring = RingReduce(lambda i: block(0, i, c), "dx", h0, f0, sems, 8)
        self.far_ring = RingReduce(lambda i: block(1, i, c), "dx", h1, f1, sems, 14)
        self.last = remote(block(1, 0, c), from_y, sems, 20, dict(dyh=1))

    def start(self):
        for n in (6, 5, 7, 4, 2, 1, 3, 0):
            self.core[n].start()

    def add_core(self, n):
        self.core[n].wait_recv()
        ref = self.block(n // 4, n % 4)
        add_into(ref, ref, self.from_core.at[n])

    def along_x(self):
        for n in (6, 5, 7):
            self.add_core(n)
        self.far_ring.start()
        for n in (2, 1, 3):
            self.add_core(n)
        self.ring.start()
        for n in (4, 0):
            self.add_core(n)

    def forward(self):
        self.far_ring.forward()
        self.ring.forward()

    def along_y(self):
        self.far_ring.arrive()
        add_into(self.far_ring.terms[0], *self.far_ring.terms)
        self.last.start()

    def finish(self, out):
        self.ring.arrive()
        self.last.wait_recv()
        add_into(out, *self.ring.terms, self.from_y)
        self.ring.drain()
        self.far_ring.drain()
        for copy in self.core + [self.last]:
            copy.wait_send()


def params(cid):
    return pltpu.CompilerParams(
        collective_id=cid, has_side_effects=True, vmem_limit_bytes=63 << 20
    )


def nn(a, b):
    return jnp.dot(a, b, preferred_element_type=F32)


def nt(a, b):
    return lax.dot_general(a, b, (((1,), (1,)), ((), ())), preferred_element_type=F32)


def tn(a, b):
    return lax.dot_general(a, b, (((0,), (0,)), ((), ())), preferred_element_type=F32)


def tiles(count, size):
    def run(body):
        @pl.loop(0, count // size)
        def _(i):
            body(pl.ds(pl.multiple_of(i * size, size), size))

    return run


def rope_tables():
    frequency = THETA ** (-(np.arange(64, dtype=np.float32) * np.float32(2.0) / np.float32(HEAD_DIM)))
    angles = np.arange(1024, dtype=np.float32)[:, None] * frequency.astype(np.float32)[None, :]
    cosine, sine = np.cos(angles), np.sin(angles)
    return (
        np.concatenate([cosine, cosine], 1).astype(np.float32),
        np.concatenate([-sine, sine], 1).astype(np.float32),
    )


class Exchange:
    PEERS = tuple(dict(dz=a, dyl=b) for b in range(2) for a in range(4) if a or b)

    def __init__(self, buf, ssem, rsem):
        yh, x, c, yl, z = place()
        self.buf = buf
        self.mine = buf.at[yl * 4 + z]
        self.copies = [
            remote(self.mine, self.mine, (ssem, rsem), i, peer)
            for i, peer in enumerate(self.PEERS)
        ]

    def start(self):
        for copy in self.copies:
            copy.start()

    def finish(self):
        for copy in self.copies:
            copy.wait_recv()
        for copy in self.copies:
            copy.wait_send()

    def sum(self):
        total = self.buf[0]
        for i in range(1, 8):
            total += self.buf[i]
        return total


def row_sums(values):
    return nt(jnp.ones((8, values.shape[1]), F32), values)


def spread(pair):
    row = lax.broadcasted_iota(jnp.int32, (8, 256), 0)
    column = lax.broadcasted_iota(jnp.int32, (8, 256), 1)
    pick = jnp.where(row == column // 128 * 4, 1.0, 0.0)
    return lax.dot_general(
        pair, pick, (((0,), (0,)), ((), ())), precision=lax.Precision.HIGHEST, preferred_element_type=F32
    )


def both(a, b):
    return jnp.where(lax.broadcasted_iota(jnp.int32, a.shape, 0) < 4, a, b)


ALL_PEERS = Exchange.PEERS + DP_PEERS
SCALE = HEAD_DIM**-0.5


def diagonal_mask(scores, first, length):
    row = lax.broadcasted_iota(jnp.int32, scores.shape, 0)
    column = lax.broadcasted_iota(jnp.int32, scores.shape, 1)
    return jnp.where((column <= row) & (column + first < length), scores, -1e30)


def attention_forward(tokens, lengths, weights, q_gain, k_gain, tables):
    full = [(2048, 256)] * 3 + [(256, 2048), (2048, 1024), (2048, 1024), (1024, 128)]
    kinds = ("row", "row", "row", "col", "row", "row", "col")

    def attention_step(
        tokens, w0, w1, w2, w3, w4, w5, w6, lengths, q_gain_all, k_gain_all, cosine, sine,
        x_out, f0, f1, f2, f3, f4, f5, f6, q_raw_out, k_raw_out, q_rot_out, k_rot_out, v_out,
        mixed_out, lse_out, scale_out, branch,
        x, wq, wk, wv, wo, q_raw, k_raw, q_rot, k_rot, v_low, mixed, lse, scales, part, sums,
        *rest,
    ):
        bufs, (ssem, rsem, gsem, hsem, wsem, vsem, esem, fsem, lsem, msem) = rest[:8], rest[8:]
        yh, xx, c, yl, z = place()
        own_columns = pl.ds(pl.multiple_of((yl * 4 + z) * 256, 256), 256)
        q_gain, k_gain = q_gain_all[:, own_columns], k_gain_all[:, own_columns]
        length = lengths[0]
        first = pltpu.make_async_copy(tokens, rows(x, yl * 4 + z), msem)
        first.start()
        greet(ALL_PEERS)
        gather = GatherTensor(x, gsem, hsem)
        shards = (w0, w1, w2, w3, w4, w5, w6)
        wholes = (wq, wk, wv, wo, f4, f5, f6)
        items = [
            GatherDp(shards[i], wholes[i], kinds[i], wsem.at[i], vsem.at[i], lsem.at[pl.ds(i, 1)])
            for i in range(6)
        ]
        down_pair = remote(w6, f6, (wsem.at[6], vsem.at[6]), 0, dict(dyh=1))
        small, large = items[:4], items[4:]
        for item in small:
            item.start()
        first.wait()
        gather.start()

        def spread_weights(stage):
            for item in small:
                if stage == 0:
                    item.forward()
                    item.forward_y()
                else:
                    item.share()
                    item.forward_far()

        gather.run(lambda slot: None, spread_weights)
        for item in small:
            item.share_far()
        for item in large:
            item.start()
        for item in small:
            item.finish()
        saves = []

        def save(source, target):
            copy = pltpu.make_async_copy(source, target, lsem.at[7 + len(saves)])
            copy.start()
            saves.append(copy)

        save(x, x_out)
        for source, target in ((wq, f0), (wk, f1), (wv, f2), (wo, f3)):
            save(source, target)

        @tiles(1024, 256)
        def _(r):
            xt = x[r, :]
            q = nn(xt, wq[...])
            k = nn(xt, wk[...])
            q_raw[r, :] = q
            k_raw[r, :] = k
            v_low[r, :] = nn(xt, wv[...]).astype(BF16)
            sums[yl * 4 + z, :, r] = both(row_sums(q * q), row_sums(k * k))

        exchange = Exchange(sums, esem, fsem)
        exchange.start()
        save(q_raw, q_raw_out)
        save(k_raw, k_raw_out)
        save(v_low, v_out)
        exchange.finish()
        down_pair.start()
        for item in large:
            item.forward()
            item.forward_y()
        scales[...] = spread(lax.rsqrt(exchange.sum() * (1.0 / 2048) + EPS))
        save(scales, scale_out)

        @tiles(1024, 256)
        def _(r):
            cos, sin = cosine[r, :], sine[r, :]
            for source, gain, s, target, factor in (
                (q_raw, q_gain, 0, q_rot, SCALE),
                (k_raw, k_gain, 128, k_rot, 1.0),
            ):
                scale = scales[r, s : s + 128]
                for h in (0, 128):
                    v = source[r, h : h + 128] * scale * gain[:, h : h + 128]
                    v = v * cos + pltpu.roll(v, 64, 1) * sin
                    target[r, h : h + 128] = (v * factor).astype(BF16)

        save(q_rot, q_rot_out)
        save(k_rot, k_rot_out)

        for h in (0, 128):
            cols = slice(h, h + 128)
            for i in range(4):
                low = i * 256
                block = slice(low, low + 256)
                q = q_rot[block, cols]
                s1 = diagonal_mask(nt(q, k_rot[block, cols]), low, length)
                peak = jnp.max(s1, 1, keepdims=True)
                if i:
                    s0 = nt(q, k_rot[0:low, cols])
                    peak = jnp.maximum(peak, jnp.max(s0, 1, keepdims=True))
                e1 = jnp.exp(s1 - peak)
                total = jnp.sum(e1, 1, keepdims=True)
                out = nn(e1.astype(BF16), v_low[block, cols])
                if i:
                    e0 = jnp.exp(s0 - peak)
                    total += jnp.sum(e0, 1, keepdims=True)
                    out += nn(e0.astype(BF16), v_low[0:low, cols])
                mixed[block, cols] = (out / total).astype(BF16)
                lse[block, cols] = jnp.broadcast_to(peak + jnp.log(total), (256, 128))

        save(mixed, mixed_out)
        save(lse, lse_out)
        scatter = ScatterTensor(part, bufs, ssem, rsem)

        def project(half):
            s = pl.ds(pl.multiple_of(half * 512, 512), 512)
            m = mixed[s, :]

            @tiles(2048, 512)
            def _(n):
                part[s, n] = nn(m, wo[:, n]).astype(BF16)

        scatter.run(project)
        for item in large:
            item.share()
        scatter.middle()
        for item in large:
            item.forward_far()
        scatter.later()
        for item in large:
            item.share_far()
        scatter.finish(branch)
        for item in large:
            item.finish()
        down_pair.wait()
        for copy in saves:
            copy.wait()

    S = jax.ShapeDtypeStruct
    acts = [((1024, 256), F32), ((1024, 256), F32)] + [((1024, 256), BF16)] * 4
    acts += [((1024, 256), F32)] * 2
    outs = [S((1024, 2048), BF16)] + [S(f, BF16) for f in full] + [S(*a) for a in acts]
    outs.append(S((128, 2048), F32))
    D = DMA
    return pl.pallas_call(
        attention_step,
        out_shape=outs,
        in_specs=[ANY] * 8 + [SMEM] + [VM] * 4,
        out_specs=[ANY] * 16 + [VM],
        scratch_shapes=[pltpu.VMEM((1024, 2048), BF16)]
        + [pltpu.VMEM(f, BF16) for f in full[:4]]
        + [pltpu.VMEM(*a) for a in acts]
        + [pltpu.VMEM((1024, 2048), BF16), pltpu.VMEM((8, 8, 1024), F32)]
        + ScatterTensor.scratch()
        + [D((23,)), D((23,)), D((17,)), D((17,)), D((7, 21)), D((7, 21)), D((7,)), D((7,)), D((24,)), D],
        compiler_params=params(1),
        name="attention_step",
    )(tokens, *weights, lengths, q_gain, k_gain, *tables)


def mlp(tokens, lengths, branch, cotangent, attn_gain, mlp_gain, weights, w_down):
    def mlp_step(
        lengths, tokens, branch, cotangent, attn_gain, mlp_gain, wg_in, wu_in, wd_pair, wd_in,
        act, d_res, d_branch, attn_part, mlp_part, wg_out, wu_out, wd_out,
        x, dd, wg, wu, wd, gate_factor, silu, inner, dg, du, part, residual, total,
        *rest,
    ):
        bufs, (ssem, rsem, gsem, hsem, esem, fsem, tsem, usem, wsem, vsem, lsem) = rest[:8], rest[8:]
        yh, xx, c, yl, z = place()
        me = yl * 4 + z
        length = lengths[0]
        loads = [
            pltpu.make_async_copy(source, target, lsem.at[i])
            for i, (source, target) in enumerate(((wg_in, wg), (wu_in, wu)))
        ]
        for copy in loads:
            copy.start()
        greet(TENSOR_PEERS + DP_PEERS[:3:2] + DP_PEERS[4:])
        item = GatherDp(wd_in, wd, "col", wsem, vsem, lsem.at[pl.ds(2, 2)], wd_pair)
        item.start()
        own = rows(x, me)

        @tiles(128, 16)
        def _(r):
            b = branch[r, :]
            scale = lax.rsqrt(jnp.mean(b * b, 1, keepdims=True) + EPS)
            value = tokens[r, :].astype(F32) + b * scale * attn_gain[...]
            residual[r, :] = value
            own[r, :] = value.astype(BF16)

        gather = GatherTensor(x, gsem, hsem)
        gather.start()
        for copy in loads:
            copy.wait()

        def gate_up(slot):
            s = pl.ds(pl.multiple_of(slot * 128, 128), 128)
            xt = x[s, :]

            @tiles(1024, 512)
            def _(n):
                gate = nn(xt, wg[:, n])
                up = nn(xt, wu[:, n])
                sigmoid = jax.nn.sigmoid(gate)
                low = gate * sigmoid
                silu[s, n] = low.astype(BF16)
                gate_factor[s, n] = (up * (sigmoid + low * (1.0 - sigmoid))).astype(BF16)
                inner[s, n] = (low * up).astype(BF16)

        def spread_down(stage):
            if stage == 0:
                item.forward()
                item.forward_far()
            else:
                item.share()
                item.share_far()

        gather.run(gate_up, spread_down)
        item.finish()

        def down(half):
            s = pl.ds(pl.multiple_of(half * 512, 512), 512)
            it = inner[s, :]

            @tiles(2048, 512)
            def _(n):
                part[s, n] = nn(it, wd[:, n]).astype(BF16)

        scatter = ScatterTensor(part, bufs, ssem, rsem)
        scatter.run(down)
        scatter.middle()
        scatter.later()
        scatter.finish(total)
        mlp_part[...] = jnp.zeros_like(mlp_part)
        attn_part[...] = jnp.zeros_like(attn_part)
        own_d = rows(dd, me)

        @tiles(128, 16)
        def _(r):
            v = total[r, :]
            position = lax.broadcasted_iota(jnp.int32, (16, 1), 0) + (me * 128 + r.start)
            ok = position < length
            scale = lax.rsqrt(jnp.mean(v * v, 1, keepdims=True) + EPS)
            normal = v * scale
            act[r, :] = jnp.where(ok, residual[r, :] + normal * mlp_gain[...], 0.0).astype(BF16)
            grad = jnp.where(ok, cotangent[r, :].astype(F32), 0.0)
            d_res[r, :] = grad
            mlp_part[...] += jnp.sum(grad * normal, 0, keepdims=True)
            weighted = mlp_gain[...] * grad
            mean = jnp.mean(v * weighted, 1, keepdims=True)
            own_d[r, :] = (scale * weighted - v * (scale * scale * scale * mean)).astype(BF16)

        gather = GatherTensor(dd, esem, fsem)
        gather.start()

        def d_inner(slot):
            s = pl.ds(pl.multiple_of(slot * 128, 128), 128)
            dt = dd[s, :]

            @tiles(1024, 512)
            def _(n):
                d = nt(dt, wd[n, :])
                dg[s, n] = (d * gate_factor[s, n].astype(F32)).astype(BF16)
                du[s, n] = (d * silu[s, n].astype(F32)).astype(BF16)

        gather.run(d_inner)

        def d_input(half):
            s = pl.ds(pl.multiple_of(half * 512, 512), 512)
            g, u = dg[s, :], du[s, :]

            @tiles(2048, 512)
            def _(n):
                part[s, n] = (nt(g, wg[n, :]) + nt(u, wu[n, :])).astype(BF16)

        scatter = ScatterTensor(part, bufs, tsem, usem)
        scatter.run(d_input)

        @tiles(1024, 512)
        def _(m):
            @tiles(2048, 1024)
            def _(n):
                wd[m, n] = tn(inner[:, m], dd[:, n]).astype(BF16)

        saves = [pltpu.make_async_copy(wd, wd_out, lsem.at[0])]
        saves[0].start()
        scatter.middle()

        @tiles(2048, 512)
        def _(m):
            wg[m, :] = tn(x[:, m], dg[...]).astype(BF16)

        saves.append(pltpu.make_async_copy(wg, wg_out, lsem.at[1]))
        saves[1].start()
        scatter.later()

        @tiles(2048, 512)
        def _(m):
            wu[m, :] = tn(x[:, m], du[...]).astype(BF16)

        saves.append(pltpu.make_async_copy(wu, wu_out, lsem.at[2]))
        saves[2].start()
        scatter.finish(total)

        @tiles(128, 16)
        def _(r):
            grad = d_res[r, :] + total[r, :]
            d_res[r, :] = grad
            b = branch[r, :]
            scale = lax.rsqrt(jnp.mean(b * b, 1, keepdims=True) + EPS)
            attn_part[...] += jnp.sum(grad * b * scale, 0, keepdims=True)
            weighted = attn_gain[...] * grad
            mean = jnp.mean(b * weighted, 1, keepdims=True)
            d_branch[r, :] = (scale * weighted - b * (scale * scale * scale * mean)).astype(BF16)

        for copy in saves:
            copy.wait()

    S = jax.ShapeDtypeStruct
    D = DMA
    W = pltpu.VMEM
    return pl.pallas_call(
        mlp_step,
        out_shape=[
            S((128, 2048), BF16),
            S((128, 2048), F32),
            S((128, 2048), BF16),
            S((1, 2048), F32),
            S((1, 2048), F32),
            S((2048, 1024), BF16),
            S((2048, 1024), BF16),
            S((1024, 2048), BF16),
        ],
        in_specs=[SMEM] + [VM] * 5 + [ANY] * 4,
        out_specs=[VM] * 5 + [ANY] * 3,
        scratch_shapes=[W((1024, 2048), BF16)] * 2
        + [W((2048, 1024), BF16)] * 2
        + [W((1024, 2048), BF16)]
        + [W((1024, 1024), BF16)] * 5
        + [W((1024, 2048), BF16)]
        + [W((128, 2048), F32)] * 2
        + ScatterTensor.scratch()
        + [D((23,))] * 2
        + [D((17,))] * 4
        + [D((23,))] * 2
        + [D((21,))] * 2
        + [D((4,))],
        compiler_params=params(2),
        name="mlp_step",
    )(lengths, tokens, branch, cotangent, attn_gain, mlp_gain, *weights, w_down)


class SumAll:
    def __init__(self, slots, hold, boxes, ssem, rsem):
        self.exchange = Exchange(slots, ssem, rsem)
        self.hold, self.boxes = hold, boxes
        self.copies = []
        for i, peer in enumerate(DP_PEERS):
            k = (1, 1, 1, 2, 0)[i]
            self.copies.append(remote(hold.at[k], boxes.at[i], (ssem, rsem), 7 + i, peer))

    def start(self):
        self.exchange.start()

    def core(self):
        self.exchange.finish()
        self.hold[0] = self.exchange.sum()
        self.copies[4].start()

    def along_x(self):
        self.copies[4].wait()
        self.hold[1] = self.hold[0] + self.boxes[4]
        for copy in self.copies[:3]:
            copy.start()

    def along_y(self):
        for copy in self.copies[:3]:
            copy.wait()
        self.hold[2] = self.hold[1] + self.boxes[0] + self.boxes[1] + self.boxes[2]
        self.copies[3].start()

    def finish(self, out):
        self.copies[3].wait()
        out[...] = self.hold[2] + self.boxes[3]


def attention_backward(lengths, own, d_res, x, weights, saved, q_gain, k_gain, parts, tables, grads):
    kinds = ("row", "row", "row", "col", "row", "row", "col")
    blocks = ((128, 256),) * 3 + ((256, 128), (128, 1024), (128, 1024), (1024, 128))

    def backward_step(
        lengths, own, d_res, q_gain_all, k_gain_all, attn_part, mlp_part, cosine, sine, x_in, w0, w1, w2, w3,
        q_raw_in, k_raw_in, q_rot_in, k_rot_in, v_in, mixed_in, lse_in, scale_in, g4, g5, g6,
        input_grad, o0, o1, o2, o3, o4, o5, o6, gain_sums,
        x, wq, wk, wv, wo, q_raw, k_raw, q_rot, k_rot, v_low, mixed, lse, scales,
        p4, p5, p6, do, dq, dk, dv, dqr, dkr, dvr, part, sums, gain_slots, gain_hold, gain_boxes,
        *rest,
    ):
        bufs, (ssem, rsem), rest = rest[:8], rest[8:10], rest[10:]
        dp_bufs, rest = [rest[8 * i : 8 * i + 8] for i in range(7)], rest[56:]
        gsem, hsem, esem, fsem, isem, jsem, lsem = rest
        yh, xx, c, yl, z = place()
        me = yl * 4 + z
        own_columns = pl.ds(pl.multiple_of(me * 256, 256), 256)
        q_gain, k_gain = q_gain_all[:, own_columns], k_gain_all[:, own_columns]
        length = lengths[0]
        first = pltpu.make_async_copy(own, rows(x, me), lsem.at[0])
        first.start()
        pairs = ((g4, p4), (g5, p5), (g6, p6), (w3, wo), (mixed_in, mixed), (q_rot_in, q_rot))
        pairs += ((k_rot_in, k_rot), (v_in, v_low), (lse_in, lse), (q_raw_in, q_raw))
        pairs += ((k_raw_in, k_raw), (scale_in, scales), (w0, wq), (w1, wk), (w2, wv))
        loads = [pltpu.make_async_copy(s, t, lsem.at[1 + i]) for i, (s, t) in enumerate(pairs)]
        for copy in loads:
            copy.start()
        greet(ALL_PEERS)
        first.wait()
        gather = GatherTensor(x, gsem, hsem)
        gather.start()
        for copy in loads[:3]:
            copy.wait()
        wholes = (wq, wk, wv, wo, p4, p5, p6)
        items = [ScatterDp(wholes[i], kinds[i], *dp_bufs[i]) for i in range(7)]
        small, large = items[:4], items[4:]
        for item in large:
            item.start()
        loads[3].wait()

        def d_mixed(slot):
            s = pl.ds(pl.multiple_of(slot * 128, 128), 128)
            do[s, :] = nt(x[s, :], wo[...]).astype(BF16)

        def along_x(stage):
            if stage == 0:
                for item in large:
                    item.along_x()

        gather.run(d_mixed, along_x)
        for copy in loads[4:]:
            copy.wait()

        @tiles(2048, 512)
        def _(n):
            wo[:, n] = tn(mixed[...], x[:, n]).astype(BF16)

        reload = pltpu.make_async_copy(x_in, x, lsem.at[0])
        reload.start()

        for h in (0, 128):
            cols = slice(h, h + 128)
            for i in range(4):
                low = i * 256
                block = slice(low, low + 256)
                q, d = q_rot[block, cols], do[block, cols]
                top = lse[block, h : h + 1]
                k1, v1 = k_rot[block, cols], v_low[block, cols]
                p1 = jnp.exp(diagonal_mask(nt(q, k1), low, length) - top)
                dp1 = nt(d, v1)
                delta = jnp.sum(p1 * dp1, 1, keepdims=True)
                if i:
                    k0, v0 = k_rot[0:low, cols], v_low[0:low, cols]
                    p0 = jnp.exp(nt(q, k0) - top)
                    dp0 = nt(d, v0)
                    delta += jnp.sum(p0 * dp0, 1, keepdims=True)
                ds1 = (p1 * (dp1 - delta)).astype(BF16)
                dq_block = nn(ds1, k1)
                dk[block, cols] = tn(ds1, q)
                dv[block, cols] = tn(p1.astype(BF16), d)
                if i:
                    ds0 = (p0 * (dp0 - delta)).astype(BF16)
                    dq_block += nn(ds0, k0)
                    dk[0:low, cols] += tn(ds0, q)
                    dv[0:low, cols] += tn(p0.astype(BF16), d)
                dq[block, cols] = dq_block

        q_total, k_total = [], []
        for i in range(4):
            r = slice(i * 256, i * 256 + 256)
            cos, sin = cosine[r, :], sine[r, :]
            for source, raw, gain, s, factor, totals in (
                (dq, q_raw, q_gain, 0, SCALE, q_total),
                (dk, k_raw, k_gain, 128, 1.0, k_total),
            ):
                scale = scales[r, s : s + 128]
                part_sums = []
                for h in (0, 128):
                    v = source[r, h : h + 128] * factor
                    v = v * cos - pltpu.roll(v, 64, 1) * sin
                    w = v * raw[r, h : h + 128]
                    part_sums.append(jnp.sum(w * scale, 0, keepdims=True))
                    source[r, h : h + 128] = v * gain[:, h : h + 128]
                totals.append(jnp.concatenate(part_sums, 1))
            sums[me, :, r] = both(
                row_sums(dq[r, :] * q_raw[r, :]), row_sums(dk[r, :] * k_raw[r, :])
            )
            dvr[r, :] = dv[r, :].astype(BF16)
        exchange = Exchange(sums, esem, fsem)
        exchange.start()
        row = lax.broadcasted_iota(jnp.int32, (8, 1024), 0)
        column = lax.broadcasted_iota(jnp.int32, (8, 1024), 1)
        message = jnp.zeros((8, 1024), F32)
        for k, line in enumerate((attn_part, attn_part, mlp_part, mlp_part)):
            line = line[:, 1024 * (k % 2) : 1024 * (k % 2) + 1024]
            message = jnp.where(row == 4 + k, line, message)
        for first_row, totals in ((0, q_total), (2, k_total)):
            line = jnp.concatenate([totals[0] + totals[1] + totals[2] + totals[3]] * 4, 1)
            message += jnp.where((row == first_row + yl) & (column // 256 == z), line, 0.0)
        gain_slots[me] = message
        total_gain = SumAll(gain_slots, gain_hold, gain_boxes, isem, jsem)
        total_gain.start()
        for item in large:
            item.forward()
        exchange.finish()
        means = spread(exchange.sum() * (1.0 / 2048))
        for i in range(4):
            r = slice(i * 256, i * 256 + 256)
            for source, raw, s, target in ((dq, q_raw, 0, dqr), (dk, k_raw, 128, dkr)):
                scale = scales[r, s : s + 128]
                factor = scale * scale * scale * means[r, s : s + 128]
                for h in (0, 128):
                    target[r, h : h + 128] = (
                        scale * source[r, h : h + 128] - raw[r, h : h + 128] * factor
                    ).astype(BF16)
        total_gain.core()

        def d_input(half):
            s = pl.ds(pl.multiple_of(half * 512, 512), 512)
            a, b, d = dqr[s, :], dkr[s, :], dvr[s, :]

            @tiles(2048, 512)
            def _(n):
                part[s, n] = (nt(a, wq[n, :]) + nt(b, wk[n, :]) + nt(d, wv[n, :])).astype(BF16)

        scatter = ScatterTensor(part, bufs, ssem, rsem)
        scatter.run(d_input)
        reload.wait()

        @tiles(2048, 512)
        def _(m):
            xt = x[:, m].T
            wq[m, :] = nn(xt, dqr[...]).astype(BF16)
            wk[m, :] = nn(xt, dkr[...]).astype(BF16)
            wv[m, :] = nn(xt, dvr[...]).astype(BF16)

        for item in small:
            item.start()
        total_gain.along_x()
        scatter.middle()
        for item in small:
            item.along_x()
        for item in large:
            item.along_y()
        scatter.later()
        total_gain.along_y()
        for item in small:
            item.forward()
        scatter.finish(input_grad)

        @tiles(128, 16)
        def _(r):
            input_grad[r, :] += d_res[r, :]

        for item, out in zip(large, (o4, o5, o6)):
            item.finish(out)
        for item in small:
            item.along_y()
        total_gain.finish(gain_sums)
        for item, out in zip(small, (o0, o1, o2, o3)):
            item.finish(out)

    S = jax.ShapeDtypeStruct
    D = DMA
    W = pltpu.VMEM
    acts = [((1024, 256), F32)] * 2 + [((1024, 256), BF16)] * 4 + [((1024, 256), F32)] * 2
    scratch = [W((1024, 2048), BF16)] + [W((2048, 256), BF16)] * 3 + [W((256, 2048), BF16)]
    scratch += [W(*a) for a in acts]
    scratch += [W((2048, 1024), BF16)] * 2 + [W((1024, 2048), BF16), W((1024, 256), BF16)]
    scratch += [W((1024, 256), F32)] * 3 + [W((1024, 256), BF16)] * 3 + [W((1024, 2048), BF16)]
    scratch += [W((8, 8, 1024), F32)] * 2 + [W((3, 8, 1024), F32), W((5, 8, 1024), F32)]
    scratch += ScatterTensor.scratch() + [D((23,))] * 2
    for b in blocks:
        scratch += ScatterDp.scratch(b)
    scratch += [D((17,)), D((17,)), D((7,)), D((7,)), D((12,)), D((12,)), D((16,))]
    return pl.pallas_call(
        backward_step,
        out_shape=[S((128, 2048), F32)] + [S(b, F32) for b in blocks] + [S((8, 1024), F32)],
        in_specs=[SMEM, ANY] + [VM] * 7 + [ANY] * 16,
        out_specs=[VM] * 9,
        scratch_shapes=scratch,
        compiler_params=params(3),
        name="backward_step",
    )(lengths, own, d_res, q_gain, k_gain, *parts, *tables, x, *weights, *saved, *grads)


def hand_over(*arrays):
    n = len(arrays)

    def hand_over_step(*refs):
        held, (lsem, ssem) = refs[2 * n : 3 * n], refs[3 * n :]
        loads = [pltpu.make_async_copy(refs[i], held[i], lsem.at[i]) for i in range(n)]
        stores = [pltpu.make_async_copy(held[i], refs[n + i], ssem.at[i]) for i in range(n)]
        for copy in loads:
            copy.start()
        for load, store in zip(loads, stores):
            load.wait()
            store.start()
        for copy in stores:
            copy.wait()

    return pl.pallas_call(
        hand_over_step,
        out_shape=[jax.ShapeDtypeStruct(a.shape, a.dtype) for a in arrays],
        in_specs=[ANY] * n,
        out_specs=[ANY] * n,
        scratch_shapes=[pltpu.VMEM(a.shape, a.dtype) for a in arrays] + [DMA((n,))] * 2,
        compiler_params=pltpu.CompilerParams(vmem_limit_bytes=63 << 20),
        name="hand_over_step",
    )(*arrays)


def local(
    tokens, lengths, w_query, w_key, w_value, w_out, w_gate, w_up, w_down,
    q_gain, k_gain, attn_gain, mlp_gain, cotangent,
):
    tables = rope_tables()
    weights = (w_query, w_key, w_value, w_out, w_gate, w_up, w_down)
    x, *res = attention_forward(tokens[0], lengths, weights, q_gain[None], k_gain[None], tables)
    weights, saved, branch = res[:7], res[7:15], res[15]
    act, d_res, d_branch, attn_part, mlp_part, *grads = mlp(
        tokens[0], lengths, branch, cotangent[0], attn_gain[None], mlp_gain[None], weights[4:], w_down
    )
    input_grad, *owned, sums = attention_backward(
        lengths,
        d_branch,
        d_res,
        x,
        weights[:4],
        saved,
        q_gain[None],
        k_gain[None],
        (attn_part, mlp_part),
        tables,
        grads,
    )
    act, input_grad, *owned = hand_over(act, input_grad, *owned)
    sums = sums.reshape(4, 2048)
    return (act[None], input_grad[None], *owned, sums[0], sums[1], sums[2], sums[3])


def solution(mesh):
    return jax.shard_map(
        local,
        mesh=mesh,
        in_specs=(
            P("dp", "tensor", None),
            P("dp"),
            P("dp", "tensor"),
            P("dp", "tensor"),
            P("dp", "tensor"),
            P("tensor", "dp"),
            P("dp", "tensor"),
            P("dp", "tensor"),
            P("tensor", "dp"),
            P(),
            P(),
            P(),
            P(),
            P("dp", "tensor", None),
        ),
        out_specs=(
            P("dp", "tensor", None),
            P("dp", "tensor", None),
            P("dp", "tensor"),
            P("dp", "tensor"),
            P("dp", "tensor"),
            P("tensor", "dp"),
            P("dp", "tensor"),
            P("dp", "tensor"),
            P("tensor", "dp"),
            P(),
            P(),
            P(),
            P(),
        ),
        check_vma=False,
    )
```

```python
import jax
import jax.numpy as jnp
import numpy as np
from jax import lax
from jax.experimental import pallas as pl
from jax.experimental.pallas import tpu as pltpu
from jax.sharding import PartitionSpec as P

HEAD_DIM = 128
EPS = 1e-06
THETA = 500000.0
MESH = pl.DeviceIdType.MESH
BF16 = jnp.bfloat16
F32 = jnp.float32
ANY = pl.BlockSpec(memory_space=pl.ANY)
VM = pl.BlockSpec(memory_space=pltpu.VMEM)
DMA = pltpu.SemaphoreType.DMA
CUT = 896
WIDTH = 2048


def place():
    d = lax.axis_index("dp")
    t = lax.axis_index("tensor")
    return d // 8, lax.rem(d // 2, 4), lax.rem(d, 2), t // 4, lax.rem(t, 4)


def other(dyh=0, dx=0, dc=0, dyl=0, dz=0):
    yh, x, c, yl, z = place()
    return (
        lax.rem(yh + dyh, 2) * 8 + lax.rem(x + dx, 4) * 2 + lax.rem(c + dc, 2),
        lax.rem(yl + dyl, 2) * 4 + lax.rem(z + dz, 4),
    )


TENSOR_PEERS = (dict(dz=1), dict(dz=3), dict(dyl=1))
DP_PEERS = (dict(dx=1), dict(dx=2), dict(dx=3), dict(dyh=1), dict(dc=1))
SMEM = pl.BlockSpec(memory_space=pltpu.SMEM)


def greet(peers):
    barrier = pltpu.get_barrier_semaphore()
    for peer in peers:
        pl.semaphore_signal(barrier, 1, device_id=other(**peer), device_id_type=MESH)
    pl.semaphore_wait(barrier, len(peers))


def remote(src, dst, sems, index, peer):
    ssem, rsem = sems
    return pltpu.make_async_remote_copy(
        src_ref=src,
        dst_ref=dst,
        send_sem=ssem.at[index],
        recv_sem=rsem.at[index],
        device_id=other(**peer),
        device_id_type=MESH,
    )


def rows(ref, slot):
    return ref.at[pl.ds(pl.multiple_of(slot * 128, 128), 128)]


def halves(ref):
    half = ref.shape[0] // 2
    return ref.at[pl.ds(0, half)], ref.at[pl.ds(half, half)]


def add_into(out, *terms):
    @pl.loop(0, out.shape[0] // 16)
    def _(i):
        r = pl.ds(pl.multiple_of(i * 16, 16), 16)
        if len(terms) == 2 and out.dtype == BF16:
            out[r, :] = terms[0][r, :] + terms[1][r, :]
        else:
            total = terms[0][r, :].astype(F32)
            for term in terms[1:]:
                total += term[r, :].astype(F32)
            out[r, :] = total.astype(out.dtype)


class RingGather:
    COPIES = 6

    def __init__(self, block, axis, sems, base, source=None):
        up, down = {axis: 1}, {axis: 3}
        src = halves(block(0) if source is None else source)
        own, behind, ahead = halves(block(0)), halves(block(3)), halves(block(1))
        self.copies = [
            remote(src[0], own[0], sems, base, up),
            remote(src[1], own[1], sems, base + 1, down),
            remote(src[1], own[1], sems, base + 2, up),
            remote(src[0], own[0], sems, base + 3, down),
            remote(behind[0], behind[0], sems, base + 4, up),
            remote(ahead[1], ahead[1], sems, base + 5, down),
        ]

    def start(self):
        for copy in self.copies[:4]:
            copy.start()

    def forward(self):
        for i in range(2):
            self.copies[i].wait_recv()
            self.copies[4 + i].start()

    def behind(self):
        self.copies[2].wait_recv()

    def ahead(self):
        self.copies[3].wait_recv()

    def far(self):
        for copy in self.copies[4:]:
            copy.wait_recv()

    def drain(self):
        for copy in self.copies:
            copy.wait_send()


class RingReduce:
    COPIES = 6

    @staticmethod
    def scratch(n, m):
        return [pltpu.VMEM((2, n // 2, m), BF16), pltpu.VMEM((2, n, m), BF16)]

    def __init__(self, block, axis, part, full, sems, base):
        up, down = {axis: 1}, {axis: 3}
        one, two, three = halves(block(1)), halves(block(2)), halves(block(3))
        from_behind, from_ahead = halves(full.at[0]), halves(full.at[1])
        self.adds = ((one[0], part.at[0]), (three[1], part.at[1]))
        self.terms = (block(0), full.at[0], full.at[1])
        self.copies = [
            remote(two[0], part.at[0], sems, base, up),
            remote(two[1], part.at[1], sems, base + 1, down),
            remote(one[1], from_behind[1], sems, base + 2, up),
            remote(three[0], from_ahead[0], sems, base + 3, down),
            remote(one[0], from_behind[0], sems, base + 4, up),
            remote(three[1], from_ahead[1], sems, base + 5, down),
        ]

    def start(self):
        for copy in self.copies[:4]:
            copy.start()

    def forward(self):
        for i in range(2):
            self.copies[i].wait_recv()
            add_into(self.adds[i][0], *self.adds[i])
            self.copies[4 + i].start()

    def arrive(self):
        for copy in self.copies[2:]:
            copy.wait_recv()

    def drain(self):
        for copy in self.copies:
            copy.wait_send()


class GatherTensor:
    COPIES = 21

    def __init__(self, buf, ssem, rsem, cut=CUT):
        yh, x, c, yl, z = place()
        self.yl, self.z = yl, z
        sems = (ssem, rsem)
        slot = lambda k, i: rows(buf, lax.rem(yl + k, 2) * 4 + lax.rem(z + i, 4))
        low = lambda ref: ref.at[:, pl.ds(0, cut)]
        high = lambda ref: ref.at[:, pl.ds(cut, WIDTH - cut)]
        self.ring = RingGather(lambda i: slot(0, i), "dz", sems, 0)
        self.pair_ring = RingGather(lambda i: high(slot(1, i)), "dz", sems, 6)
        own = slot(0, 0)
        pair = dict(dyl=1)
        self.high = remote(high(own), high(own), sems, 12, pair)
        self.low = []
        for n, i in enumerate((0, 3, 1, 2)):
            for half in halves(low(slot(0, i))):
                self.low.append(remote(half, half, sems, 13 + len(self.low), pair))

    def start(self):
        self.high.start()
        self.ring.start()
        self.low[0].start()
        self.low[1].start()

    def run(self, process, spare=None):
        yl, z = self.yl, self.z

        @pl.loop(0, 2)
        def _(k):
            @pl.when(k == 1)
            def _():
                self.ring.forward()
                self.low[2].start()
                self.low[5].start()
                self.high.wait_recv()
                self.pair_ring.start()
                self.ring.behind()
                self.low[3].start()
                self.ring.ahead()
                self.low[4].start()
                self.low[0].wait_recv()
                self.low[1].wait_recv()

            process(lax.rem(yl + k, 2) * 4 + z)

        if spare is not None:
            spare(0)

        @pl.loop(0, 6)
        def _(j):
            @pl.when(j == 2)
            def _():
                self.ring.far()
                self.low[6].start()
                self.low[7].start()
                self.pair_ring.forward()

            @pl.when(j == 3)
            def _():
                if spare is not None:
                    spare(1)
                self.pair_ring.behind()
                self.low[2].wait_recv()
                self.low[3].wait_recv()

            @pl.when(j == 4)
            def _():
                self.pair_ring.ahead()
                self.low[4].wait_recv()
                self.low[5].wait_recv()

            @pl.when(j == 5)
            def _():
                self.pair_ring.far()
                self.low[6].wait_recv()
                self.low[7].wait_recv()

            i = lax.rem(j, 3)
            step = (3 * i * i - 7 * i + 6) // 2
            process(lax.rem(yl + j // 3, 2) * 4 + lax.rem(z + step, 4))

        self.ring.drain()
        self.pair_ring.drain()
        for copy in [self.high] + self.low:
            copy.wait_send()


class ScatterTensor:
    COPIES = 23

    @staticmethod
    def scratch():
        return (
            [pltpu.VMEM((4, 128, CUT), BF16), pltpu.VMEM((128, WIDTH - CUT), BF16)]
            + RingReduce.scratch(128, CUT)
            + RingReduce.scratch(128, WIDTH - CUT) * 2
        )

    def __init__(self, part, bufs, ssem, rsem):
        yh, x, c, yl, z = place()
        self.yl = yl
        self.from_pair, self.last = bufs[0], bufs[1]
        sems = (ssem, rsem)
        slot = lambda k, i: rows(part, lax.rem(yl + k, 2) * 4 + lax.rem(z + i, 4))
        low = lambda k, i: slot(k, i).at[:, pl.ds(0, CUT)]
        high = lambda k, i: slot(k, i).at[:, pl.ds(CUT, WIDTH - CUT)]
        pair = dict(dyl=1)
        self.low = lambda i: low(0, i)
        self.low_ring = RingReduce(lambda i: low(0, i), "dz", bufs[2], bufs[3], sems, 0)
        self.pair_ring = RingReduce(lambda i: high(1, i), "dz", bufs[4], bufs[5], sems, 6)
        self.own_ring = RingReduce(lambda i: high(0, i), "dz", bufs[6], bufs[7], sems, 12)
        self.first = [remote(low(1, i), bufs[0].at[i], sems, 18 + i, pair) for i in range(4)]
        self.second = remote(high(1, 0), bufs[1], sems, 22, pair)

    def run(self, process):
        @pl.loop(0, 4)
        def _(k):
            process(lax.rem(self.yl + 1 + k // 2, 2), lax.rem((k + 1) // 2, 2))

            @pl.when(k == 0)
            def _():
                for i in (2, 1, 3, 0):
                    self.first[i].start()

            @pl.when(k == 1)
            def _():
                self.pair_ring.start()

    def add_first(self, i):
        self.first[i].wait_recv()
        add_into(self.low(i), self.low(i), self.from_pair.at[i])

    def step(self, n):
        low = self.low_ring.copies
        if n == 0:
            self.pair_ring.forward()
            self.own_ring.start()
            self.add_first(2)
            low[0].start()
            low[1].start()
        if n == 1:
            self.add_first(1)
            low[2].start()
            self.own_ring.forward()
        if n == 2:
            self.pair_ring.arrive()
            add_into(self.pair_ring.terms[0], *self.pair_ring.terms)
            self.second.start()
            self.add_first(3)
            low[3].start()
        if n == 3:
            self.low_ring.forward()
            self.add_first(0)

    def finish(self, out):
        self.own_ring.arrive()
        self.second.wait_recv()
        add_into(out.at[:, pl.ds(CUT, WIDTH - CUT)], *self.own_ring.terms, self.last)
        self.low_ring.arrive()
        add_into(out.at[:, pl.ds(0, CUT)], *self.low_ring.terms)
        for ring in (self.low_ring, self.pair_ring, self.own_ring):
            ring.drain()
        for copy in self.first + [self.second]:
            copy.wait_send()


def block_of(ref, kind, slot):
    if kind == "row":
        size = ref.shape[0] // 16
        return ref.at[pl.ds(pl.multiple_of(slot * size, size), size)]
    if kind == "folded":
        return ref.at[
            pl.ds(pl.multiple_of(lax.rem(slot, 8) * 128, 128), 128),
            pl.ds(pl.multiple_of(slot // 8 * 256, 256), 256),
        ]
    size = ref.shape[1] // 16
    return ref.at[:, pl.ds(pl.multiple_of(slot * size, size), size)]


class GatherDp:
    COPIES = 21

    def __init__(self, shard, out, kind, ssem, rsem, lsem):
        yh, x, c, yl, z = place()
        sems = (ssem, rsem)
        block = lambda k, i: block_of(
            out, kind, lax.rem(yh + k, 2) * 8 + lax.rem(x + i, 4) * 2 + c
        )
        self.local = pltpu.make_async_copy(shard, block(0, 0), lsem)
        self.ring = RingGather(lambda i: block(0, i), "dx", sems, 0, shard)
        self.far_ring = RingGather(lambda i: block(1, i), "dx", sems, 6)
        self.own_y = remote(shard, block(0, 0), sems, 12, dict(dyh=1))
        core = dict(dc=1)
        self.core = [remote(shard, block(0, 0), sems, 13, core)]
        for n in range(1, 8):
            ref = block(n // 4, n % 4)
            self.core.append(remote(ref, ref, sems, 13 + n, core))

    def start(self):
        self.ring.start()
        self.core[0].start()
        self.local.start()

    def forward(self):
        self.ring.forward()

    def forward_y(self):
        self.own_y.wait_recv()
        self.far_ring.start()
        self.core[4].start()

    def share(self):
        self.ring.behind()
        self.core[3].start()
        self.ring.ahead()
        self.core[1].start()
        self.ring.far()
        self.core[2].start()

    def forward_far(self):
        self.far_ring.forward()

    def share_far(self):
        self.far_ring.behind()
        self.core[7].start()
        self.far_ring.ahead()
        self.core[5].start()
        self.far_ring.far()
        self.core[6].start()

    def finish(self):
        for copy in self.core:
            copy.wait_recv()
        self.local.wait()
        self.ring.drain()
        self.far_ring.drain()
        for copy in [self.own_y] + self.core:
            copy.wait_send()


class ScatterDp:
    COPIES = 21

    @staticmethod
    def scratch(block):
        return (
            [pltpu.VMEM(block, BF16)]
            + RingReduce.scratch(*block) * 2
            + [DMA((21,)), DMA((21,))]
        )

    def __init__(self, part, kind, from_core, from_y, h0, f0, h1, f1, ssem, rsem):
        yh, x, c, yl, z = place()
        sems = (ssem, rsem)
        self.from_core, self.from_y = from_core, from_y
        block = lambda k, i, d: block_of(
            part, kind, lax.rem(yh + k, 2) * 8 + lax.rem(x + i, 4) * 2 + d
        )
        self.block = lambda k, i: block(k, i, c)
        self.core = [
            remote(block(n // 4, n % 4, 1 - c), from_core(n), sems, n, dict(dc=1))
            for n in range(8)
        ]
        self.ring = RingReduce(lambda i: block(0, i, c), "dx", h0, f0, sems, 8)
        self.far_ring = RingReduce(lambda i: block(1, i, c), "dx", h1, f1, sems, 14)
        self.last = remote(block(1, 0, c), from_y, sems, 20, dict(dyh=1))

    def start(self):
        for n in (6, 5, 7, 4, 2, 1, 3, 0):
            self.core[n].start()

    def add_core(self, n):
        self.core[n].wait_recv()
        ref = self.block(n // 4, n % 4)
        add_into(ref, ref, self.from_core(n))

    def along_x(self):
        for n in (6, 5, 7):
            self.add_core(n)
        self.far_ring.start()
        for n in (2, 1, 3):
            self.add_core(n)
        self.ring.start()
        for n in (4, 0):
            self.add_core(n)

    def forward(self):
        self.far_ring.forward()
        self.ring.forward()

    def along_y(self):
        self.far_ring.arrive()
        add_into(self.far_ring.terms[0], *self.far_ring.terms)
        self.last.start()

    def finish(self, out):
        self.ring.arrive()
        self.last.wait_recv()
        add_into(out, *self.ring.terms, self.from_y)
        self.ring.drain()
        self.far_ring.drain()
        for copy in self.core + [self.last]:
            copy.wait_send()


def params(cid):
    return pltpu.CompilerParams(
        collective_id=cid, has_side_effects=True, vmem_limit_bytes=65400 << 10
    )


def nn(a, b):
    return jnp.dot(a, b, preferred_element_type=F32)


def nt(a, b):
    return lax.dot_general(a, b, (((1,), (1,)), ((), ())), preferred_element_type=F32)


def tn(a, b):
    return lax.dot_general(a, b, (((0,), (0,)), ((), ())), preferred_element_type=F32)


def tiles(count, size):
    def run(body):
        @pl.loop(0, count // size)
        def _(i):
            body(pl.ds(pl.multiple_of(i * size, size), size))

    return run


def rope_table():
    frequency = THETA ** (-(np.arange(64, dtype=np.float32) * np.float32(2.0) / np.float32(HEAD_DIM)))
    angles = np.arange(1024, dtype=np.float32)[:, None] * frequency.astype(np.float32)[None, :]
    cosine, sine = np.cos(angles), np.sin(angles)
    return np.concatenate([cosine, sine], 1).astype(np.float32)


def cos_sin(table):
    turned = pltpu.roll(table, 64, 1)
    first = lax.broadcasted_iota(jnp.int32, table.shape, 1) < 64
    return jnp.where(first, table, turned), jnp.where(first, -turned, table)


class Exchange:
    PEERS = tuple(dict(dz=a, dyl=b) for b in range(2) for a in range(4) if a or b)

    def __init__(self, buf, ssem, rsem):
        yh, x, c, yl, z = place()
        self.buf = buf
        self.mine = buf.at[yl * 4 + z]
        self.copies = [
            remote(self.mine, self.mine, (ssem, rsem), i, peer)
            for i, peer in enumerate(self.PEERS)
        ]

    def start(self):
        for copy in self.copies:
            copy.start()

    def finish(self):
        for copy in self.copies:
            copy.wait_recv()
        for copy in self.copies:
            copy.wait_send()

    def sum(self):
        total = self.buf[0]
        for i in range(1, 8):
            total += self.buf[i]
        return total


def row_sums(values):
    return nt(jnp.ones((8, values.shape[1]), F32), values)


def spread(out, pair):
    row = lax.broadcasted_iota(jnp.int32, (8, 256), 0)
    column = lax.broadcasted_iota(jnp.int32, (8, 256), 1)
    for i in range(4):
        pick = jnp.where(row == column // 128 * 4 + i, 1.0, 0.0)
        out[pl.ds(256 * i, 256), :] = lax.dot_general(
            pair,
            pick,
            (((0,), (0,)), ((), ())),
            precision=lax.Precision.HIGHEST,
            preferred_element_type=F32,
        )


def note_sums(out, r, a, b):
    row = lax.broadcasted_iota(jnp.int32, (8, 256), 0)
    sums = jnp.where(row < 4, row_sums(a), row_sums(b))
    out[...] = jnp.where(lax.rem(row, 4) == r.start // 256, sums, out[...])


ALL_PEERS = Exchange.PEERS + DP_PEERS
SCALE = HEAD_DIM**-0.5


def diagonal_mask(scores, first, length):
    row = lax.broadcasted_iota(jnp.int32, scores.shape, 0)
    column = lax.broadcasted_iota(jnp.int32, scores.shape, 1)
    return jnp.where((column <= row) & (column + first < length), scores, -1e30)


class SumAll:
    def __init__(self, slots, hold, boxes, ssem, rsem):
        self.exchange = Exchange(slots, ssem, rsem)
        self.hold, self.boxes = hold, boxes
        self.copies = []
        for i, peer in enumerate(DP_PEERS):
            k = (1, 1, 1, 2, 0)[i]
            self.copies.append(remote(hold.at[k], boxes.at[i], (ssem, rsem), 7 + i, peer))

    def start(self):
        self.exchange.start()

    def core(self):
        self.exchange.finish()
        self.hold[0] = self.exchange.sum()
        self.copies[4].start()

    def along_x(self):
        self.copies[4].wait()
        self.hold[1] = self.hold[0] + self.boxes[4]
        for copy in self.copies[:3]:
            copy.start()

    def along_y(self):
        for copy in self.copies[:3]:
            copy.wait()
        self.hold[2] = self.hold[1] + self.boxes[0] + self.boxes[1] + self.boxes[2]
        self.copies[3].start()

    def finish(self, out):
        self.copies[3].wait()
        out[...] = self.hold[2] + self.boxes[3]


def whole_layer(tokens, lengths, cotangent, gains, weights, table):
    kinds = ("row", "row", "row", "col", "row", "row", "col")
    blocks = ((128, 256),) * 3 + ((256, 128), (128, 1024), (128, 1024), (1024, 128))

    def layer_step(
        lengths, cotangent, q_gain_all, k_gain_all, attn_gain, mlp_gain, table,
        tokens, i0, i1, i2, i3, i4, i5, i6,
        act, input_grad, o0, o1, o2, o3, o4, o5, o6,
        q_sum, k_sum, attn_sum, mlp_sum, x_kept, heads_kept, raw_kept,
        x, dd, wg, wu, wd, gate_factor, silu, inner, dg, du, part, residual, attn_part, mlp_part, q_line, k_line,
        wq, wk, wv, wo, stats, branch, do, dq, dk, dv, sums, gain_slots, gain_hold, gain_boxes,
        *rest,
    ):
        bufs, rest = rest[:8], rest[8:]
        dp_bufs, rest = [rest[7 * i : 7 * i + 7] for i in range(7)], rest[49:]
        s0, s1, s2, s3, g0, g1, g2, g3, esems, fsems, isems, wsems = [
            rest[2 * i : 2 * i + 2] for i in range(12)
        ]
        lsem, msem, ready = rest[24:]
        yh, xx, c, yl, z = place()
        me = yl * 4 + z
        length = lengths[0]
        total = input_grad
        own_columns = pl.ds(pl.multiple_of(me * 256, 256), 256)
        q_gain, k_gain = q_gain_all[:, own_columns], k_gain_all[:, own_columns]
        q_rot, k_rot, v_low, mixed = (dg.at[:, pl.ds(256 * i, 256)] for i in range(4))
        q_raw, k_raw, dvr = (du.at[:, pl.ds(256 * i, 256)] for i in range(3))
        dqr, dkr = q_raw, k_raw
        raw = du.at[:, pl.ds(0, 512)]
        load_heads = pltpu.make_async_copy(heads_kept, dg, msem.at[0])
        load_raw = pltpu.make_async_copy(raw_kept, raw, msem.at[2])
        reload = pltpu.make_async_copy(x_kept, x, msem.at[1])
        keep_x = pltpu.make_async_copy(dd, x_kept, msem.at[1])
        keep_heads = pltpu.make_async_copy(dg, heads_kept, msem.at[0])
        keep_raw = pltpu.make_async_copy(raw, raw_kept, msem.at[2])
        first = pltpu.make_async_copy(tokens, rows(dd, me), msem.at[3])
        first.start()
        greet(ALL_PEERS)
        shards = (i0, i1, i2, i3, i4, i5, i6)
        targets = (wq, wk, wv, wo, wg, wu, wd)
        spreads = [
            GatherDp(shards[i], targets[i], kinds[i], wsems[0].at[i], wsems[1].at[i], lsem.at[i])
            for i in range(7)
        ]
        small, large, down_weights = spreads[:4], spreads[4:6], spreads[6]
        for spread_item in small:
            spread_item.start()
            spread_item.own_y.start()
        first.wait()
        gather = GatherTensor(dd, *g0, 512)
        gather.start()

        def spread_small(stage):
            for spread_item in small:
                if stage == 0:
                    spread_item.forward()
                    spread_item.forward_y()
                else:
                    spread_item.share()
                    spread_item.forward_far()

        gather.run(lambda slot: None, spread_small)
        for spread_item in small:
            spread_item.share_far()
        for spread_item in large:
            spread_item.start()
            spread_item.own_y.start()
        for spread_item in small:
            spread_item.finish()
        sums[me] = jnp.zeros((8, 256), F32)
        keep_x.start()

        @tiles(1024, 256)
        def _(r):
            q = nn(dd[r, :], wq[...])
            k = nn(dd[r, :], wk[...])
            dq[r, :] = q
            dk[r, :] = k
            du[r, 0:256] = q.astype(BF16)
            du[r, 256:512] = k.astype(BF16)
            v_low[r, :] = nn(dd[r, :], wv[...]).astype(BF16)
            note_sums(sums.at[me], r, q * q, k * k)

        exchange = Exchange(sums, *esems)
        exchange.start()
        keep_raw.start()
        for spread_item in large:
            spread_item.forward()
        exchange.finish()
        for spread_item in large:
            spread_item.forward_y()
        down_weights.own_y.start()
        down_weights.start()
        spread(dv, lax.rsqrt(exchange.sum() * (1.0 / 2048) + EPS))
        narrow = lax.broadcasted_iota(jnp.int32, (1024, 128), 1) < 64
        stats[:, 128:256] = jnp.where(narrow, dv[:, 0:128], dv[:, 128:256])

        @tiles(1024, 256)
        def _(r):
            cos, sin = cos_sin(table[r, :])
            for source, gain, s, target, factor in (
                (dq, q_gain, 0, q_rot, SCALE),
                (dk, k_gain, 128, k_rot, 1.0),
            ):
                scale = dv[r, s : s + 128]
                for h in (0, 128):
                    v = source[r, h : h + 128] * scale * gain[:, h : h + 128]
                    v = v * cos + pltpu.roll(v, 64, 1) * sin
                    target[r, h : h + 128] = (v * factor).astype(BF16)

        @pl.loop(0, 2)
        def _(h):
            cols = pl.ds(pl.multiple_of(h * 128, 128), 128)
            mine = lax.broadcasted_iota(jnp.int32, (256, 128), 1) // 64 == h
            for i in range(4):
                low = i * 256
                block = slice(low, low + 256)
                q = q_rot[block, cols]
                near = diagonal_mask(nt(q, k_rot[block, cols]), low, length)
                peak = jnp.max(near, 1, keepdims=True)
                if i:
                    past = nt(q, k_rot[0:low, cols])
                    peak = jnp.maximum(peak, jnp.max(past, 1, keepdims=True))
                e1 = jnp.exp(near - peak)
                denom = jnp.sum(e1, 1, keepdims=True)
                out = nn(e1.astype(BF16), v_low[block, cols])
                if i:
                    e0 = jnp.exp(past - peak)
                    denom += jnp.sum(e0, 1, keepdims=True)
                    out += nn(e0.astype(BF16), v_low[0:low, cols])
                mixed[block, cols] = (out / denom).astype(BF16)
                lse = peak + jnp.log(denom)
                stats[block, 0:128] = jnp.where(mine, lse, stats[block, 0:128])

        keep_heads.start()

        def project(half, side):
            s = pl.ds(pl.multiple_of(half * 512, 512), 512)

            @pl.loop(0, 2)
            def _(i):
                n = pl.ds(pl.multiple_of(side * 1024 + i * 512, 512), 512)
                part[s, n] = nn(mixed[s, :], wo[:, n]).astype(BF16)

        scatter = ScatterTensor(part, bufs, *s0)
        scatter.run(project)
        scatter.step(0)
        for spread_item in large:
            spread_item.share()
            spread_item.forward_far()
        scatter.step(1)
        scatter.step(2)
        down_weights.forward()
        down_weights.forward_y()
        for spread_item in large:
            spread_item.share_far()
        scatter.step(3)
        scatter.finish(branch)
        own = rows(x, me)
        own_tokens = rows(dd, me)
        for copy in (keep_x, keep_raw, keep_heads):
            copy.wait()

        def tell(i):
            pl.semaphore_signal(ready.at[i], 1, device_id=other(dc=1), device_id_type=MESH)

        @tiles(128, 16)
        def _(r):
            b = branch[r, :]
            scale = lax.rsqrt(jnp.mean(b * b, 1, keepdims=True) + EPS)
            value = own_tokens[r, :].astype(F32) + b * scale * attn_gain[...]
            residual[r, :] = value
            own[r, :] = value.astype(BF16)

        gather = GatherTensor(x, *g1)
        gather.start()
        for spread_item in large:
            spread_item.finish()

        def gate_up(slot):
            s = pl.ds(pl.multiple_of(slot * 128, 128), 128)

            @tiles(1024, 512)
            def _(n):
                gate = nn(x[s, :], wg[:, n])
                up = nn(x[s, :], wu[:, n])
                sigmoid = jax.nn.sigmoid(gate)
                low = gate * sigmoid
                silu[s, n] = low.astype(BF16)
                gate_factor[s, n] = (up * (sigmoid + low * (1.0 - sigmoid))).astype(BF16)
                inner[s, n] = (low * up).astype(BF16)

        def spread_down(stage):
            if stage == 0:
                down_weights.share()
                down_weights.forward_far()
            else:
                down_weights.share_far()

        gather.run(gate_up, spread_down)
        down_weights.finish()

        def down(half, side):
            s = pl.ds(pl.multiple_of(half * 512, 512), 512)

            @pl.loop(0, 2)
            def _(i):
                n = pl.ds(pl.multiple_of(side * 1024 + i * 512, 512), 512)
                part[s, n] = nn(inner[s, :], wd[:, n]).astype(BF16)

        scatter = ScatterTensor(part, bufs, *s1)
        scatter.run(down)
        for n in range(4):
            scatter.step(n)
        scatter.finish(total)
        mlp_part[...] = jnp.zeros_like(mlp_part)
        attn_part[...] = jnp.zeros_like(attn_part)
        own_d = rows(dd, me)

        @tiles(128, 16)
        def _(r):
            v = total[r, :]
            position = lax.broadcasted_iota(jnp.int32, (16, 1), 0) + (me * 128 + r.start)
            ok = position < length
            scale = lax.rsqrt(jnp.mean(v * v, 1, keepdims=True) + EPS)
            normal = v * scale
            part[r, :] = jnp.where(ok, residual[r, :] + normal * mlp_gain[...], 0.0).astype(BF16)
            grad = jnp.where(ok, cotangent[r, :].astype(F32), 0.0)
            residual[r, :] = grad
            mlp_part[...] += jnp.sum(grad * normal, 0, keepdims=True)
            weighted = mlp_gain[...] * grad
            mean = jnp.mean(v * weighted, 1, keepdims=True)
            own_d[r, :] = (scale * weighted - v * (scale * scale * scale * mean)).astype(BF16)

        gather = GatherTensor(dd, *g2)
        gather.start()
        store_act = pltpu.make_async_copy(part.at[pl.ds(0, 128)], act, msem.at[1])
        store_act.start()

        def d_inner(slot):
            s = pl.ds(pl.multiple_of(slot * 128, 128), 128)

            @tiles(1024, 512)
            def _(n):
                d = nt(dd[s, :], wd[n, :])
                dg[s, n] = (d * gate_factor[s, n].astype(F32)).astype(BF16)
                du[s, n] = (d * silu[s, n].astype(F32)).astype(BF16)

        gather.run(d_inner)
        store_act.wait()
        tell(0)

        def d_input(half, side):
            s = pl.ds(pl.multiple_of(half * 512, 512), 512)

            @pl.loop(0, 2)
            def _(i):
                n = pl.ds(pl.multiple_of(side * 1024 + i * 512, 512), 512)
                part[s, n] = (nt(dg[s, :], wg[n, :]) + nt(du[s, :], wu[n, :])).astype(BF16)

        scatter = ScatterTensor(part, bufs, *s2)
        scatter.run(d_input)
        scatter.step(0)

        def down_grad(i):
            m = pl.ds(i * 512, 512)

            @tiles(2048, 512)
            def _(n):
                wd[m, n] = tn(inner[:, m], dd[:, n]).astype(BF16)

        def gate_grad(first):
            @pl.loop(first, first + 2)
            def _(i):
                m = pl.ds(pl.multiple_of(i * 512, 512), 512)

                @tiles(1024, 512)
                def _(n):
                    wg[m, n] = tn(x[:, m], dg[:, n]).astype(BF16)

        down_grad(0)
        down_grad(1)
        scatter.step(1)
        tell(1)

        def by_rows(ref):
            return lambda n: ref.at[pl.ds(n * 128, 128)]

        def by_columns(ref):
            return lambda n: ref.at[:, pl.ds(n * 128, 128)]

        small_slots = [by_rows(gate_factor.at[:, pl.ds(256 * i, 256)]) for i in range(3)]
        small_slots.append(
            lambda n: gate_factor.at[
                pl.ds(n // 2 * 256, 256), pl.ds(768 + n % 2 * 128, 128)
            ]
        )
        slots = small_slots + [by_rows(silu), by_rows(inner), by_columns(gate_factor)]
        wholes = (wq, wk, dd, wo, wg, wu, wd)
        scatter_kinds = kinds[:2] + ("folded",) + kinds[3:]
        items = [ScatterDp(wholes[i], scatter_kinds[i], slots[i], *dp_bufs[i]) for i in range(7)]
        qk, value_item, out_item, gate_item, up_item, down_item = items[:2], *items[2:]
        pl.semaphore_wait(ready.at[0], 1)
        down_item.start()
        scatter.step(2)
        gate_grad(0)
        scatter.step(3)
        gate_grad(2)
        gate_item.start()
        load_heads.start()
        scatter.finish(total)

        @tiles(128, 16)
        def _(r):
            grad = residual[r, :] + total[r, :]
            residual[r, :] = grad
            b = branch[r, :]
            scale = lax.rsqrt(jnp.mean(b * b, 1, keepdims=True) + EPS)
            attn_part[...] += jnp.sum(grad * b * scale, 0, keepdims=True)
            weighted = attn_gain[...] * grad
            mean = jnp.mean(b * weighted, 1, keepdims=True)
            own_d[r, :] = (scale * weighted - b * (scale * scale * scale * mean)).astype(BF16)

        gather = GatherTensor(dd, *g3, 768)
        gather.start()
        down_item.along_x()
        tell(2)

        gate_item.along_x()

        def d_mixed(slot):
            s = pl.ds(pl.multiple_of(slot * 128, 128), 128)
            do[s, :] = nt(dd[s, :], wo[...]).astype(BF16)

        def beside(stage):
            if stage == 0:
                down_item.forward()

                @tiles(2048, 512)
                def _(m):
                    @tiles(1024, 512)
                    def _(n):
                        wu[m, n] = tn(x[:, m], du[:, n]).astype(BF16)

                reload.start()
                load_raw.start()
                pl.semaphore_wait(ready.at[1], 1)
                up_item.start()
            else:
                gate_item.forward()
                down_item.along_y()

        gather.run(d_mixed, beside)
        up_item.along_x()
        load_heads.wait()
        load_raw.wait()

        @tiles(2048, 512)
        def _(n):
            wo[:, n] = tn(mixed[...], dd[:, n]).astype(BF16)

        pl.semaphore_wait(ready.at[2], 1)
        out_item.start()
        gate_item.along_y()

        @pl.loop(0, 2)
        def _(h):
            cols = pl.ds(pl.multiple_of(h * 128, 128), 128)
            for i in range(4):
                low = i * 256
                block = slice(low, low + 256)
                q, d = q_rot[block, cols], do[block, cols]
                top = jnp.where(h == 0, stats[block, 0:1], stats[block, 64:65])
                k1, v1 = k_rot[block, cols], v_low[block, cols]
                p1 = jnp.exp(diagonal_mask(nt(q, k1), low, length) - top)
                dp1 = nt(d, v1)
                delta = jnp.sum(p1 * dp1, 1, keepdims=True)
                if i:
                    k0, v0 = k_rot[0:low, cols], v_low[0:low, cols]
                    p0 = jnp.exp(nt(q, k0) - top)
                    dp0 = nt(d, v0)
                    delta += jnp.sum(p0 * dp0, 1, keepdims=True)
                ds1 = (p1 * (dp1 - delta)).astype(BF16)
                dq_block = nn(ds1, k1)
                dk[block, cols] = tn(ds1, q)
                dv[block, cols] = tn(p1.astype(BF16), d)
                if i:
                    ds0 = (p0 * (dp0 - delta)).astype(BF16)
                    dq_block += nn(ds0, k0)
                    dk[0:low, cols] += tn(ds0, q)
                    dv[0:low, cols] += tn(p0.astype(BF16), d)
                dq[block, cols] = dq_block

        up_item.forward()
        q_line[...] = jnp.zeros_like(q_line)
        k_line[...] = jnp.zeros_like(k_line)
        sums[me] = jnp.zeros((8, 256), F32)

        @tiles(1024, 256)
        def _(r):
            cos, sin = cos_sin(table[r, :])
            for source, rawer, gain, s, factor, line in (
                (dq, q_raw, q_gain, 128, SCALE, q_line),
                (dk, k_raw, k_gain, 192, 1.0, k_line),
            ):
                scale = stats[r, s : s + 1]
                for h in (0, 128):
                    v = source[r, h : h + 128] * factor
                    v = v * cos - pltpu.roll(v, 64, 1) * sin
                    w = v * rawer[r, h : h + 128].astype(F32)
                    line[:, h : h + 128] += jnp.sum(w * scale, 0, keepdims=True)
                    source[r, h : h + 128] = v * gain[:, h : h + 128]
            note_sums(
                sums.at[me],
                r,
                dq[r, :] * q_raw[r, :].astype(F32),
                dk[r, :] * k_raw[r, :].astype(F32),
            )
            dvr[r, :] = dv[r, :].astype(BF16)

        exchange = Exchange(sums, *fsems)
        exchange.start()
        reload.wait()
        row = lax.broadcasted_iota(jnp.int32, (8, 1024), 0)
        column = lax.broadcasted_iota(jnp.int32, (8, 1024), 1)
        message = jnp.zeros((8, 1024), F32)
        for k, line in enumerate((attn_part, attn_part, mlp_part, mlp_part)):
            line = line[:, 1024 * (k % 2) : 1024 * (k % 2) + 1024]
            message = jnp.where(row == 4 + k, line, message)
        for first_row, line in ((0, q_line), (2, k_line)):
            line = jnp.concatenate([line[...]] * 4, 1)
            message += jnp.where((row == first_row + yl) & (column // 256 == z), line, 0.0)
        gain_slots[me] = message
        total_gain = SumAll(gain_slots, gain_hold, gain_boxes, *isems)

        @pl.loop(0, 4)
        def _(i):
            m = pl.ds(pl.multiple_of(i * 512, 512), 512)
            r = pl.ds(pl.multiple_of(lax.rem(i, 2) * 512, 512), 512)
            columns = pl.ds(pl.multiple_of(i // 2 * 256, 256), 256)
            dd[r, columns] = tn(x[:, m], dvr[...]).astype(BF16)

        value_item.start()
        out_item.along_x()
        exchange.finish()
        total_gain.start()
        spread(dv, exchange.sum() * (1.0 / 2048))

        @tiles(1024, 256)
        def _(r):
            for source, rawer, s, target in ((dq, q_raw, 0, dqr), (dk, k_raw, 128, dkr)):
                scale = stats[r, 128 + s // 2 : 129 + s // 2]
                factor = scale * scale * scale * dv[r, s : s + 128]
                for h in (0, 128):
                    target[r, h : h + 128] = (
                        scale * source[r, h : h + 128]
                        - rawer[r, h : h + 128].astype(F32) * factor
                    ).astype(BF16)

        def d_tokens(half, side):
            s = pl.ds(pl.multiple_of(half * 512, 512), 512)

            @pl.loop(0, 2)
            def _(i):
                n = pl.ds(pl.multiple_of(side * 1024 + i * 512, 512), 512)
                terms = nt(dqr[s, :], wq[n, :]) + nt(dkr[s, :], wk[n, :]) + nt(dvr[s, :], wv[n, :])
                part[s, n] = terms.astype(BF16)

        scatter = ScatterTensor(part, bufs, *s3)
        scatter.run(d_tokens)
        up_item.along_y()
        value_item.along_x()
        scatter.step(0)

        @tiles(2048, 512)
        def _(m):
            xt = x[:, m].T
            wq[m, :] = nn(xt, dqr[...]).astype(BF16)
            wk[m, :] = nn(xt, dkr[...]).astype(BF16)

        for item in qk:
            item.start()
        out_item.forward()
        total_gain.core()
        scatter.step(1)
        for item in qk:
            item.along_x()
        value_item.forward()
        total_gain.along_x()
        scatter.step(2)
        out_item.along_y()
        scatter.step(3)
        for item in qk:
            item.forward()
        total_gain.along_y()
        stores = []

        def store(item, source, target):
            item.finish(source)
            stores.append(pltpu.make_async_copy(source, target, lsem.at[len(stores)]))
            stores[-1].start()

        store(down_item, dv.at[:, pl.ds(0, 128)], o6)
        gate_item.finish(o4)
        up_item.finish(o5)
        value_item.along_y()
        store(out_item, dv.at[pl.ds(0, 256), pl.ds(128, 128)], o3)
        scatter.finish(input_grad)

        @tiles(128, 16)
        def _(r):
            input_grad[r, :] += residual[r, :]

        for item in qk:
            item.along_y()
        total_gain.finish(gain_slots.at[0])
        for i, out in enumerate((q_sum, k_sum, attn_sum, mlp_sum)):
            out[:, 0:1024] = gain_slots[0, 2 * i : 2 * i + 1, :]
            out[:, 1024:2048] = gain_slots[0, 2 * i + 1 : 2 * i + 2, :]
        store(value_item, dk.at[pl.ds(256, 128)], o2)
        for i, out in enumerate((o0, o1)):
            store(qk[i], dk.at[pl.ds(128 * i, 128)], out)
        for copy in stores:
            copy.wait()

    S = jax.ShapeDtypeStruct
    W = pltpu.VMEM
    scratch = [W((1024, 2048), BF16)] * 2 + [W((2048, 1024), BF16)] * 2 + [W((1024, 2048), BF16)]
    scratch += [W((1024, 1024), BF16)] * 5 + [W((1024, 2048), BF16)]
    scratch += [W((128, 2048), F32)] + [W((1, 2048), F32)] * 2 + [W((1, 256), F32)] * 2
    scratch += [W((2048, 256), BF16)] * 3 + [W((256, 2048), BF16)]
    scratch += [W((1024, 256), F32), W((128, 2048), F32), W((1024, 256), BF16)]
    scratch += [W((1024, 256), F32)] * 3
    scratch += [W((8, 8, 256), F32), W((8, 8, 1024), F32)] + [W((3, 8, 1024), F32), W((5, 8, 1024), F32)]
    scratch += ScatterTensor.scratch()
    for b in blocks:
        scratch += ScatterDp.scratch(b)
    for n in (23, 23, 23, 23, 21, 21, 21, 21, 7, 7, 12):
        scratch += [DMA((n,))] * 2
    scratch += [DMA((7, 21))] * 2
    scratch += [DMA((8,)), DMA((4,)), pltpu.SemaphoreType.REGULAR((3,))]
    return pl.pallas_call(
        layer_step,
        out_shape=[S((128, 2048), BF16), S((128, 2048), F32)]
        + [S(b, F32) for b in blocks]
        + [S((1, 2048), F32)] * 4
        + [S((1024, 2048), BF16), S((1024, 1024), BF16), S((1024, 512), BF16)],
        in_specs=[SMEM] + [VM] * 6 + [ANY] * 8,
        out_specs=[ANY, VM] + [ANY] * 4 + [VM] * 2 + [ANY] + [VM] * 4 + [ANY] * 3,
        scratch_shapes=scratch,
        compiler_params=params(1),
        name="layer_step",
    )(lengths, cotangent, *gains, table, tokens, *weights)[:13]


def hand_over(*arrays):
    n = len(arrays)

    def hand_over_step(*refs):
        held, (lsem, ssem) = refs[2 * n : 3 * n], refs[3 * n :]
        loads = [pltpu.make_async_copy(refs[i], held[i], lsem.at[i]) for i in range(n)]
        stores = [pltpu.make_async_copy(held[i], refs[n + i], ssem.at[i]) for i in range(n)]
        for copy in loads:
            copy.start()
        for load, store in zip(loads, stores):
            load.wait()
            store.start()
        for copy in stores:
            copy.wait()

    return pl.pallas_call(
        hand_over_step,
        out_shape=[jax.ShapeDtypeStruct(a.shape, a.dtype) for a in arrays],
        in_specs=[ANY] * n,
        out_specs=[ANY] * n,
        scratch_shapes=[pltpu.VMEM(a.shape, a.dtype) for a in arrays] + [DMA((n,))] * 2,
        compiler_params=pltpu.CompilerParams(vmem_limit_bytes=63 << 20),
        name="hand_over_step",
    )(*arrays)


def local(
    tokens, lengths, w_query, w_key, w_value, w_out, w_gate, w_up, w_down,
    q_gain, k_gain, attn_gain, mlp_gain, cotangent,
):
    weights = (w_query, w_key, w_value, w_out, w_gate, w_up, w_down)
    gains = (q_gain[None], k_gain[None], attn_gain[None], mlp_gain[None])
    results = whole_layer(tokens[0], lengths, cotangent[0], gains, weights, rope_table())
    act, input_grad, *grads = hand_over(*results)
    return (act[None], input_grad[None], *grads[:7], *(g.reshape(2048) for g in grads[7:]))


def solution(mesh):
    return jax.shard_map(
        local,
        mesh=mesh,
        in_specs=(
            P("dp", "tensor", None),
            P("dp"),
            P("dp", "tensor"),
            P("dp", "tensor"),
            P("dp", "tensor"),
            P("tensor", "dp"),
            P("dp", "tensor"),
            P("dp", "tensor"),
            P("tensor", "dp"),
            P(),
            P(),
            P(),
            P(),
            P("dp", "tensor", None),
        ),
        out_specs=(
            P("dp", "tensor", None),
            P("dp", "tensor", None),
            P("dp", "tensor"),
            P("dp", "tensor"),
            P("dp", "tensor"),
            P("tensor", "dp"),
            P("dp", "tensor"),
            P("dp", "tensor"),
            P("tensor", "dp"),
            P(),
            P(),
            P(),
            P(),
        ),
        check_vma=False,
    )
```

```python
import jax
import jax.numpy as jnp
import numpy as np
from jax import lax
from jax.experimental import pallas as pl
from jax.experimental.pallas import tpu as pltpu
from jax.sharding import PartitionSpec as P

HEAD_DIM = 128
EPS = 1e-06
THETA = 500000.0
MESH = pl.DeviceIdType.MESH
BF16 = jnp.bfloat16
F32 = jnp.float32
ANY = pl.BlockSpec(memory_space=pl.ANY)
VM = pl.BlockSpec(memory_space=pltpu.VMEM)
DMA = pltpu.SemaphoreType.DMA
CUT = 896
WIDTH = 2048


def place():
    d = lax.axis_index("dp")
    t = lax.axis_index("tensor")
    return d // 8, lax.rem(d // 2, 4), lax.rem(d, 2), t // 4, lax.rem(t, 4)


def other(dyh=0, dx=0, dc=0, dyl=0, dz=0):
    yh, x, c, yl, z = place()
    return (
        lax.rem(yh + dyh, 2) * 8 + lax.rem(x + dx, 4) * 2 + lax.rem(c + dc, 2),
        lax.rem(yl + dyl, 2) * 4 + lax.rem(z + dz, 4),
    )


TENSOR_PEERS = (dict(dz=1), dict(dz=3), dict(dyl=1))
DP_PEERS = (dict(dx=1), dict(dx=2), dict(dx=3), dict(dyh=1), dict(dc=1))
SMEM = pl.BlockSpec(memory_space=pltpu.SMEM)


def greet(peers):
    barrier = pltpu.get_barrier_semaphore()
    for peer in peers:
        pl.semaphore_signal(barrier, 1, device_id=other(**peer), device_id_type=MESH)
    pl.semaphore_wait(barrier, len(peers))


def remote(src, dst, sems, index, peer):
    ssem, rsem = sems
    return pltpu.make_async_remote_copy(
        src_ref=src,
        dst_ref=dst,
        send_sem=ssem,
        recv_sem=rsem.at[index],
        device_id=other(**peer),
        device_id_type=MESH,
    )


def all_of(bytes_of, sem):
    pltpu.make_async_copy(bytes_of, bytes_of, sem).wait()


def rows(ref, slot):
    return ref.at[pl.ds(pl.multiple_of(slot * 128, 128), 128)]


def halves(ref):
    half = ref.shape[0] // 2
    return ref.at[pl.ds(0, half)], ref.at[pl.ds(half, half)]


def add_into(out, *terms):
    step = min(out.shape[0], 16 if out.shape[1] > 1024 else 64 if out.shape[1] > 128 else 128)

    @pl.loop(0, out.shape[0] // step)
    def _(i):
        r = pl.ds(pl.multiple_of(i * step, step), step)
        if len(terms) == 2 and out.dtype == BF16:
            out[r, :] = terms[0][r, :] + terms[1][r, :]
        else:
            total = terms[0][r, :].astype(F32)
            for term in terms[1:]:
                total += term[r, :].astype(F32)
            out[r, :] = total.astype(out.dtype)


class RingGather:
    COPIES = 6

    def __init__(self, block, axis, sems, base, source=None):
        up, down = {axis: 1}, {axis: 3}
        src = halves(block(0) if source is None else source)
        own, behind, ahead = halves(block(0)), halves(block(3)), halves(block(1))
        self.copies = [
            remote(src[0], own[0], sems, base, up),
            remote(src[1], own[1], sems, base + 1, down),
            remote(src[1], own[1], sems, base + 2, up),
            remote(src[0], own[0], sems, base + 3, down),
            remote(behind[0], behind[0], sems, base + 4, up),
            remote(ahead[1], ahead[1], sems, base + 5, down),
        ]

    def start(self):
        for copy in self.copies[:4]:
            copy.start()

    def forward(self):
        for i in range(2):
            self.copies[i].wait_recv()
            self.copies[4 + i].start()

    def behind(self):
        self.copies[2].wait_recv()

    def ahead(self):
        self.copies[3].wait_recv()

    def far(self):
        for copy in self.copies[4:]:
            copy.wait_recv()


class RingReduce:
    COPIES = 6

    @staticmethod
    def scratch(n, m):
        return [pltpu.VMEM((2, n // 2, m), BF16), pltpu.VMEM((2, n, m), BF16)]

    def __init__(self, block, axis, part, full, sems, base):
        up, down = {axis: 1}, {axis: 3}
        one, two, three = halves(block(1)), halves(block(2)), halves(block(3))
        from_behind, from_ahead = halves(full.at[0]), halves(full.at[1])
        self.adds = ((one[0], part.at[0]), (three[1], part.at[1]))
        self.terms = (block(0), full.at[0], full.at[1])
        self.copies = [
            remote(two[0], part.at[0], sems, base, up),
            remote(two[1], part.at[1], sems, base + 1, down),
            remote(one[1], from_behind[1], sems, base + 2, up),
            remote(three[0], from_ahead[0], sems, base + 3, down),
            remote(one[0], from_behind[0], sems, base + 4, up),
            remote(three[1], from_ahead[1], sems, base + 5, down),
        ]

    def start(self):
        for copy in self.copies[:4]:
            copy.start()

    def forward(self):
        for i in range(2):
            self.copies[i].wait_recv()
            add_into(self.adds[i][0], *self.adds[i])
            self.copies[4 + i].start()

    def arrive(self):
        for copy in self.copies[2:]:
            copy.wait_recv()


class GatherTensor:
    COPIES = 21

    def __init__(self, buf, ssem, rsem, cut=CUT):
        yh, x, c, yl, z = place()
        self.yl, self.z = yl, z
        self.sent, self.ssem = buf.at[pl.ds(0, 896)], ssem
        sems = (ssem, rsem)
        slot = lambda k, i: rows(buf, lax.rem(yl + k, 2) * 4 + lax.rem(z + i, 4))
        low = lambda ref: ref.at[:, pl.ds(0, cut)]
        high = lambda ref: ref.at[:, pl.ds(cut, WIDTH - cut)]
        self.ring = RingGather(lambda i: slot(0, i), "dz", sems, 0)
        self.pair_ring = RingGather(lambda i: high(slot(1, i)), "dz", sems, 6)
        own = slot(0, 0)
        pair = dict(dyl=1)
        self.high = remote(high(own), high(own), sems, 12, pair)
        self.low = []
        for n, i in enumerate((0, 3, 1, 2)):
            for half in halves(low(slot(0, i))):
                self.low.append(remote(half, half, sems, 13 + len(self.low), pair))

    def start(self):
        self.high.start()
        self.ring.start()
        self.low[0].start()
        self.low[1].start()

    def run(self, process, spare=None, by_half=None, early=None):
        yl, z = self.yl, self.z

        @pl.loop(0, 2)
        def _(k):
            @pl.when(k == 1)
            def _():
                self.ring.forward()
                self.low[2].start()
                self.low[5].start()
                if early is not None:
                    early()
                self.high.wait_recv()
                self.pair_ring.start()
                self.ring.behind()
                self.low[3].start()
                self.ring.ahead()
                self.low[4].start()
                self.low[0].wait_recv()
                self.low[1].wait_recv()

            process(lax.rem(yl + k, 2) * 4 + z)

        if spare is not None:
            spare(0)

        @pl.loop(0, 6 if by_half is None else 7)
        def _(j):
            if by_half is not None:

                @pl.when(lax.rem(j, 3) == 0)
                def _():
                    @pl.when(j > 0)
                    def _():
                        by_half(lax.rem(yl + j // 6, 2))

            @pl.when(j == 2)
            def _():
                self.ring.far()
                self.low[6].start()
                self.low[7].start()
                self.pair_ring.forward()

            @pl.when(j == 3)
            def _():
                if spare is not None:
                    spare(1)
                self.pair_ring.behind()
                self.low[2].wait_recv()
                self.low[3].wait_recv()

            @pl.when(j == 4)
            def _():
                self.pair_ring.ahead()
                self.low[4].wait_recv()
                self.low[5].wait_recv()

            @pl.when(j == 5)
            def _():
                if spare is not None:
                    spare(2)
                self.pair_ring.far()
                self.low[6].wait_recv()
                self.low[7].wait_recv()

            i = lax.rem(j, 3)
            step = (3 * i * i - 7 * i + 6) // 2

            @pl.when(j < 6)
            def _():
                process(lax.rem(yl + j // 3, 2) * 4 + lax.rem(z + step, 4))

        all_of(self.sent, self.ssem)


class ScatterTensor:
    COPIES = 23

    @staticmethod
    def scratch(least, most):
        return (
            [pltpu.VMEM((4, 128, most), BF16), pltpu.VMEM((128, WIDTH - least), BF16)]
            + RingReduce.scratch(128, most)
            + RingReduce.scratch(128, WIDTH - least) * 2
        )

    def __init__(self, part, bufs, ssem, rsem, cut=CUT):
        yh, x, c, yl, z = place()
        self.z = z
        narrow = lambda ref, n: ref.at[:, :, pl.ds(0, n)]
        wide = WIDTH - cut
        bufs = [
            narrow(bufs[0], cut),
            bufs[1].at[:, pl.ds(0, wide)],
            *(narrow(ref, cut) for ref in bufs[2:4]),
            *(narrow(ref, wide) for ref in bufs[4:]),
        ]
        self.yl = yl
        self.from_pair, self.last = bufs[0], bufs[1]
        self.sent, self.ssem = part.at[pl.ds(0, 896)], ssem
        sems = (ssem, rsem)
        slot = lambda k, i: rows(part, lax.rem(yl + k, 2) * 4 + lax.rem(z + i, 4))
        low = lambda k, i: slot(k, i).at[:, pl.ds(0, cut)]
        high = lambda k, i: slot(k, i).at[:, pl.ds(cut, wide)]
        self.cut = cut
        pair = dict(dyl=1)
        self.low = lambda i: low(0, i)
        self.low_ring = RingReduce(lambda i: low(0, i), "dz", bufs[2], bufs[3], sems, 0)
        self.pair_ring = RingReduce(lambda i: high(1, i), "dz", bufs[4], bufs[5], sems, 6)
        self.own_ring = RingReduce(lambda i: high(0, i), "dz", bufs[6], bufs[7], sems, 12)
        self.first = lambda i: remote(low(1, i), bufs[0].at[i], sems, 18 + i, pair)
        self.second = remote(high(1, 0), bufs[1], sems, 22, pair)

    def run(self, process, before=None):
        yl, z = self.yl, self.z

        @pl.loop(0, 4)
        def _(k):
            half = lax.rem(yl + 1 + k // 2, 2)
            if before is not None:

                @pl.when(lax.rem(k, 2) == 0)
                def _():
                    before(half)

            process(half * 512 + lax.rem((z + 2) // 2 + k, 2) * 256)
            beside = 3 - 2 * lax.rem(z, 2)

            @pl.when(k == 0)
            def _():
                self.first(2).start()
                self.pair_ring.copies[0].start()
                self.pair_ring.copies[1].start()
                self.first(beside).start()

            @pl.when(k == 1)
            def _():
                self.first(4 - beside).start()
                self.pair_ring.copies[2].start()
                self.pair_ring.copies[3].start()
                self.first(0).start()

    def add_first(self, i):
        self.first(i).wait_recv()
        add_into(self.low(i), self.low(i), self.from_pair.at[i])

    def add_low(self, i):
        self.add_first(i)
        for k in (1, 3):

            @pl.when(i == k)
            def _():
                self.low_ring.copies[2 + k // 3].start()

    def step(self, n):
        beside = 3 - 2 * lax.rem(self.z, 2)
        if n == 0:
            self.pair_ring.forward()
            self.own_ring.start()
            self.add_first(2)
            self.low_ring.copies[0].start()
            self.low_ring.copies[1].start()
        if n == 1:
            self.own_ring.forward()
            self.add_low(beside)
        if n == 2:
            self.pair_ring.arrive()
            add_into(self.pair_ring.terms[0], *self.pair_ring.terms)
            self.second.start()
            self.add_low(4 - beside)
        if n == 3:
            self.low_ring.forward()
            self.add_first(0)

    def finish(self, out):
        self.own_ring.arrive()
        self.second.wait_recv()
        add_into(out.at[:, pl.ds(self.cut, WIDTH - self.cut)], *self.own_ring.terms, self.last)
        self.low_ring.arrive()
        add_into(out.at[:, pl.ds(0, self.cut)], *self.low_ring.terms)
        all_of(self.sent, self.ssem)


def block_of(ref, kind, slot):
    if kind == "row":
        size = ref.shape[0] // 16
        return ref.at[pl.ds(pl.multiple_of(slot * size, size), size)]
    if kind == "folded":
        return ref.at[
            pl.ds(pl.multiple_of(lax.rem(slot, 8) * 128, 128), 128),
            pl.ds(pl.multiple_of(slot // 8 * 256, 256), 256),
        ]
    size = ref.shape[1] // 16
    return ref.at[:, pl.ds(pl.multiple_of(slot * size, size), size)]


def some_of(ref, kind, count):
    if kind == "row":
        return ref.at[pl.ds(0, ref.shape[0] // 16 * count)]
    if kind == "folded":
        return ref.at[pl.ds(0, 64 * count), pl.ds(0, 512)]
    return ref.at[:, pl.ds(0, ref.shape[1] // 16 * count)]


class GatherDp:
    COPIES = 21

    def __init__(self, shard, out, kind, ssem, rsem, lsem):
        yh, x, c, yl, z = place()
        sems = (ssem, rsem)
        block = lambda k, i: block_of(
            out, kind, lax.rem(yh + k, 2) * 8 + lax.rem(x + i, 4) * 2 + c
        )
        self.sent, self.ssem = some_of(out, kind, 15), ssem
        self.local = pltpu.make_async_copy(shard, block(0, 0), lsem)
        self.ring = RingGather(lambda i: block(0, i), "dx", sems, 0, shard)
        self.far_ring = RingGather(lambda i: block(1, i), "dx", sems, 6)
        self.own_y = remote(shard, block(0, 0), sems, 12, dict(dyh=1))
        core = dict(dc=1)
        self.core = [remote(shard, block(0, 0), sems, 13, core)]
        for n in range(1, 8):
            ref = block(n // 4, n % 4)
            self.core.append(remote(ref, ref, sems, 13, core))
        self.shared, self.shared_sem = some_of(out, kind, 8), rsem.at[13]

    def start(self):
        self.ring.start()
        self.core[0].start()
        self.local.start()

    def forward(self):
        self.ring.forward()

    def forward_y(self):
        self.own_y.wait_recv()
        self.far_ring.start()
        self.core[4].start()

    def share(self):
        self.ring.behind()
        self.core[3].start()
        self.ring.ahead()
        self.core[1].start()
        self.ring.far()
        self.core[2].start()

    def forward_far(self):
        self.far_ring.forward()

    def share_far(self):
        self.far_ring.behind()
        self.core[7].start()
        self.far_ring.ahead()
        self.core[5].start()
        self.far_ring.far()
        self.core[6].start()

    def finish(self):
        all_of(self.shared, self.shared_sem)
        self.local.wait()
        all_of(self.sent, self.ssem)


class ScatterDp:
    COPIES = 21

    @staticmethod
    def scratch(block):
        return (
            [pltpu.VMEM(block, BF16)]
            + RingReduce.scratch(*block) * 2
            + [DMA, DMA((14,))]
        )

    def __init__(self, part, kind, from_core, from_y, h0, f0, h1, f1, ssem, rsem):
        yh, x, c, yl, z = place()
        sems = (ssem, rsem)
        self.from_core, self.from_y = from_core, from_y
        self.sent, self.ssem = some_of(part, kind, 15), ssem
        block = lambda k, i, d: block_of(
            part, kind, lax.rem(yh + k, 2) * 8 + lax.rem(x + i, 4) * 2 + d
        )
        self.block = lambda k, i: block(k, i, c)
        self.core = [
            remote(block(n // 4, n % 4, 1 - c), from_core(n), sems, 0, dict(dc=1))
            for n in range(8)
        ]
        self.ring = RingReduce(lambda i: block(0, i, c), "dx", h0, f0, sems, 1)
        self.far_ring = RingReduce(lambda i: block(1, i, c), "dx", h1, f1, sems, 7)
        self.last = remote(block(1, 0, c), from_y, sems, 13, dict(dyh=1))
        self.shared, self.shared_sem = some_of(part, kind, 8), rsem.at[0]

    def start(self):
        for n in (6, 5, 7, 4, 2, 1, 3, 0):
            self.core[n].start()

    def add_core(self, n):
        ref = self.block(n // 4, n % 4)
        add_into(ref, ref, self.from_core(n))

    def along_x(self):
        all_of(self.shared, self.shared_sem)
        for n in (6, 5, 7):
            self.add_core(n)
        self.far_ring.start()
        for n in (2, 1, 3):
            self.add_core(n)
        self.ring.start()
        for n in (4, 0):
            self.add_core(n)

    def forward(self):
        self.far_ring.forward()
        self.ring.forward()

    def along_y(self):
        self.far_ring.arrive()
        add_into(self.far_ring.terms[0], *self.far_ring.terms)
        self.last.start()

    def finish(self, out):
        self.ring.arrive()
        self.last.wait_recv()
        add_into(out, *self.ring.terms, self.from_y)
        all_of(self.sent, self.ssem)


def params(cid):
    return pltpu.CompilerParams(
        collective_id=cid, has_side_effects=True, vmem_limit_bytes=65400 << 10
    )


def nn(a, b):
    return jnp.dot(a, b, preferred_element_type=F32)


def nt(a, b):
    return lax.dot_general(a, b, (((1,), (1,)), ((), ())), preferred_element_type=F32)


def tn(a, b):
    return lax.dot_general(a, b, (((0,), (0,)), ((), ())), preferred_element_type=F32)


def tiles(count, size):
    def run(body):
        @pl.loop(0, count // size)
        def _(i):
            body(pl.ds(pl.multiple_of(i * size, size), size))

    return run


def rope_table():
    frequency = THETA ** (-(np.arange(64, dtype=np.float32) * np.float32(2.0) / np.float32(HEAD_DIM)))
    angles = np.arange(1024, dtype=np.float32)[:, None] * frequency.astype(np.float32)[None, :]
    cosine, sine = np.cos(angles), np.sin(angles)
    return np.concatenate([cosine, sine], 1).astype(np.float32)


def cos_sin(table):
    turned = pltpu.roll(table, 64, 1)
    first = lax.broadcasted_iota(jnp.int32, table.shape, 1) < 64
    return jnp.where(first, table, turned), jnp.where(first, -turned, table)


class Exchange:
    PEERS = tuple(dict(dz=a, dyl=b) for b in range(2) for a in range(4) if a or b)

    def __init__(self, buf, ssem, rsem):
        yh, x, c, yl, z = place()
        self.buf, self.ssem = buf, ssem
        self.mine = buf.at[yl * 4 + z]
        self.copies = [
            remote(self.mine, self.mine, (ssem, rsem), i, peer)
            for i, peer in enumerate(self.PEERS)
        ]

    def start(self):
        for copy in self.copies:
            copy.start()

    def finish(self):
        for copy in self.copies:
            copy.wait_recv()
        all_of(self.buf.at[pl.ds(0, 7)], self.ssem)

    def sum(self):
        total = self.buf[0]
        for i in range(1, 8):
            total += self.buf[i]
        return total


def row_sums(values):
    return nt(jnp.ones((8, values.shape[1]), F32), values)


def spread(out, pair):
    row = lax.broadcasted_iota(jnp.int32, (8, 256), 0)
    column = lax.broadcasted_iota(jnp.int32, (8, 256), 1)
    for i in range(4):
        pick = jnp.where(row == column // 128 * 4 + i, 1.0, 0.0)
        out[pl.ds(256 * i, 256), :] = lax.dot_general(
            pair,
            pick,
            (((0,), (0,)), ((), ())),
            precision=lax.Precision.HIGHEST,
            preferred_element_type=F32,
        )


def note_sums(out, r, a, b):
    row = lax.broadcasted_iota(jnp.int32, (8, 256), 0)
    sums = jnp.where(row < 4, row_sums(a), row_sums(b))
    out[...] = jnp.where(lax.rem(row, 4) == r.start // 256, sums, out[...])


ALL_PEERS = Exchange.PEERS + DP_PEERS
SCALE = HEAD_DIM**-0.5


def diagonal_mask(scores, first, length):
    row = lax.broadcasted_iota(jnp.int32, scores.shape, 0)
    column = lax.broadcasted_iota(jnp.int32, scores.shape, 1)
    return jnp.where((column <= row) & (column + first < length), scores, -1e30)


class SumAll:
    def __init__(self, slots, hold, boxes, ssem, rsem):
        self.exchange = Exchange(slots, ssem.at[5], rsem)
        self.hold, self.boxes = hold, boxes
        self.copies = []
        for i, peer in enumerate(DP_PEERS):
            k = (1, 1, 1, 2, 0)[i]
            self.copies.append(remote(hold.at[k], boxes.at[i], (ssem.at[i], rsem), 7 + i, peer))

    def start(self):
        self.exchange.start()

    def core(self):
        self.exchange.finish()
        self.hold[0] = self.exchange.sum()
        self.copies[4].start()

    def along_x(self):
        self.copies[4].wait()
        self.hold[1] = self.hold[0] + self.boxes[4]
        for copy in self.copies[:3]:
            copy.start()

    def along_y(self):
        for copy in self.copies[:3]:
            copy.wait()
        self.hold[2] = self.hold[1] + self.boxes[0] + self.boxes[1] + self.boxes[2]
        self.copies[3].start()

    def finish(self, out):
        self.copies[3].wait()
        out[...] = self.hold[2] + self.boxes[3]


def whole_layer(tokens, lengths, cotangent, gains, weights, table):
    kinds = ("row", "row", "row", "col", "row", "row", "col")
    blocks = ((128, 256),) * 3 + ((256, 128), (128, 1024), (128, 1024), (1024, 128))

    def layer_step(
        lengths, cotangent, q_gain_all, k_gain_all, attn_gain, mlp_gain, table,
        tokens, i0, i1, i2, i3, i4, i5, i6,
        act, input_grad, o0, o1, o2, o3, o4, o5, o6,
        q_sum, k_sum, attn_sum, mlp_sum, x_kept, heads_kept, raw_kept,
        x, dd, wg, wu, wd, gate_factor, silu, inner, dg, du, part, residual, attn_part, mlp_part, q_line, k_line,
        wq, wk, wv, wo, stats, branch, do, dq, dk, dv, sums, gain_slots, gain_hold, gain_boxes,
        *rest,
    ):
        bufs, rest = rest[:8], rest[8:]
        dp_bufs, rest = [rest[7 * i : 7 * i + 7] for i in range(7)], rest[49:]
        scatter_sems, gather_sems, sum_sems, isems, wsems = [
            rest[2 * i : 2 * i + 2] for i in range(5)
        ]
        lsem, msem, ready = rest[10:]
        yh, xx, c, yl, z = place()
        me = yl * 4 + z
        length = lengths[0]
        total = input_grad
        own_columns = pl.ds(pl.multiple_of(me * 256, 256), 256)
        q_gain, k_gain = q_gain_all[:, own_columns], k_gain_all[:, own_columns]
        q_rot, k_rot, v_low, mixed = (dg.at[:, pl.ds(256 * i, 256)] for i in range(4))
        q_raw, k_raw, dvr = (du.at[:, pl.ds(256 * i, 256)] for i in range(3))
        dqr, dkr = q_raw, k_raw
        raw = du.at[:, pl.ds(0, 512)]
        load_heads = pltpu.make_async_copy(heads_kept, dg, msem.at[0])
        load_raw = pltpu.make_async_copy(raw_kept, raw, msem.at[2])
        reload = pltpu.make_async_copy(x_kept, x, msem.at[1])
        keep_x = pltpu.make_async_copy(dd, x_kept, msem.at[1])
        keep_heads = pltpu.make_async_copy(dg, heads_kept, msem.at[0])
        keep_raw = pltpu.make_async_copy(raw, raw_kept, msem.at[2])
        first = pltpu.make_async_copy(tokens, rows(dd, me), msem.at[3])
        first.start()
        greet(ALL_PEERS)
        shards = (i0, i1, i2, i3, i4, i5, i6)
        targets = (wq, wk, wv, wo, wg, wu, wd)
        spreads = [
            GatherDp(shards[i], targets[i], kinds[i], wsems[0].at[i], wsems[1].at[i], lsem.at[i])
            for i in range(7)
        ]
        small, large, down_weights = spreads[:4], spreads[4:6], spreads[6]
        for spread_item in small:
            spread_item.start()
            spread_item.own_y.start()
        first.wait()
        gather = GatherTensor(dd, *gather_sems, 640)
        gather.start()

        def forward_small():
            for spread_item in small:
                spread_item.forward()
                spread_item.forward_y()

        def spread_small(stage):
            for spread_item in small:
                if stage == 0:
                    spread_item.share()
                    spread_item.forward_far()
                elif stage == 1:
                    spread_item.share_far()
            if stage == 2:
                down_weights.own_y.start()

        gather.run(lambda slot: None, spread_small, early=forward_small)
        for spread_item in large:
            spread_item.start()
        large[0].own_y.start()
        for spread_item in small:
            spread_item.finish()
        sums[me] = jnp.zeros((8, 256), F32)
        keep_x.start()

        @tiles(1024, 256)
        def _(r):
            q = nn(dd[r, :], wq[...])
            k = nn(dd[r, :], wk[...])
            dq[r, :] = q
            dk[r, :] = k
            du[r, 0:256] = q.astype(BF16)
            du[r, 256:512] = k.astype(BF16)
            v_low[r, :] = nn(dd[r, :], wv[...]).astype(BF16)
            note_sums(sums.at[me], r, q * q, k * k)

        exchange = Exchange(sums, *sum_sems)
        exchange.start()
        keep_raw.start()
        exchange.finish()
        large[1].own_y.start()
        for spread_item in large:
            spread_item.forward()
        large[0].forward_y()
        spread(dv, lax.rsqrt(exchange.sum() * (1.0 / 2048) + EPS))
        narrow = lax.broadcasted_iota(jnp.int32, (1024, 128), 1) < 64
        stats[:, 128:256] = jnp.where(narrow, dv[:, 0:128], dv[:, 128:256])

        @tiles(1024, 256)
        def _(r):
            cos, sin = cos_sin(table[r, :])
            for source, gain, s, target, factor in (
                (dq, q_gain, 0, q_rot, SCALE),
                (dk, k_gain, 128, k_rot, 1.0),
            ):
                scale = dv[r, s : s + 128]
                for h in (0, 128):
                    v = source[r, h : h + 128] * scale * gain[:, h : h + 128]
                    v = v * cos + pltpu.roll(v, 64, 1) * sin
                    target[r, h : h + 128] = (v * factor).astype(BF16)

        def attend(half):
            for top in range(2):

                @pl.when(half == top)
                def _():
                    @pl.loop(0, 2)
                    def _(h):
                        cols = pl.ds(pl.multiple_of(h * 128, 128), 128)
                        mine = lax.broadcasted_iota(jnp.int32, (256, 128), 1) // 64 == h
                        for i in (2 * top, 2 * top + 1):
                            low = i * 256
                            block = slice(low, low + 256)
                            q = q_rot[block, cols]
                            near = diagonal_mask(nt(q, k_rot[block, cols]), low, length)
                            peak = jnp.max(near, 1, keepdims=True)
                            if i:
                                past = nt(q, k_rot[0:low, cols])
                                peak = jnp.maximum(peak, jnp.max(past, 1, keepdims=True))
                            e1 = jnp.exp(near - peak)
                            denom = jnp.sum(e1, 1, keepdims=True)
                            out = nn(e1.astype(BF16), v_low[block, cols])
                            if i:
                                e0 = jnp.exp(past - peak)
                                denom += jnp.sum(e0, 1, keepdims=True)
                                out += nn(e0.astype(BF16), v_low[0:low, cols])
                            mixed[block, cols] = (out / denom).astype(BF16)
                            lse = peak + jnp.log(denom)
                            stats[block, 0:128] = jnp.where(mine, lse, stats[block, 0:128])

        def project(first_row):
            s = pl.ds(pl.multiple_of(first_row, 256), 256)

            @pl.loop(0, 2)
            def _(i):
                n = pl.ds(pl.multiple_of(i * 1024, 1024), 1024)
                part[s, n] = nn(mixed[s, :], wo[:, n]).astype(BF16)

        scatter = ScatterTensor(part, bufs, *scatter_sems)
        scatter.run(project, attend)
        keep_heads.start()
        large[1].forward_y()
        scatter.step(0)
        for spread_item in large:
            spread_item.share()
        scatter.step(1)
        for spread_item in large:
            spread_item.forward_far()
        down_weights.start()
        down_weights.forward_y()
        scatter.step(2)
        scatter.step(3)
        for spread_item in large:
            spread_item.share_far()
        scatter.finish(branch)
        own = rows(x, me)
        own_tokens = rows(dd, me)
        for copy in (keep_x, keep_raw, keep_heads):
            copy.wait()

        def tell(i):
            pl.semaphore_signal(ready.at[i], 1, device_id=other(dc=1), device_id_type=MESH)

        @tiles(128, 16)
        def _(r):
            b = branch[r, :]
            scale = lax.rsqrt(jnp.mean(b * b, 1, keepdims=True) + EPS)
            value = own_tokens[r, :].astype(F32) + b * scale * attn_gain[...]
            residual[r, :] = value
            own[r, :] = value.astype(BF16)

        gather = GatherTensor(x, *gather_sems)
        gather.start()
        down_weights.forward()
        for spread_item in large:
            spread_item.finish()

        def gate_up(slot):
            s = pl.ds(pl.multiple_of(slot * 128, 128), 128)

            @tiles(1024, 512)
            def _(n):
                gate = nn(x[s, :], wg[:, n])
                up = nn(x[s, :], wu[:, n])
                sigmoid = jax.nn.sigmoid(gate)
                low = gate * sigmoid
                silu[s, n] = low.astype(BF16)
                gate_factor[s, n] = (up * (sigmoid + low * (1.0 - sigmoid))).astype(BF16)
                inner[s, n] = (low * up).astype(BF16)

        def spread_down(stage):
            if stage == 0:
                down_weights.share()
                down_weights.forward_far()
            elif stage == 1:
                down_weights.share_far()
        gather.run(gate_up, spread_down)
        down_weights.finish()

        def down(first_row):
            s = pl.ds(pl.multiple_of(first_row, 256), 256)

            @pl.loop(0, 2)
            def _(i):
                n = pl.ds(pl.multiple_of(i * 1024, 1024), 1024)
                part[s, n] = nn(inner[s, :], wd[:, n]).astype(BF16)

        scatter = ScatterTensor(part, bufs, *scatter_sems)
        scatter.run(down)
        for n in range(4):
            scatter.step(n)
        scatter.finish(total)
        mlp_part[...] = jnp.zeros_like(mlp_part)
        attn_part[...] = jnp.zeros_like(attn_part)
        own_d = rows(dd, me)

        @tiles(128, 16)
        def _(r):
            v = total[r, :]
            position = lax.broadcasted_iota(jnp.int32, (16, 1), 0) + (me * 128 + r.start)
            ok = position < length
            scale = lax.rsqrt(jnp.mean(v * v, 1, keepdims=True) + EPS)
            normal = v * scale
            part[r, :] = jnp.where(ok, residual[r, :] + normal * mlp_gain[...], 0.0).astype(BF16)
            grad = jnp.where(ok, cotangent[r, :].astype(F32), 0.0)
            residual[r, :] = grad
            mlp_part[...] += jnp.sum(grad * normal, 0, keepdims=True)
            weighted = mlp_gain[...] * grad
            mean = jnp.mean(v * weighted, 1, keepdims=True)
            own_d[r, :] = (scale * weighted - v * (scale * scale * scale * mean)).astype(BF16)

        gather = GatherTensor(dd, *gather_sems)
        gather.start()
        store_act = pltpu.make_async_copy(part.at[pl.ds(0, 128)], act, msem.at[1])
        store_act.start()

        def d_inner(slot):
            s = pl.ds(pl.multiple_of(slot * 128, 128), 128)

            @tiles(1024, 512)
            def _(n):
                d = nt(dd[s, :], wd[n, :])
                dg[s, n] = (d * gate_factor[s, n].astype(F32)).astype(BF16)
                du[s, n] = (d * silu[s, n].astype(F32)).astype(BF16)

        gather.run(d_inner)
        store_act.wait()
        tell(0)

        def d_input(first_row):
            s = pl.ds(pl.multiple_of(first_row, 256), 256)

            @pl.loop(0, 2)
            def _(i):
                n = pl.ds(pl.multiple_of(i * 1024, 1024), 1024)
                part[s, n] = (nt(dg[s, :], wg[n, :]) + nt(du[s, :], wu[n, :])).astype(BF16)

        scatter = ScatterTensor(part, bufs, *scatter_sems)
        scatter.run(d_input)
        scatter.step(0)

        def down_grad(i):
            m = pl.ds(i * 512, 512)

            @tiles(2048, 512)
            def _(n):
                wd[m, n] = tn(inner[:, m], dd[:, n]).astype(BF16)

        def gate_grad(first):
            @pl.loop(first, first + 2)
            def _(i):
                m = pl.ds(pl.multiple_of(i * 512, 512), 512)

                @tiles(1024, 512)
                def _(n):
                    wg[m, n] = tn(x[:, m], dg[:, n]).astype(BF16)

        down_grad(0)
        down_grad(1)
        scatter.step(1)
        tell(1)

        def by_rows(ref):
            return lambda n: ref.at[pl.ds(n * 128, 128)]

        def by_columns(ref):
            return lambda n: ref.at[:, pl.ds(n * 128, 128)]

        small_slots = [by_rows(gate_factor.at[:, pl.ds(256 * i, 256)]) for i in range(3)]
        small_slots.append(
            lambda n: gate_factor.at[
                pl.ds(n // 2 * 256, 256), pl.ds(768 + n % 2 * 128, 128)
            ]
        )
        slots = small_slots + [by_rows(silu), by_rows(inner), by_columns(gate_factor)]
        wholes = (wq, wk, silu, wo, wg, wu, wd)
        scatter_kinds = kinds[:2] + ("folded",) + kinds[3:]
        items = [ScatterDp(wholes[i], scatter_kinds[i], slots[i], *dp_bufs[i]) for i in range(7)]
        qk, value_item, out_item, gate_item, up_item, down_item = items[:2], *items[2:]
        pl.semaphore_wait(ready.at[0], 1)
        down_item.start()
        scatter.step(2)
        gate_grad(0)
        scatter.step(3)
        gate_grad(2)
        down_item.along_x()
        tell(2)
        gate_item.start()
        load_heads.start()
        scatter.finish(total)

        @tiles(128, 16)
        def _(r):
            grad = residual[r, :] + total[r, :]
            residual[r, :] = grad
            b = branch[r, :]
            scale = lax.rsqrt(jnp.mean(b * b, 1, keepdims=True) + EPS)
            attn_part[...] += jnp.sum(grad * b * scale, 0, keepdims=True)
            weighted = attn_gain[...] * grad
            mean = jnp.mean(b * weighted, 1, keepdims=True)
            own_d[r, :] = (scale * weighted - b * (scale * scale * scale * mean)).astype(BF16)

        gather = GatherTensor(dd, *gather_sems, 768)
        gather.start()


        gate_item.along_x()

        @tiles(2048, 512)
        def _(m):
            @tiles(1024, 512)
            def _(n):
                wu[m, n] = tn(x[:, m], du[:, n]).astype(BF16)

        reload.start()
        load_raw.start()
        pl.semaphore_wait(ready.at[1], 1)
        up_item.start()
        dk[...] = jnp.zeros_like(dk)
        dv[...] = jnp.zeros_like(dv)

        def attend_back(half):
            for top in range(2):

                @pl.when(half == top)
                def _():
                    @pl.loop(0, 2)
                    def _(h):
                        cols = pl.ds(pl.multiple_of(h * 128, 128), 128)
                        for i in (2 * top, 2 * top + 1):
                            low = i * 256
                            block = slice(low, low + 256)
                            q, d = q_rot[block, cols], do[block, cols]
                            peak = jnp.where(h == 0, stats[block, 0:1], stats[block, 64:65])
                            k1, v1 = k_rot[block, cols], v_low[block, cols]
                            p1 = jnp.exp(diagonal_mask(nt(q, k1), low, length) - peak)
                            dp1 = nt(d, v1)
                            delta = jnp.sum(p1 * dp1, 1, keepdims=True)
                            if i:
                                k0, v0 = k_rot[0:low, cols], v_low[0:low, cols]
                                p0 = jnp.exp(nt(q, k0) - peak)
                                dp0 = nt(d, v0)
                                delta += jnp.sum(p0 * dp0, 1, keepdims=True)
                            ds1 = (p1 * (dp1 - delta)).astype(BF16)
                            dq_block = nn(ds1, k1)
                            dk[block, cols] += tn(ds1, q)
                            dv[block, cols] += tn(p1.astype(BF16), d)
                            if i:
                                ds0 = (p0 * (dp0 - delta)).astype(BF16)
                                dq_block += nn(ds0, k0)
                                dk[0:low, cols] += tn(ds0, q)
                                dv[0:low, cols] += tn(p0.astype(BF16), d)
                            dq[block, cols] = dq_block

        def d_mixed(slot):
            s = pl.ds(pl.multiple_of(slot * 128, 128), 128)
            do[s, :] = nt(dd[s, :], wo[...]).astype(BF16)

        def beside(stage):
            if stage == 0:
                down_item.forward()
                load_heads.wait()
            elif stage == 1:
                gate_item.forward()
                up_item.along_x()
            else:
                down_item.along_y()

        gather.run(d_mixed, beside, attend_back)
        load_raw.wait()

        q_line[...] = jnp.zeros_like(q_line)
        k_line[...] = jnp.zeros_like(k_line)
        sums[me] = jnp.zeros((8, 256), F32)

        @tiles(1024, 256)
        def _(r):
            cos, sin = cos_sin(table[r, :])
            for source, rawer, gain, s, factor, line in (
                (dq, q_raw, q_gain, 128, SCALE, q_line),
                (dk, k_raw, k_gain, 192, 1.0, k_line),
            ):
                scale = stats[r, s : s + 1]
                for h in (0, 128):
                    v = source[r, h : h + 128] * factor
                    v = v * cos - pltpu.roll(v, 64, 1) * sin
                    w = v * rawer[r, h : h + 128].astype(F32)
                    line[:, h : h + 128] += jnp.sum(w * scale, 0, keepdims=True)
                    source[r, h : h + 128] = v * gain[:, h : h + 128]
            note_sums(
                sums.at[me],
                r,
                dq[r, :] * q_raw[r, :].astype(F32),
                dk[r, :] * k_raw[r, :].astype(F32),
            )
            dvr[r, :] = dv[r, :].astype(BF16)

        exchange = Exchange(sums, *sum_sems)
        exchange.start()
        reload.wait()
        row = lax.broadcasted_iota(jnp.int32, (8, 1024), 0)
        column = lax.broadcasted_iota(jnp.int32, (8, 1024), 1)
        message = jnp.zeros((8, 1024), F32)
        for k, line in enumerate((attn_part, attn_part, mlp_part, mlp_part)):
            line = line[:, 1024 * (k % 2) : 1024 * (k % 2) + 1024]
            message = jnp.where(row == 4 + k, line, message)
        for first_row, line in ((0, q_line), (2, k_line)):
            line = jnp.concatenate([line[...]] * 4, 1)
            message += jnp.where((row == first_row + yl) & (column // 256 == z), line, 0.0)
        gain_slots[me] = message
        total_gain = SumAll(gain_slots, gain_hold, gain_boxes, *isems)

        @pl.loop(0, 4)
        def _(i):
            m = pl.ds(pl.multiple_of(i * 512, 512), 512)
            r = pl.ds(pl.multiple_of(lax.rem(i, 2) * 512, 512), 512)
            columns = pl.ds(pl.multiple_of(i // 2 * 256, 256), 256)
            silu[r, columns] = tn(x[:, m], dvr[...]).astype(BF16)

        pl.semaphore_wait(ready.at[2], 1)
        value_item.start()
        exchange.finish()
        total_gain.start()
        gate_item.along_y()
        spread(dv, exchange.sum() * (1.0 / 2048))

        @tiles(1024, 256)
        def _(r):
            for source, rawer, s, target in ((dq, q_raw, 0, dqr), (dk, k_raw, 128, dkr)):
                scale = stats[r, 128 + s // 2 : 129 + s // 2]
                factor = scale * scale * scale * dv[r, s : s + 128]
                for h in (0, 128):
                    target[r, h : h + 128] = (
                        scale * source[r, h : h + 128]
                        - rawer[r, h : h + 128].astype(F32) * factor
                    ).astype(BF16)

        def d_tokens(first_row):
            s = pl.ds(pl.multiple_of(first_row, 256), 256)

            @pl.loop(0, 2)
            def _(i):
                n = pl.ds(pl.multiple_of(i * 1024, 1024), 1024)
                terms = nt(dqr[s, :], wq[n, :]) + nt(dkr[s, :], wk[n, :]) + nt(dvr[s, :], wv[n, :])
                part[s, n] = terms.astype(BF16)

        scatter = ScatterTensor(part, bufs, *scatter_sems, 512)
        scatter.run(d_tokens)
        up_item.forward()
        total_gain.core()
        scatter.step(0)
        value_item.along_x()
        total_gain.along_x()

        @tiles(2048, 512)
        def _(m):
            xt = x[:, m].T
            wq[m, :] = nn(xt, dqr[...]).astype(BF16)
            wk[m, :] = nn(xt, dkr[...]).astype(BF16)

        for item in qk:
            item.start()

        @tiles(2048, 512)
        def _(n):
            wo[:, n] = tn(mixed[...], dd[:, n]).astype(BF16)

        out_item.start()
        for item in qk:
            item.along_x()
        scatter.step(1)
        out_item.along_x()
        up_item.along_y()
        total_gain.along_y()
        value_item.forward()
        scatter.step(2)
        for item in qk:
            item.forward()
        out_item.forward()
        scatter.step(3)
        value_item.along_y()
        for item in qk:
            item.along_y()
        out_item.along_y()
        stores = []

        def store(item, source, target):
            item.finish(source)
            stores.append(pltpu.make_async_copy(source, target, lsem.at[len(stores)]))
            stores[-1].start()

        store(down_item, dv.at[:, pl.ds(0, 128)], o6)
        gate_item.finish(o4)
        scatter.finish(input_grad)

        @tiles(128, 16)
        def _(r):
            input_grad[r, :] += residual[r, :]

        up_item.finish(o5)
        total_gain.finish(gain_slots.at[0])
        for i, out in enumerate((q_sum, k_sum, attn_sum, mlp_sum)):
            out[:, 0:1024] = gain_slots[0, 2 * i : 2 * i + 1, :]
            out[:, 1024:2048] = gain_slots[0, 2 * i + 1 : 2 * i + 2, :]
        store(value_item, dk.at[pl.ds(256, 128)], o2)
        for i, out in enumerate((o0, o1)):
            store(qk[i], dk.at[pl.ds(128 * i, 128)], out)
        store(out_item, dv.at[pl.ds(0, 256), pl.ds(128, 128)], o3)
        for copy in stores:
            copy.wait()

    S = jax.ShapeDtypeStruct
    W = pltpu.VMEM
    scratch = [W((1024, 2048), BF16)] * 2 + [W((2048, 1024), BF16)] * 2 + [W((1024, 2048), BF16)]
    scratch += [W((1024, 1024), BF16)] * 5 + [W((1024, 2048), BF16)]
    scratch += [W((128, 2048), F32)] + [W((1, 2048), F32)] * 2 + [W((1, 256), F32)] * 2
    scratch += [W((2048, 256), BF16)] * 3 + [W((256, 2048), BF16)]
    scratch += [W((1024, 256), F32), W((128, 2048), F32), W((1024, 256), BF16)]
    scratch += [W((1024, 256), F32)] * 3
    scratch += [W((8, 8, 256), F32), W((8, 8, 1024), F32)] + [W((3, 8, 1024), F32), W((5, 8, 1024), F32)]
    scratch += ScatterTensor.scratch(512, CUT)
    for b in blocks:
        scratch += ScatterDp.scratch(b)
    scratch += [DMA, DMA((23,)), DMA, DMA((21,)), DMA, DMA((7,)), DMA((6,)), DMA((12,))]
    scratch += [DMA((7,)), DMA((7, 14))]
    scratch += [DMA((8,)), DMA((4,)), pltpu.SemaphoreType.REGULAR((3,))]
    return pl.pallas_call(
        layer_step,
        out_shape=[S((128, 2048), BF16), S((128, 2048), F32)]
        + [S(b, F32) for b in blocks]
        + [S((1, 2048), F32)] * 4
        + [S((1024, 2048), BF16), S((1024, 1024), BF16), S((1024, 512), BF16)],
        in_specs=[SMEM] + [VM] * 6 + [ANY] * 8,
        out_specs=[ANY, VM] + [ANY] * 4 + [VM] * 2 + [ANY] + [VM] * 4 + [ANY] * 3,
        scratch_shapes=scratch,
        compiler_params=params(1),
        name="layer_step",
    )(lengths, cotangent, *gains, table, tokens, *weights)[:13]


def hand_over(*arrays):
    n = len(arrays)

    def hand_over_step(*refs):
        held, (lsem, ssem) = refs[2 * n : 3 * n], refs[3 * n :]
        loads = [pltpu.make_async_copy(refs[i], held[i], lsem.at[i]) for i in range(n)]
        stores = [pltpu.make_async_copy(held[i], refs[n + i], ssem.at[i]) for i in range(n)]
        for copy in loads:
            copy.start()
        for load, store in zip(loads, stores):
            load.wait()
            store.start()
        for copy in stores:
            copy.wait()

    return pl.pallas_call(
        hand_over_step,
        out_shape=[jax.ShapeDtypeStruct(a.shape, a.dtype) for a in arrays],
        in_specs=[ANY] * n,
        out_specs=[ANY] * n,
        scratch_shapes=[pltpu.VMEM(a.shape, a.dtype) for a in arrays] + [DMA((n,))] * 2,
        compiler_params=pltpu.CompilerParams(vmem_limit_bytes=63 << 20),
        name="hand_over_step",
    )(*arrays)


def local(
    tokens, lengths, w_query, w_key, w_value, w_out, w_gate, w_up, w_down,
    q_gain, k_gain, attn_gain, mlp_gain, cotangent,
):
    weights = (w_query, w_key, w_value, w_out, w_gate, w_up, w_down)
    gains = (q_gain[None], k_gain[None], attn_gain[None], mlp_gain[None])
    results = whole_layer(tokens[0], lengths, cotangent[0], gains, weights, rope_table())
    act, input_grad, *grads = hand_over(*results)
    return (act[None], input_grad[None], *grads[:7], *(g.reshape(2048) for g in grads[7:]))


def solution(mesh):
    return jax.shard_map(
        local,
        mesh=mesh,
        in_specs=(
            P("dp", "tensor", None),
            P("dp"),
            P("dp", "tensor"),
            P("dp", "tensor"),
            P("dp", "tensor"),
            P("tensor", "dp"),
            P("dp", "tensor"),
            P("dp", "tensor"),
            P("tensor", "dp"),
            P(),
            P(),
            P(),
            P(),
            P("dp", "tensor", None),
        ),
        out_specs=(
            P("dp", "tensor", None),
            P("dp", "tensor", None),
            P("dp", "tensor"),
            P("dp", "tensor"),
            P("dp", "tensor"),
            P("tensor", "dp"),
            P("dp", "tensor"),
            P("dp", "tensor"),
            P("tensor", "dp"),
            P(),
            P(),
            P(),
            P(),
        ),
        check_vma=False,
    )
```

```python
import jax
import jax.numpy as jnp
import numpy as np
from jax import lax
from jax.experimental import pallas as pl
from jax.experimental.pallas import tpu as pltpu
from jax.sharding import PartitionSpec as P

HEAD_DIM = 128
EPS = 1e-06
THETA = 500000.0
MESH = pl.DeviceIdType.MESH
BF16 = jnp.bfloat16
F32 = jnp.float32
ANY = pl.BlockSpec(memory_space=pl.ANY)
VM = pl.BlockSpec(memory_space=pltpu.VMEM)
DMA = pltpu.SemaphoreType.DMA
CUT = 896
WIDTH = 2048


def place():
    d = lax.axis_index("dp")
    t = lax.axis_index("tensor")
    return d // 8, lax.rem(d // 2, 4), lax.rem(d, 2), t // 4, lax.rem(t, 4)


def other(dyh=0, dx=0, dc=0, dyl=0, dz=0):
    yh, x, c, yl, z = place()
    return (
        lax.rem(yh + dyh, 2) * 8 + lax.rem(x + dx, 4) * 2 + lax.rem(c + dc, 2),
        lax.rem(yl + dyl, 2) * 4 + lax.rem(z + dz, 4),
    )


TENSOR_PEERS = (dict(dz=1), dict(dz=3), dict(dyl=1))
DP_PEERS = (dict(dx=1), dict(dx=2), dict(dx=3), dict(dyh=1), dict(dc=1))
SMEM = pl.BlockSpec(memory_space=pltpu.SMEM)


def greet(peers):
    barrier = pltpu.get_barrier_semaphore()
    for peer in peers:
        pl.semaphore_signal(barrier, 1, device_id=other(**peer), device_id_type=MESH)
    pl.semaphore_wait(barrier, len(peers))


def remote(src, dst, sems, index, peer):
    ssem, rsem = sems
    return pltpu.make_async_remote_copy(
        src_ref=src,
        dst_ref=dst,
        send_sem=ssem,
        recv_sem=rsem.at[index],
        device_id=other(**peer),
        device_id_type=MESH,
    )


def all_of(bytes_of, sem):
    pltpu.make_async_copy(bytes_of, bytes_of, sem).wait()


def rows(ref, slot):
    return ref.at[pl.ds(pl.multiple_of(slot * 128, 128), 128)]


def halves(ref):
    half = ref.shape[0] // 2
    return ref.at[pl.ds(0, half)], ref.at[pl.ds(half, half)]


def add_into(out, *terms):
    step = min(out.shape[0], 16 if out.shape[1] > 1024 else 64 if out.shape[1] > 128 else 128)

    @pl.loop(0, out.shape[0] // step)
    def _(i):
        r = pl.ds(pl.multiple_of(i * step, step), step)
        if len(terms) == 2 and out.dtype == BF16:
            out[r, :] = terms[0][r, :] + terms[1][r, :]
        else:
            total = terms[0][r, :].astype(F32)
            for term in terms[1:]:
                total += term[r, :].astype(F32)
            out[r, :] = total.astype(out.dtype)


class RingGather:
    COPIES = 6

    def __init__(self, block, axis, sems, base, source=None):
        up, down = {axis: 1}, {axis: 3}
        src = halves(block(0) if source is None else source)
        own, behind, ahead = halves(block(0)), halves(block(3)), halves(block(1))
        self.copies = [
            remote(src[0], own[0], sems, base, up),
            remote(src[1], own[1], sems, base + 1, down),
            remote(src[1], own[1], sems, base + 2, up),
            remote(src[0], own[0], sems, base + 3, down),
            remote(behind[0], behind[0], sems, base + 4, up),
            remote(ahead[1], ahead[1], sems, base + 5, down),
        ]

    def start(self):
        for copy in self.copies[:4]:
            copy.start()

    def forward(self):
        for i in range(2):
            self.copies[i].wait_recv()
            self.copies[4 + i].start()

    def behind(self):
        self.copies[2].wait_recv()

    def ahead(self):
        self.copies[3].wait_recv()

    def far(self):
        for copy in self.copies[4:]:
            copy.wait_recv()


class RingReduce:
    COPIES = 6

    @staticmethod
    def scratch(n, m):
        return [pltpu.VMEM((2, n // 2, m), BF16), pltpu.VMEM((2, n, m), BF16)]

    def __init__(self, block, axis, part, full, sems, base):
        up, down = {axis: 1}, {axis: 3}
        one, two, three = halves(block(1)), halves(block(2)), halves(block(3))
        from_behind, from_ahead = halves(full.at[0]), halves(full.at[1])
        self.adds = ((one[0], part.at[0]), (three[1], part.at[1]))
        self.terms = (block(0), full.at[0], full.at[1])
        self.copies = [
            remote(two[0], part.at[0], sems, base, up),
            remote(two[1], part.at[1], sems, base + 1, down),
            remote(one[1], from_behind[1], sems, base + 2, up),
            remote(three[0], from_ahead[0], sems, base + 3, down),
            remote(one[0], from_behind[0], sems, base + 4, up),
            remote(three[1], from_ahead[1], sems, base + 5, down),
        ]

    def start(self):
        for copy in self.copies[:4]:
            copy.start()

    def forward(self):
        for i in range(2):
            self.copies[i].wait_recv()
            add_into(self.adds[i][0], *self.adds[i])
            self.copies[4 + i].start()

    def arrive(self):
        for copy in self.copies[2:]:
            copy.wait_recv()


class GatherTensor:
    COPIES = 21

    def __init__(self, buf, ssem, rsem, cut=CUT):
        yh, x, c, yl, z = place()
        self.yl, self.z = yl, z
        self.sent, self.ssem = buf.at[pl.ds(0, 896)], ssem
        sems = (ssem, rsem)
        slot = lambda k, i: rows(buf, lax.rem(yl + k, 2) * 4 + lax.rem(z + i, 4))
        low = lambda ref: ref.at[:, pl.ds(0, cut)]
        high = lambda ref: ref.at[:, pl.ds(cut, WIDTH - cut)]
        self.ring = RingGather(lambda i: slot(0, i), "dz", sems, 0)
        self.pair_ring = RingGather(lambda i: high(slot(1, i)), "dz", sems, 6)
        own = slot(0, 0)
        pair = dict(dyl=1)
        self.high = remote(high(own), high(own), sems, 12, pair)
        self.low = []
        for n, i in enumerate((0, 3, 1, 2)):
            for half in halves(low(slot(0, i))):
                self.low.append(remote(half, half, sems, 13 + len(self.low), pair))

    def start(self):
        self.high.start()
        self.ring.start()
        self.low[0].start()
        self.low[1].start()

    def run(self, process, spare=None, by_block=None, early=None, first=3):
        yl, z = self.yl, self.z

        @pl.loop(0, 2)
        def _(k):
            @pl.when(k == 1)
            def _():
                self.ring.forward()
                self.low[2].start()
                self.low[5].start()
                if early is not None:
                    early()
                self.high.wait_recv()
                self.pair_ring.start()
                self.ring.behind()
                self.low[3].start()
                self.ring.ahead()
                self.low[4].start()
                self.low[0].wait_recv()
                self.low[1].wait_recv()

            process(lax.rem(yl + k, 2) * 4 + z)

        if spare is not None:
            spare(0)

        @pl.loop(0, 6 if by_block is None else 7)
        def _(j):
            if spare is not None:
                for stage, at in ((1, 3), (2, 5)):

                    @pl.when(j == at)
                    def _():
                        spare(stage)

            if by_block is not None:
                last = j // 6
                rest = 2 - 2 * yl + last * (1 - z // 2) + (1 - last) * (z // 2)

                @pl.when((j >= 5) | (j == first))
                def _():
                    @pl.loop(0, 3)
                    def _(t):
                        third = t // 2

                        @pl.when(((t < 2) & (j == first)) | ((t == 2) & (j >= 5)))
                        def _():
                            by_block((1 - third) * (2 * yl + t) + third * rest)

            @pl.when(j == 2)
            def _():
                self.ring.far()
                self.low[6].start()
                self.low[7].start()
                self.pair_ring.forward()

            @pl.when(j == 3)
            def _():
                self.pair_ring.behind()
                self.low[2].wait_recv()
                self.low[3].wait_recv()

            @pl.when(j == 4)
            def _():
                self.pair_ring.ahead()
                self.low[4].wait_recv()
                self.low[5].wait_recv()

            @pl.when(j == 5)
            def _():
                self.pair_ring.far()
                self.low[6].wait_recv()
                self.low[7].wait_recv()

            i = lax.rem(j, 3)
            step = (3 * i * i - 7 * i + 6) // 2

            @pl.when(j < 6)
            def _():
                process(lax.rem(yl + j // 3, 2) * 4 + lax.rem(z + step, 4))

        all_of(self.sent, self.ssem)


class ScatterTensor:
    COPIES = 23

    @staticmethod
    def scratch(least, most):
        return (
            [pltpu.VMEM((4, 128, most), BF16), pltpu.VMEM((128, WIDTH - least), BF16)]
            + RingReduce.scratch(128, most)
            + RingReduce.scratch(128, WIDTH - least) * 2
        )

    def __init__(self, part, bufs, ssem, rsem, cut=CUT):
        yh, x, c, yl, z = place()
        self.z = z
        narrow = lambda ref, n: ref.at[:, :, pl.ds(0, n)]
        wide = WIDTH - cut
        bufs = [
            narrow(bufs[0], cut),
            bufs[1].at[:, pl.ds(0, wide)],
            *(narrow(ref, cut) for ref in bufs[2:4]),
            *(narrow(ref, wide) for ref in bufs[4:]),
        ]
        self.yl = yl
        self.from_pair, self.last = bufs[0], bufs[1]
        self.sent, self.ssem = part.at[pl.ds(0, 896)], ssem
        sems = (ssem, rsem)
        slot = lambda k, i: rows(part, lax.rem(yl + k, 2) * 4 + lax.rem(z + i, 4))
        low = lambda k, i: slot(k, i).at[:, pl.ds(0, cut)]
        high = lambda k, i: slot(k, i).at[:, pl.ds(cut, wide)]
        self.cut = cut
        pair = dict(dyl=1)
        self.low = lambda i: low(0, i)
        self.low_ring = RingReduce(lambda i: low(0, i), "dz", bufs[2], bufs[3], sems, 0)
        self.pair_ring = RingReduce(lambda i: high(1, i), "dz", bufs[4], bufs[5], sems, 6)
        self.own_ring = RingReduce(lambda i: high(0, i), "dz", bufs[6], bufs[7], sems, 12)
        self.first = lambda i: remote(low(1, i), bufs[0].at[i], sems, 18 + i, pair)
        self.second = remote(high(1, 0), bufs[1], sems, 22, pair)

    def run(self, process):
        yl, z = self.yl, self.z

        @pl.loop(0, 4)
        def _(k):
            half = lax.rem(yl + 1 + k // 2, 2)
            process(half * 512 + lax.rem((z + 2) // 2 + k, 2) * 256)
            beside = 3 - 2 * lax.rem(z, 2)

            @pl.when(k == 0)
            def _():
                self.first(2).start()
                self.pair_ring.copies[0].start()
                self.pair_ring.copies[1].start()
                self.first(beside).start()

            @pl.when(k == 1)
            def _():
                self.first(4 - beside).start()
                self.pair_ring.copies[2].start()
                self.pair_ring.copies[3].start()
                self.first(0).start()

    def add_first(self, i):
        self.first(i).wait_recv()
        add_into(self.low(i), self.low(i), self.from_pair.at[i])

    def add_low(self, i):
        self.add_first(i)
        for k in (1, 3):

            @pl.when(i == k)
            def _():
                self.low_ring.copies[2 + k // 3].start()

    def step(self, n):
        beside = 3 - 2 * lax.rem(self.z, 2)
        if n == 0:
            self.pair_ring.forward()
            self.own_ring.start()
            self.add_first(2)
            self.low_ring.copies[0].start()
            self.low_ring.copies[1].start()
        if n == 1:
            self.own_ring.forward()
            self.add_low(beside)
        if n == 2:
            self.pair_ring.arrive()
            add_into(self.pair_ring.terms[0], *self.pair_ring.terms)
            self.second.start()
            self.add_low(4 - beside)
        if n == 3:
            self.low_ring.forward()
            self.add_first(0)

    def finish(self, out):
        self.own_ring.arrive()
        self.second.wait_recv()
        add_into(out.at[:, pl.ds(self.cut, WIDTH - self.cut)], *self.own_ring.terms, self.last)
        self.low_ring.arrive()
        add_into(out.at[:, pl.ds(0, self.cut)], *self.low_ring.terms)
        all_of(self.sent, self.ssem)


def block_of(ref, kind, slot):
    if kind == "row":
        size = ref.shape[0] // 16
        return ref.at[pl.ds(pl.multiple_of(slot * size, size), size)]
    if kind == "folded":
        return ref.at[
            pl.ds(pl.multiple_of(lax.rem(slot, 8) * 128, 128), 128),
            pl.ds(pl.multiple_of(slot // 8 * 256, 256), 256),
        ]
    size = ref.shape[1] // 16
    return ref.at[:, pl.ds(pl.multiple_of(slot * size, size), size)]


def some_of(ref, kind, count):
    if kind == "row":
        return ref.at[pl.ds(0, ref.shape[0] // 16 * count)]
    if kind == "folded":
        return ref.at[pl.ds(0, 64 * count), pl.ds(0, 512)]
    return ref.at[:, pl.ds(0, ref.shape[1] // 16 * count)]


class GatherDp:
    COPIES = 21

    def __init__(self, shard, out, kind, ssem, rsem, lsem):
        yh, x, c, yl, z = place()
        sems = (ssem, rsem)
        block = lambda k, i: block_of(
            out, kind, lax.rem(yh + k, 2) * 8 + lax.rem(x + i, 4) * 2 + c
        )
        self.sent, self.ssem = some_of(out, kind, 15), ssem
        self.local = pltpu.make_async_copy(shard, block(0, 0), lsem)
        self.ring = RingGather(lambda i: block(0, i), "dx", sems, 0, shard)
        self.far_ring = RingGather(lambda i: block(1, i), "dx", sems, 6)
        self.own_y = remote(shard, block(0, 0), sems, 12, dict(dyh=1))
        core = dict(dc=1)
        self.core = [remote(shard, block(0, 0), sems, 13, core)]
        for n in range(1, 8):
            ref = block(n // 4, n % 4)
            self.core.append(remote(ref, ref, sems, 13, core))
        self.shared, self.shared_sem = some_of(out, kind, 8), rsem.at[13]

    def start(self):
        self.ring.start()
        self.core[0].start()
        self.local.start()

    def forward(self):
        self.ring.forward()

    def forward_y(self):
        self.own_y.wait_recv()
        self.far_ring.start()
        self.core[4].start()

    def share(self):
        self.ring.behind()
        self.core[3].start()
        self.ring.ahead()
        self.core[1].start()
        self.ring.far()
        self.core[2].start()

    def forward_far(self):
        self.far_ring.forward()

    def share_far(self):
        self.far_ring.behind()
        self.core[7].start()
        self.far_ring.ahead()
        self.core[5].start()
        self.far_ring.far()
        self.core[6].start()

    def finish(self):
        all_of(self.shared, self.shared_sem)
        self.local.wait()
        all_of(self.sent, self.ssem)


class ScatterDp:
    COPIES = 21

    @staticmethod
    def scratch(block):
        return (
            [pltpu.VMEM(block, BF16)]
            + RingReduce.scratch(*block) * 2
            + [DMA, DMA((14,))]
        )

    def __init__(self, part, kind, from_core, from_y, h0, f0, h1, f1, ssem, rsem):
        yh, x, c, yl, z = place()
        sems = (ssem, rsem)
        self.from_core, self.from_y = from_core, from_y
        self.sent, self.ssem = some_of(part, kind, 15), ssem
        block = lambda k, i, d: block_of(
            part, kind, lax.rem(yh + k, 2) * 8 + lax.rem(x + i, 4) * 2 + d
        )
        self.block = lambda k, i: block(k, i, c)
        self.core = [
            remote(block(n // 4, n % 4, 1 - c), from_core(n), sems, 0, dict(dc=1))
            for n in range(8)
        ]
        self.ring = RingReduce(lambda i: block(0, i, c), "dx", h0, f0, sems, 1)
        self.far_ring = RingReduce(lambda i: block(1, i, c), "dx", h1, f1, sems, 7)
        self.last = remote(block(1, 0, c), from_y, sems, 13, dict(dyh=1))
        self.shared, self.shared_sem = some_of(part, kind, 8), rsem.at[0]

    def start(self):
        for n in (6, 5, 7, 4, 2, 1, 3, 0):
            self.core[n].start()

    def add_core(self, n):
        ref = self.block(n // 4, n % 4)
        add_into(ref, ref, self.from_core(n))

    def along_x(self):
        all_of(self.shared, self.shared_sem)
        for n in (6, 5, 7):
            self.add_core(n)
        self.far_ring.start()
        for n in (2, 1, 3):
            self.add_core(n)
        self.ring.start()
        for n in (4, 0):
            self.add_core(n)

    def forward(self):
        self.far_ring.forward()
        self.ring.forward()

    def along_y(self):
        self.far_ring.arrive()
        add_into(self.far_ring.terms[0], *self.far_ring.terms)
        self.last.start()

    def finish(self, out):
        self.ring.arrive()
        self.last.wait_recv()
        add_into(out, *self.ring.terms, self.from_y)
        all_of(self.sent, self.ssem)


def params(cid):
    return pltpu.CompilerParams(
        collective_id=cid, has_side_effects=True, vmem_limit_bytes=65400 << 10
    )


def nn(a, b):
    return jnp.dot(a, b, preferred_element_type=F32)


def nt(a, b):
    return lax.dot_general(a, b, (((1,), (1,)), ((), ())), preferred_element_type=F32)


def tn(a, b):
    return lax.dot_general(a, b, (((0,), (0,)), ((), ())), preferred_element_type=F32)


def tiles(count, size):
    def run(body):
        @pl.loop(0, count // size)
        def _(i):
            body(pl.ds(pl.multiple_of(i * size, size), size))

    return run


def rope_table():
    frequency = THETA ** (-(np.arange(64, dtype=np.float32) * np.float32(2.0) / np.float32(HEAD_DIM)))
    angles = np.arange(1024, dtype=np.float32)[:, None] * frequency.astype(np.float32)[None, :]
    cosine, sine = np.cos(angles), np.sin(angles)
    return np.concatenate([cosine, sine], 1).astype(np.float32)


def cos_sin(table):
    turned = pltpu.roll(table, 64, 1)
    first = lax.broadcasted_iota(jnp.int32, table.shape, 1) < 64
    return jnp.where(first, table, turned), jnp.where(first, -turned, table)


class Exchange:
    PEERS = tuple(dict(dz=a, dyl=b) for b in range(2) for a in range(4) if a or b)

    def __init__(self, buf, ssem, rsem):
        yh, x, c, yl, z = place()
        self.buf, self.ssem = buf, ssem
        self.mine = buf.at[yl * 4 + z]
        self.copies = [
            remote(self.mine, self.mine, (ssem, rsem), i, peer)
            for i, peer in enumerate(self.PEERS)
        ]

    def start(self):
        for copy in self.copies:
            copy.start()

    def finish(self):
        for copy in self.copies:
            copy.wait_recv()
        all_of(self.buf.at[pl.ds(0, 7)], self.ssem)

    def sum(self):
        total = self.buf[0]
        for i in range(1, 8):
            total += self.buf[i]
        return total


def row_sums(values):
    return nt(jnp.ones((8, values.shape[1]), F32), values)


def spread(out, pair):
    row = lax.broadcasted_iota(jnp.int32, (8, 256), 0)
    column = lax.broadcasted_iota(jnp.int32, (8, 256), 1)
    for i in range(4):
        pick = jnp.where(row == column // 128 * 4 + i, 1.0, 0.0)
        out[pl.ds(256 * i, 256), :] = lax.dot_general(
            pair,
            pick,
            (((0,), (0,)), ((), ())),
            precision=lax.Precision.HIGHEST,
            preferred_element_type=F32,
        )


def note_sums(out, r, a, b):
    row = lax.broadcasted_iota(jnp.int32, (8, 256), 0)
    sums = jnp.where(row < 4, row_sums(a), row_sums(b))
    out[...] = jnp.where(lax.rem(row, 4) == r.start // 256, sums, out[...])


ALL_PEERS = Exchange.PEERS + DP_PEERS
SCALE = HEAD_DIM**-0.5


def diagonal_mask(scores, first, length):
    row = lax.broadcasted_iota(jnp.int32, scores.shape, 0)
    column = lax.broadcasted_iota(jnp.int32, scores.shape, 1)
    return jnp.where((column <= row) & (column + first < length), scores, -1e30)


class SumAll:
    def __init__(self, slots, hold, boxes, ssem, rsem):
        self.exchange = Exchange(slots, ssem.at[5], rsem)
        self.hold, self.boxes = hold, boxes
        self.copies = []
        for i, peer in enumerate(DP_PEERS):
            k = (1, 1, 1, 2, 0)[i]
            self.copies.append(remote(hold.at[k], boxes.at[i], (ssem.at[i], rsem), 7 + i, peer))

    def start(self):
        self.exchange.start()

    def core(self):
        self.exchange.finish()
        self.hold[0] = self.exchange.sum()
        self.copies[4].start()

    def along_x(self):
        self.copies[4].wait()
        self.hold[1] = self.hold[0] + self.boxes[4]
        for copy in self.copies[:3]:
            copy.start()

    def along_y(self):
        for copy in self.copies[:3]:
            copy.wait()
        self.hold[2] = self.hold[1] + self.boxes[0] + self.boxes[1] + self.boxes[2]
        self.copies[3].start()

    def finish(self, out):
        self.copies[3].wait()
        out[...] = self.hold[2] + self.boxes[3]


def whole_layer(tokens, lengths, cotangent, gains, weights, table):
    kinds = ("row", "row", "row", "col", "row", "row", "col")
    blocks = ((128, 256),) * 3 + ((256, 128), (128, 1024), (128, 1024), (1024, 128))

    def layer_step(
        lengths, cotangent, q_gain_all, k_gain_all, attn_gain, mlp_gain, table,
        tokens, i0, i1, i2, i3, i4, i5, i6,
        act, input_grad, o0, o1, o2, o3, o4, o5, o6,
        q_sum, k_sum, attn_sum, mlp_sum, x_kept, heads_kept, raw_kept,
        x, dd, wg, wu, wd, gate_factor, silu, inner, dg, du, part, residual, attn_part, mlp_part, q_line, k_line,
        wq, wk, wv, wo, stats, branch, total, gate_out, up_out, do, dq, dk, dv, sums, gain_slots, gain_hold, gain_boxes,
        *rest,
    ):
        bufs, rest = rest[:8], rest[8:]
        dp_bufs, rest = [rest[7 * i : 7 * i + 7] for i in range(7)], rest[49:]
        scatter_sems, gather_sems, sum_sems, isems, wsems = [
            rest[2 * i : 2 * i + 2] for i in range(5)
        ]
        lsem, msem, ready = rest[10:]
        yh, xx, c, yl, z = place()
        me = yl * 4 + z
        length = lengths[0]
        own_columns = pl.ds(pl.multiple_of(me * 256, 256), 256)
        q_gain, k_gain = q_gain_all[:, own_columns], k_gain_all[:, own_columns]
        q_rot, k_rot, v_low, mixed = (dg.at[:, pl.ds(256 * i, 256)] for i in range(4))
        q_raw, k_raw, dvr = (du.at[:, pl.ds(256 * i, 256)] for i in range(3))
        dqr, dkr = q_raw, k_raw
        raw = du.at[:, pl.ds(0, 512)]
        load_heads = pltpu.make_async_copy(heads_kept, dg, msem.at[0])
        load_raw = pltpu.make_async_copy(raw_kept, raw, msem.at[2])
        reload = pltpu.make_async_copy(x_kept, x, msem.at[1])
        keep_x = pltpu.make_async_copy(dd, x_kept, msem.at[1])
        keep_heads = pltpu.make_async_copy(dg, heads_kept, msem.at[0])
        keep_raw = pltpu.make_async_copy(raw, raw_kept, msem.at[2])
        first = pltpu.make_async_copy(tokens, rows(dd, me), msem.at[3])
        first.start()
        greet(ALL_PEERS)
        shards = (i0, i1, i2, i3, i4, i5, i6)
        targets = (wq, wk, wv, wo, wg, wu, wd)
        spreads = [
            GatherDp(shards[i], targets[i], kinds[i], wsems[0].at[i], wsems[1].at[i], lsem.at[i])
            for i in range(7)
        ]
        small, large, down_weights = spreads[:4], spreads[4:6], spreads[6]
        for spread_item in small:
            spread_item.start()
            spread_item.own_y.start()
        first.wait()
        gather = GatherTensor(dd, *gather_sems, 384)
        gather.start()

        sums[me] = jnp.zeros((8, 256), F32)

        def forward_small():
            for spread_item in small:
                spread_item.forward()
                spread_item.forward_y()

        def spread_small(stage):
            for spread_item in small:
                if stage == 0:
                    spread_item.share()
                    spread_item.forward_far()
                elif stage == 1:
                    spread_item.share_far()
                else:
                    spread_item.finish()
            if stage == 1:
                down_weights.own_y.start()
            if stage == 2:
                for spread_item in large:
                    spread_item.start()
                large[0].own_y.start()

        def heads(i):
            r = pl.ds(pl.multiple_of(i * 256, 256), 256)
            q = nn(dd[r, :], wq[...])
            k = nn(dd[r, :], wk[...])
            dq[r, :] = q
            dk[r, :] = k
            du[r, 0:256] = q.astype(BF16)
            du[r, 256:512] = k.astype(BF16)
            v_low[r, :] = nn(dd[r, :], wv[...]).astype(BF16)
            note_sums(sums.at[me], r, q * q, k * k)

        gather.run(lambda slot: None, spread_small, heads, forward_small, 5)
        keep_x.start()
        exchange = Exchange(sums, *sum_sems)
        exchange.start()
        keep_raw.start()
        exchange.finish()
        large[1].own_y.start()
        for spread_item in large:
            spread_item.forward()
        large[0].forward_y()
        spread(dv, lax.rsqrt(exchange.sum() * (1.0 / 2048) + EPS))
        narrow = lax.broadcasted_iota(jnp.int32, (1024, 128), 1) < 64
        stats[:, 128:256] = jnp.where(narrow, dv[:, 0:128], dv[:, 128:256])

        @tiles(1024, 256)
        def _(r):
            cos, sin = cos_sin(table[r, :])
            for source, gain, s, target, factor in (
                (dq, q_gain, 0, q_rot, SCALE),
                (dk, k_gain, 128, k_rot, 1.0),
            ):
                scale = dv[r, s : s + 128]
                for h in (0, 128):
                    v = source[r, h : h + 128] * scale * gain[:, h : h + 128]
                    v = v * cos + pltpu.roll(v, 64, 1) * sin
                    target[r, h : h + 128] = (v * factor).astype(BF16)

        def attend(wanted):
            for i in range(4):

                @pl.when(wanted == i)
                def _():
                    @pl.loop(0, 2)
                    def _(h):
                        cols = pl.ds(pl.multiple_of(h * 128, 128), 128)
                        mine = lax.broadcasted_iota(jnp.int32, (256, 128), 1) // 64 == h
                        low = i * 256
                        block = slice(low, low + 256)
                        q = q_rot[block, cols]
                        near = diagonal_mask(nt(q, k_rot[block, cols]), low, length)
                        peak = jnp.max(near, 1, keepdims=True)
                        if i:
                            past = nt(q, k_rot[0:low, cols])
                            peak = jnp.maximum(peak, jnp.max(past, 1, keepdims=True))
                        e1 = jnp.exp(near - peak)
                        denom = jnp.sum(e1, 1, keepdims=True)
                        out = nn(e1.astype(BF16), v_low[block, cols])
                        if i:
                            e0 = jnp.exp(past - peak)
                            denom += jnp.sum(e0, 1, keepdims=True)
                            out += nn(e0.astype(BF16), v_low[0:low, cols])
                        mixed[block, cols] = (out / denom).astype(BF16)
                        lse = peak + jnp.log(denom)
                        stats[block, 0:128] = jnp.where(mine, lse, stats[block, 0:128])

        def project(first_row):
            attend(first_row // 256)
            s = pl.ds(pl.multiple_of(first_row, 256), 256)

            @pl.loop(0, 2)
            def _(i):
                n = pl.ds(pl.multiple_of(i * 1024, 1024), 1024)
                part[s, n] = nn(mixed[s, :], wo[:, n]).astype(BF16)

        scatter = ScatterTensor(part, bufs, *scatter_sems)
        scatter.run(project)
        keep_heads.start()
        large[1].forward_y()
        scatter.step(0)
        for spread_item in large:
            spread_item.share()
        scatter.step(1)
        for spread_item in large:
            spread_item.forward_far()
        down_weights.start()
        down_weights.forward_y()
        scatter.step(2)
        scatter.step(3)
        for spread_item in large:
            spread_item.share_far()
        scatter.finish(branch)
        own = rows(x, me)
        own_tokens = rows(dd, me)
        for copy in (keep_x, keep_raw, keep_heads):
            copy.wait()

        def tell(i):
            pl.semaphore_signal(ready.at[i], 1, device_id=other(dc=1), device_id_type=MESH)

        @tiles(128, 16)
        def _(r):
            b = branch[r, :]
            scale = lax.rsqrt(jnp.mean(b * b, 1, keepdims=True) + EPS)
            value = own_tokens[r, :].astype(F32) + b * scale * attn_gain[...]
            residual[r, :] = value
            own[r, :] = value.astype(BF16)

        gather = GatherTensor(x, *gather_sems)
        gather.start()
        down_weights.forward()
        for spread_item in large:
            spread_item.finish()

        def gate_up(slot):
            s = pl.ds(pl.multiple_of(slot * 128, 128), 128)

            @tiles(1024, 512)
            def _(n):
                gate = nn(x[s, :], wg[:, n])
                up = nn(x[s, :], wu[:, n])
                sigmoid = jax.nn.sigmoid(gate)
                low = gate * sigmoid
                silu[s, n] = low.astype(BF16)
                gate_factor[s, n] = (up * (sigmoid + low * (1.0 - sigmoid))).astype(BF16)
                inner[s, n] = (low * up).astype(BF16)

        def spread_down(stage):
            if stage == 0:
                down_weights.share()
                down_weights.forward_far()
            elif stage == 1:
                down_weights.share_far()
        gather.run(gate_up, spread_down)
        down_weights.finish()

        def down(first_row):
            s = pl.ds(pl.multiple_of(first_row, 256), 256)

            @pl.loop(0, 2)
            def _(i):
                n = pl.ds(pl.multiple_of(i * 1024, 1024), 1024)
                part[s, n] = nn(inner[s, :], wd[:, n]).astype(BF16)

        scatter = ScatterTensor(part, bufs, *scatter_sems)
        scatter.run(down)
        for n in range(4):
            scatter.step(n)
        scatter.finish(total)
        mlp_part[...] = jnp.zeros_like(mlp_part)
        attn_part[...] = jnp.zeros_like(attn_part)
        own_d = rows(dd, me)

        @tiles(128, 16)
        def _(r):
            v = total[r, :]
            position = lax.broadcasted_iota(jnp.int32, (16, 1), 0) + (me * 128 + r.start)
            ok = position < length
            scale = lax.rsqrt(jnp.mean(v * v, 1, keepdims=True) + EPS)
            normal = v * scale
            part[r, :] = jnp.where(ok, residual[r, :] + normal * mlp_gain[...], 0.0).astype(BF16)
            grad = jnp.where(ok, cotangent[r, :].astype(F32), 0.0)
            residual[r, :] = grad
            mlp_part[...] += jnp.sum(grad * normal, 0, keepdims=True)
            weighted = mlp_gain[...] * grad
            mean = jnp.mean(v * weighted, 1, keepdims=True)
            own_d[r, :] = (scale * weighted - v * (scale * scale * scale * mean)).astype(BF16)

        gather = GatherTensor(dd, *gather_sems)
        gather.start()
        store_act = pltpu.make_async_copy(part.at[pl.ds(0, 128)], act, msem.at[1])
        store_act.start()

        def d_inner(slot):
            s = pl.ds(pl.multiple_of(slot * 128, 128), 128)

            @tiles(1024, 512)
            def _(n):
                d = nt(dd[s, :], wd[n, :])
                dg[s, n] = (d * gate_factor[s, n].astype(F32)).astype(BF16)
                du[s, n] = (d * silu[s, n].astype(F32)).astype(BF16)

        gather.run(d_inner)
        store_act.wait()
        tell(0)

        def d_input(first_row):
            s = pl.ds(pl.multiple_of(first_row, 256), 256)

            @pl.loop(0, 2)
            def _(i):
                n = pl.ds(pl.multiple_of(i * 1024, 1024), 1024)
                part[s, n] = (nt(dg[s, :], wg[n, :]) + nt(du[s, :], wu[n, :])).astype(BF16)

        scatter = ScatterTensor(part, bufs, *scatter_sems)
        scatter.run(d_input)
        scatter.step(0)

        def down_grad(i):
            m = pl.ds(i * 512, 512)

            @tiles(2048, 512)
            def _(n):
                wd[m, n] = tn(inner[:, m], dd[:, n]).astype(BF16)

        def gate_grad(first):
            @pl.loop(first, first + 2)
            def _(i):
                m = pl.ds(pl.multiple_of(i * 512, 512), 512)

                @tiles(1024, 512)
                def _(n):
                    wg[m, n] = tn(x[:, m], dg[:, n]).astype(BF16)

        down_grad(0)
        down_grad(1)
        scatter.step(1)
        tell(1)

        def by_rows(ref):
            return lambda n: ref.at[pl.ds(n * 128, 128)]

        def by_columns(ref):
            return lambda n: ref.at[:, pl.ds(n * 128, 128)]

        small_slots = [by_rows(gate_factor.at[:, pl.ds(256 * i, 256)]) for i in range(3)]
        small_slots.append(
            lambda n: gate_factor.at[
                pl.ds(n // 2 * 256, 256), pl.ds(768 + n % 2 * 128, 128)
            ]
        )
        slots = small_slots + [by_rows(silu), by_rows(inner), by_columns(gate_factor)]
        wholes = (wq, wk, silu, wo, wg, wu, wd)
        scatter_kinds = kinds[:2] + ("folded",) + kinds[3:]
        items = [ScatterDp(wholes[i], scatter_kinds[i], slots[i], *dp_bufs[i]) for i in range(7)]
        qk, value_item, out_item, gate_item, up_item, down_item = items[:2], *items[2:]
        pl.semaphore_wait(ready.at[0], 1)
        down_item.start()
        scatter.step(2)
        gate_grad(0)
        scatter.step(3)
        gate_grad(2)
        gate_item.start()
        load_heads.start()
        down_item.along_x()
        tell(2)
        scatter.finish(total)

        @tiles(128, 16)
        def _(r):
            grad = residual[r, :] + total[r, :]
            residual[r, :] = grad
            b = branch[r, :]
            scale = lax.rsqrt(jnp.mean(b * b, 1, keepdims=True) + EPS)
            attn_part[...] += jnp.sum(grad * b * scale, 0, keepdims=True)
            weighted = attn_gain[...] * grad
            mean = jnp.mean(b * weighted, 1, keepdims=True)
            own_d[r, :] = (scale * weighted - b * (scale * scale * scale * mean)).astype(BF16)

        gather = GatherTensor(dd, *gather_sems, 768)
        gather.start()


        @tiles(2048, 512)
        def _(m):
            @tiles(1024, 512)
            def _(n):
                wu[m, n] = tn(x[:, m], du[:, n]).astype(BF16)

        reload.start()
        load_raw.start()
        gate_item.along_x()
        pl.semaphore_wait(ready.at[1], 1)
        up_item.start()
        dk[...] = jnp.zeros_like(dk)
        dv[...] = jnp.zeros_like(dv)

        def attend_back(wanted):
            for i in range(4):

                @pl.when(wanted == i)
                def _():
                    @pl.loop(0, 2)
                    def _(h):
                        cols = pl.ds(pl.multiple_of(h * 128, 128), 128)
                        low = i * 256
                        block = slice(low, low + 256)
                        q, d = q_rot[block, cols], do[block, cols]
                        peak = jnp.where(h == 0, stats[block, 0:1], stats[block, 64:65])
                        k1, v1 = k_rot[block, cols], v_low[block, cols]
                        p1 = jnp.exp(diagonal_mask(nt(q, k1), low, length) - peak)
                        dp1 = nt(d, v1)
                        delta = jnp.sum(p1 * dp1, 1, keepdims=True)
                        if i:
                            k0, v0 = k_rot[0:low, cols], v_low[0:low, cols]
                            p0 = jnp.exp(nt(q, k0) - peak)
                            dp0 = nt(d, v0)
                            delta += jnp.sum(p0 * dp0, 1, keepdims=True)
                        ds1 = (p1 * (dp1 - delta)).astype(BF16)
                        dq_block = nn(ds1, k1)
                        dk[block, cols] += tn(ds1, q)
                        dv[block, cols] += tn(p1.astype(BF16), d)
                        if i:
                            ds0 = (p0 * (dp0 - delta)).astype(BF16)
                            dq_block += nn(ds0, k0)
                            dk[0:low, cols] += tn(ds0, q)
                            dv[0:low, cols] += tn(p0.astype(BF16), d)
                        dq[block, cols] = dq_block

        def d_mixed(slot):
            s = pl.ds(pl.multiple_of(slot * 128, 128), 128)
            do[s, :] = nt(dd[s, :], wo[...]).astype(BF16)

        def beside(stage):
            if stage == 0:
                down_item.forward()
                load_heads.wait()
            elif stage == 1:
                gate_item.forward()
                up_item.along_x()
            else:
                down_item.along_y()

        gather.run(d_mixed, beside, attend_back)
        load_raw.wait()

        q_line[...] = jnp.zeros_like(q_line)
        k_line[...] = jnp.zeros_like(k_line)
        sums[me] = jnp.zeros((8, 256), F32)

        @tiles(1024, 256)
        def _(r):
            cos, sin = cos_sin(table[r, :])
            for source, rawer, gain, s, factor, line in (
                (dq, q_raw, q_gain, 128, SCALE, q_line),
                (dk, k_raw, k_gain, 192, 1.0, k_line),
            ):
                scale = stats[r, s : s + 1]
                for h in (0, 128):
                    v = source[r, h : h + 128] * factor
                    v = v * cos - pltpu.roll(v, 64, 1) * sin
                    w = v * rawer[r, h : h + 128].astype(F32)
                    line[:, h : h + 128] += jnp.sum(w * scale, 0, keepdims=True)
                    source[r, h : h + 128] = v * gain[:, h : h + 128]
            note_sums(
                sums.at[me],
                r,
                dq[r, :] * q_raw[r, :].astype(F32),
                dk[r, :] * k_raw[r, :].astype(F32),
            )
            dvr[r, :] = dv[r, :].astype(BF16)

        exchange = Exchange(sums, *sum_sems)
        exchange.start()
        reload.wait()
        row = lax.broadcasted_iota(jnp.int32, (8, 1024), 0)
        column = lax.broadcasted_iota(jnp.int32, (8, 1024), 1)
        message = jnp.zeros((8, 1024), F32)
        for k, line in enumerate((attn_part, attn_part, mlp_part, mlp_part)):
            line = line[:, 1024 * (k % 2) : 1024 * (k % 2) + 1024]
            message = jnp.where(row == 4 + k, line, message)
        for first_row, line in ((0, q_line), (2, k_line)):
            line = jnp.concatenate([line[...]] * 4, 1)
            message += jnp.where((row == first_row + yl) & (column // 256 == z), line, 0.0)
        gain_slots[me] = message
        total_gain = SumAll(gain_slots, gain_hold, gain_boxes, *isems)

        @pl.loop(0, 4)
        def _(i):
            m = pl.ds(pl.multiple_of(i * 512, 512), 512)
            r = pl.ds(pl.multiple_of(lax.rem(i, 2) * 512, 512), 512)
            columns = pl.ds(pl.multiple_of(i // 2 * 256, 256), 256)
            silu[r, columns] = tn(x[:, m], dvr[...]).astype(BF16)

        pl.semaphore_wait(ready.at[2], 1)
        value_item.start()
        exchange.finish()
        total_gain.start()
        gate_item.along_y()
        spread(dv, exchange.sum() * (1.0 / 2048))

        @tiles(1024, 256)
        def _(r):
            for source, rawer, s, target in ((dq, q_raw, 0, dqr), (dk, k_raw, 128, dkr)):
                scale = stats[r, 128 + s // 2 : 129 + s // 2]
                factor = scale * scale * scale * dv[r, s : s + 128]
                for h in (0, 128):
                    target[r, h : h + 128] = (
                        scale * source[r, h : h + 128]
                        - rawer[r, h : h + 128].astype(F32) * factor
                    ).astype(BF16)

        def d_tokens(first_row):
            s = pl.ds(pl.multiple_of(first_row, 256), 256)

            @pl.loop(0, 2)
            def _(i):
                n = pl.ds(pl.multiple_of(i * 1024, 1024), 1024)
                terms = nt(dqr[s, :], wq[n, :]) + nt(dkr[s, :], wk[n, :]) + nt(dvr[s, :], wv[n, :])
                part[s, n] = terms.astype(BF16)

        scatter = ScatterTensor(part, bufs, *scatter_sems, 640)
        scatter.run(d_tokens)
        up_item.forward()
        total_gain.core()
        scatter.step(0)
        value_item.along_x()

        @tiles(2048, 512)
        def _(m):
            xt = x[:, m].T
            wq[m, :] = nn(xt, dqr[...]).astype(BF16)
            wk[m, :] = nn(xt, dkr[...]).astype(BF16)

        for item in qk:
            item.start()

        @tiles(2048, 512)
        def _(n):
            wo[:, n] = tn(mixed[...], dd[:, n]).astype(BF16)

        out_item.start()
        total_gain.along_x()
        scatter.step(2)
        value_item.forward()
        for item in qk:
            item.along_x()
        scatter.step(1)
        out_item.along_x()
        up_item.along_y()
        total_gain.along_y()
        scatter.step(3)
        for item in qk:
            item.forward()
        out_item.forward()
        value_item.along_y()
        stores = []

        def store(item, source, target):
            item.finish(source)
            stores.append(pltpu.make_async_copy(source, target, lsem.at[len(stores)]))
            stores[-1].start()

        store(down_item, dv.at[:, pl.ds(0, 128)], o6)
        store(gate_item, gate_out, o4)
        for item in qk:
            item.along_y()
        out_item.along_y()
        scatter.finish(total)

        @tiles(128, 16)
        def _(r):
            total[r, :] += residual[r, :]

        stores.append(pltpu.make_async_copy(total, input_grad, lsem.at[len(stores)]))
        stores[-1].start()
        store(up_item, up_out, o5)
        total_gain.finish(gain_slots.at[0])
        for i, out in enumerate((q_sum, k_sum, attn_sum, mlp_sum)):
            out[:, 0:1024] = gain_slots[0, 2 * i : 2 * i + 1, :]
            out[:, 1024:2048] = gain_slots[0, 2 * i + 1 : 2 * i + 2, :]
        store(value_item, dk.at[pl.ds(256, 128)], o2)
        for i, out in enumerate((o0, o1)):
            store(qk[i], dk.at[pl.ds(128 * i, 128)], out)
        store(out_item, dv.at[pl.ds(0, 256), pl.ds(128, 128)], o3)
        for copy in stores:
            copy.wait()

    S = jax.ShapeDtypeStruct
    W = pltpu.VMEM
    scratch = [W((1024, 2048), BF16)] * 2 + [W((2048, 1024), BF16)] * 2 + [W((1024, 2048), BF16)]
    scratch += [W((1024, 1024), BF16)] * 5 + [W((1024, 2048), BF16)]
    scratch += [W((128, 2048), F32)] + [W((1, 2048), F32)] * 2 + [W((1, 256), F32)] * 2
    scratch += [W((2048, 256), BF16)] * 3 + [W((256, 2048), BF16)]
    scratch += [W((1024, 256), F32)] + [W((128, 2048), F32)] * 2
    scratch += [W((128, 1024), F32)] * 2 + [W((1024, 256), BF16)]
    scratch += [W((1024, 256), F32)] * 3
    scratch += [W((8, 8, 256), F32), W((8, 8, 1024), F32)] + [W((3, 8, 1024), F32), W((5, 8, 1024), F32)]
    scratch += ScatterTensor.scratch(640, CUT)
    for b in blocks:
        scratch += ScatterDp.scratch(b)
    scratch += [DMA, DMA((23,)), DMA, DMA((21,)), DMA, DMA((7,)), DMA((6,)), DMA((12,))]
    scratch += [DMA((7,)), DMA((7, 14))]
    scratch += [DMA((8,)), DMA((4,)), pltpu.SemaphoreType.REGULAR((3,))]
    return pl.pallas_call(
        layer_step,
        out_shape=[S((128, 2048), BF16), S((128, 2048), F32)]
        + [S(b, F32) for b in blocks]
        + [S((1, 2048), F32)] * 4
        + [S((1024, 2048), BF16), S((1024, 1024), BF16), S((1024, 512), BF16)],
        in_specs=[SMEM] + [VM] * 6 + [ANY] * 8,
        out_specs=[ANY] * 9 + [VM] * 4 + [ANY] * 3,
        scratch_shapes=scratch,
        compiler_params=params(1),
        name="layer_step",
    )(lengths, cotangent, *gains, table, tokens, *weights)[:13]


def hand_over(*arrays):
    n = len(arrays)

    def hand_over_step(*refs):
        held, (lsem, ssem) = refs[2 * n : 3 * n], refs[3 * n :]
        loads = [pltpu.make_async_copy(refs[i], held[i], lsem.at[i]) for i in range(n)]
        stores = [pltpu.make_async_copy(held[i], refs[n + i], ssem.at[i]) for i in range(n)]
        for copy in loads:
            copy.start()
        for load, store in zip(loads, stores):
            load.wait()
            store.start()
        for copy in stores:
            copy.wait()

    return pl.pallas_call(
        hand_over_step,
        out_shape=[jax.ShapeDtypeStruct(a.shape, a.dtype) for a in arrays],
        in_specs=[ANY] * n,
        out_specs=[ANY] * n,
        scratch_shapes=[pltpu.VMEM(a.shape, a.dtype) for a in arrays] + [DMA((n,))] * 2,
        compiler_params=pltpu.CompilerParams(vmem_limit_bytes=63 << 20),
        name="hand_over_step",
    )(*arrays)


def local(
    tokens, lengths, w_query, w_key, w_value, w_out, w_gate, w_up, w_down,
    q_gain, k_gain, attn_gain, mlp_gain, cotangent,
):
    weights = (w_query, w_key, w_value, w_out, w_gate, w_up, w_down)
    gains = (q_gain[None], k_gain[None], attn_gain[None], mlp_gain[None])
    results = whole_layer(tokens[0], lengths, cotangent[0], gains, weights, rope_table())
    act, input_grad, *grads = hand_over(*results)
    return (act[None], input_grad[None], *grads[:7], *(g.reshape(2048) for g in grads[7:]))


def solution(mesh):
    return jax.shard_map(
        local,
        mesh=mesh,
        in_specs=(
            P("dp", "tensor", None),
            P("dp"),
            P("dp", "tensor"),
            P("dp", "tensor"),
            P("dp", "tensor"),
            P("tensor", "dp"),
            P("dp", "tensor"),
            P("dp", "tensor"),
            P("tensor", "dp"),
            P(),
            P(),
            P(),
            P(),
            P("dp", "tensor", None),
        ),
        out_specs=(
            P("dp", "tensor", None),
            P("dp", "tensor", None),
            P("dp", "tensor"),
            P("dp", "tensor"),
            P("dp", "tensor"),
            P("tensor", "dp"),
            P("dp", "tensor"),
            P("dp", "tensor"),
            P("tensor", "dp"),
            P(),
            P(),
            P(),
            P(),
        ),
        check_vma=False,
    )
```

```python
import jax
import jax.numpy as jnp
import numpy as np
from jax import lax
from jax.experimental import pallas as pl
from jax.experimental.pallas import tpu as pltpu
from jax.sharding import PartitionSpec as P

HEAD_DIM = 128
EPS = 1e-06
THETA = 500000.0
MESH = pl.DeviceIdType.MESH
BF16 = jnp.bfloat16
F32 = jnp.float32
ANY = pl.BlockSpec(memory_space=pl.ANY)
VM = pl.BlockSpec(memory_space=pltpu.VMEM)
DMA = pltpu.SemaphoreType.DMA
CUT = 896
WIDTH = 2048


def place():
    d = lax.axis_index("dp")
    t = lax.axis_index("tensor")
    return d // 8, lax.rem(d // 2, 4), lax.rem(d, 2), t // 4, lax.rem(t, 4)


def other(dyh=0, dx=0, dc=0, dyl=0, dz=0):
    yh, x, c, yl, z = place()
    return (
        lax.rem(yh + dyh, 2) * 8 + lax.rem(x + dx, 4) * 2 + lax.rem(c + dc, 2),
        lax.rem(yl + dyl, 2) * 4 + lax.rem(z + dz, 4),
    )


TENSOR_PEERS = (dict(dz=1), dict(dz=3), dict(dyl=1))
DP_PEERS = (dict(dx=1), dict(dx=2), dict(dx=3), dict(dyh=1), dict(dc=1))
SMEM = pl.BlockSpec(memory_space=pltpu.SMEM)


def greet(peers):
    barrier = pltpu.get_barrier_semaphore()
    for peer in peers:
        pl.semaphore_signal(barrier, 1, device_id=other(**peer), device_id_type=MESH)
    pl.semaphore_wait(barrier, len(peers))


def remote(src, dst, sems, index, peer):
    ssem, rsem = sems
    return pltpu.make_async_remote_copy(
        src_ref=src,
        dst_ref=dst,
        send_sem=ssem,
        recv_sem=rsem.at[index],
        device_id=other(**peer),
        device_id_type=MESH,
    )


def all_of(bytes_of, sem):
    pltpu.make_async_copy(bytes_of, bytes_of, sem).wait()


def rows(ref, slot):
    return ref.at[pl.ds(pl.multiple_of(slot * 128, 128), 128)]


def halves(ref):
    half = ref.shape[0] // 2
    return ref.at[pl.ds(0, half)], ref.at[pl.ds(half, half)]


def add_into(out, *terms):
    step = min(out.shape[0], 16 if out.shape[1] > 1024 else 64 if out.shape[1] > 128 else 128)

    @pl.loop(0, out.shape[0] // step)
    def _(i):
        r = pl.ds(pl.multiple_of(i * step, step), step)
        if len(terms) == 2 and out.dtype == BF16:
            out[r, :] = terms[0][r, :] + terms[1][r, :]
        else:
            total = terms[0][r, :].astype(F32)
            for term in terms[1:]:
                total += term[r, :].astype(F32)
            out[r, :] = total.astype(out.dtype)


class RingGather:
    COPIES = 6

    def __init__(self, block, axis, sems, base, source=None):
        up, down = {axis: 1}, {axis: 3}
        src = halves(block(0) if source is None else source)
        own, behind, ahead = halves(block(0)), halves(block(3)), halves(block(1))
        self.copies = [
            remote(src[0], own[0], sems, base, up),
            remote(src[1], own[1], sems, base + 1, down),
            remote(src[1], own[1], sems, base + 2, up),
            remote(src[0], own[0], sems, base + 3, down),
            remote(behind[0], behind[0], sems, base + 4, up),
            remote(ahead[1], ahead[1], sems, base + 5, down),
        ]

    def start(self):
        for copy in self.copies[:4]:
            copy.start()

    def forward(self):
        for i in range(2):
            self.copies[i].wait_recv()
            self.copies[4 + i].start()

    def behind(self):
        self.copies[2].wait_recv()

    def ahead(self):
        self.copies[3].wait_recv()

    def far(self):
        for copy in self.copies[4:]:
            copy.wait_recv()


class RingReduce:
    COPIES = 6

    @staticmethod
    def scratch(n, m):
        return [pltpu.VMEM((2, n // 2, m), BF16), pltpu.VMEM((2, n, m), BF16)]

    def __init__(self, block, axis, part, full, sems, base):
        up, down = {axis: 1}, {axis: 3}
        one, two, three = halves(block(1)), halves(block(2)), halves(block(3))
        from_behind, from_ahead = halves(full.at[0]), halves(full.at[1])
        self.adds = ((one[0], part.at[0]), (three[1], part.at[1]))
        self.terms = (block(0), full.at[0], full.at[1])
        self.full, self.full_sem = full, sems[1].at[base + 2]
        self.copies = [
            remote(two[0], part.at[0], sems, base, up),
            remote(two[1], part.at[1], sems, base + 1, down),
            remote(one[1], from_behind[1], sems, base + 2, up),
            remote(three[0], from_ahead[0], sems, base + 2, down),
            remote(one[0], from_behind[0], sems, base + 2, up),
            remote(three[1], from_ahead[1], sems, base + 2, down),
        ]

    def start(self):
        for copy in self.copies[:4]:
            copy.start()

    def forward(self):
        for i in range(2):
            self.copies[i].wait_recv()
            add_into(self.adds[i][0], *self.adds[i])
            self.copies[4 + i].start()

    def arrive(self):
        all_of(self.full, self.full_sem)


class GatherTensor:
    COPIES = 21

    def __init__(self, buf, ssem, rsem, cut=CUT):
        yh, x, c, yl, z = place()
        self.yl, self.z = yl, z
        self.sent, self.ssem = buf.at[pl.ds(0, 896)], ssem
        sems = (ssem, rsem)
        slot = lambda k, i: rows(buf, lax.rem(yl + k, 2) * 4 + lax.rem(z + i, 4))
        low = lambda ref: ref.at[:, pl.ds(0, cut)]
        high = lambda ref: ref.at[:, pl.ds(cut, WIDTH - cut)]
        self.ring = RingGather(lambda i: slot(0, i), "dz", sems, 0)
        self.pair_ring = RingGather(lambda i: high(slot(1, i)), "dz", sems, 6)
        own = slot(0, 0)
        pair = dict(dyl=1)
        self.high = remote(high(own), high(own), sems, 12, pair)
        self.low = []
        for n, i in enumerate((0, 3, 1, 2)):
            for half in halves(low(slot(0, i))):
                self.low.append(remote(half, half, sems, 13 + len(self.low), pair))

    def start(self):
        self.high.start()
        self.ring.start()
        self.low[0].start()
        self.low[1].start()

    def run(self, process, spare=None, by_block=None, early=None, first=3):
        yl, z = self.yl, self.z

        @pl.loop(0, 2)
        def _(k):
            @pl.when(k == 1)
            def _():
                self.ring.forward()
                self.low[2].start()
                self.low[5].start()
                if early is not None:
                    early()
                self.high.wait_recv()
                self.pair_ring.start()
                self.ring.behind()
                self.low[3].start()
                self.ring.ahead()
                self.low[4].start()
                self.low[0].wait_recv()
                self.low[1].wait_recv()

            process(lax.rem(yl + k, 2) * 4 + z)

        if spare is not None:
            spare(0)

        @pl.loop(0, 6 if by_block is None else 7)
        def _(j):
            if spare is not None:
                for stage, at in ((1, 3), (2, 5)):

                    @pl.when(j == at)
                    def _():
                        spare(stage)

            if by_block is not None:
                last = j // 6
                rest = 2 - 2 * yl + last * (1 - z // 2) + (1 - last) * (z // 2)

                @pl.when((j >= 5) | (j == first))
                def _():
                    @pl.loop(0, 3)
                    def _(t):
                        third = t // 2

                        @pl.when(((t < 2) & (j == first)) | ((t == 2) & (j >= 5)))
                        def _():
                            by_block((1 - third) * (2 * yl + t) + third * rest)

            @pl.when(j == 2)
            def _():
                self.ring.far()
                self.low[6].start()
                self.low[7].start()
                self.pair_ring.forward()

            @pl.when(j == 3)
            def _():
                self.pair_ring.behind()
                self.low[2].wait_recv()
                self.low[3].wait_recv()

            @pl.when(j == 4)
            def _():
                self.pair_ring.ahead()
                self.low[4].wait_recv()
                self.low[5].wait_recv()

            @pl.when(j == 5)
            def _():
                self.pair_ring.far()
                self.low[6].wait_recv()
                self.low[7].wait_recv()

            i = lax.rem(j, 3)
            step = (3 * i * i - 7 * i + 6) // 2

            @pl.when(j < 6)
            def _():
                process(lax.rem(yl + j // 3, 2) * 4 + lax.rem(z + step, 4))

        all_of(self.sent, self.ssem)


class ScatterTensor:
    COPIES = 23

    @staticmethod
    def scratch(least, most):
        return (
            [pltpu.VMEM((4, 128, most), BF16), pltpu.VMEM((128, WIDTH - least), BF16)]
            + RingReduce.scratch(128, most)
            + RingReduce.scratch(128, WIDTH - least) * 2
        )

    def __init__(self, part, bufs, ssem, rsem, cut=CUT):
        yh, x, c, yl, z = place()
        self.z = z
        narrow = lambda ref, n: ref.at[:, :, pl.ds(0, n)]
        wide = WIDTH - cut
        bufs = [
            narrow(bufs[0], cut),
            bufs[1].at[:, pl.ds(0, wide)],
            *(narrow(ref, cut) for ref in bufs[2:4]),
            *(narrow(ref, wide) for ref in bufs[4:]),
        ]
        self.yl = yl
        self.from_pair, self.last = bufs[0], bufs[1]
        self.sent, self.ssem = part.at[pl.ds(0, 896)], ssem
        sems = (ssem, rsem)
        slot = lambda k, i: rows(part, lax.rem(yl + k, 2) * 4 + lax.rem(z + i, 4))
        low = lambda k, i: slot(k, i).at[:, pl.ds(0, cut)]
        high = lambda k, i: slot(k, i).at[:, pl.ds(cut, wide)]
        self.cut = cut
        pair = dict(dyl=1)
        self.low = lambda i: low(0, i)
        self.low_ring = RingReduce(lambda i: low(0, i), "dz", bufs[2], bufs[3], sems, 0)
        self.pair_ring = RingReduce(lambda i: high(1, i), "dz", bufs[4], bufs[5], sems, 3)
        self.own_ring = RingReduce(lambda i: high(0, i), "dz", bufs[6], bufs[7], sems, 6)
        self.first = lambda i: remote(low(1, i), bufs[0].at[i], sems, 9 + i, pair)
        self.second = remote(high(1, 0), bufs[1], sems, 13, pair)

    def run(self, process):
        yl, z = self.yl, self.z

        @pl.loop(0, 4)
        def _(k):
            half = lax.rem(yl + 1 + k // 2, 2)
            process(half * 512 + lax.rem((z + 2) // 2 + k, 2) * 256)
            beside = 3 - 2 * lax.rem(z, 2)

            @pl.when(k == 0)
            def _():
                self.first(2).start()
                self.pair_ring.copies[0].start()
                self.pair_ring.copies[1].start()
                self.first(beside).start()

            @pl.when(k == 1)
            def _():
                self.first(4 - beside).start()
                self.pair_ring.copies[2].start()
                self.pair_ring.copies[3].start()
                self.first(0).start()

    def add_first(self, i):
        self.first(i).wait_recv()
        add_into(self.low(i), self.low(i), self.from_pair.at[i])

    def add_low(self, i):
        self.add_first(i)
        for k in (1, 3):

            @pl.when(i == k)
            def _():
                self.low_ring.copies[2 + k // 3].start()

    def step(self, n):
        beside = 3 - 2 * lax.rem(self.z, 2)
        if n == 0:
            self.pair_ring.forward()
            self.own_ring.start()
            self.add_first(2)
            self.low_ring.copies[0].start()
            self.low_ring.copies[1].start()
        if n == 1:
            self.own_ring.forward()
            self.add_low(beside)
        if n == 2:
            self.pair_ring.arrive()
            add_into(self.pair_ring.terms[0], *self.pair_ring.terms)
            self.second.start()
            self.add_low(4 - beside)
        if n == 3:
            self.low_ring.forward()
            self.add_first(0)

    def finish(self, out):
        self.own_ring.arrive()
        self.second.wait_recv()
        add_into(out.at[:, pl.ds(self.cut, WIDTH - self.cut)], *self.own_ring.terms, self.last)
        self.low_ring.arrive()
        add_into(out.at[:, pl.ds(0, self.cut)], *self.low_ring.terms)
        all_of(self.sent, self.ssem)


def block_of(ref, kind, slot):
    if kind == "row":
        size = ref.shape[0] // 16
        return ref.at[pl.ds(pl.multiple_of(slot * size, size), size)]
    if kind == "folded":
        return ref.at[
            pl.ds(pl.multiple_of(lax.rem(slot, 8) * 128, 128), 128),
            pl.ds(pl.multiple_of(slot // 8 * 256, 256), 256),
        ]
    size = ref.shape[1] // 16
    return ref.at[:, pl.ds(pl.multiple_of(slot * size, size), size)]


def some_of(ref, kind, count):
    if kind == "row":
        return ref.at[pl.ds(0, ref.shape[0] // 16 * count)]
    if kind == "folded":
        return ref.at[pl.ds(0, 64 * count), pl.ds(0, 512)]
    return ref.at[:, pl.ds(0, ref.shape[1] // 16 * count)]


class GatherDp:
    COPIES = 21

    def __init__(self, shard, out, kind, ssem, rsem, lsem):
        yh, x, c, yl, z = place()
        sems = (ssem, rsem)
        block = lambda k, i: block_of(
            out, kind, lax.rem(yh + k, 2) * 8 + lax.rem(x + i, 4) * 2 + c
        )
        self.sent, self.ssem = some_of(out, kind, 15), ssem
        self.local = pltpu.make_async_copy(shard, block(0, 0), lsem)
        self.ring = RingGather(lambda i: block(0, i), "dx", sems, 0, shard)
        self.far_ring = RingGather(lambda i: block(1, i), "dx", sems, 6)
        self.own_y = remote(shard, block(0, 0), sems, 12, dict(dyh=1))
        core = dict(dc=1)
        self.core = [remote(shard, block(0, 0), sems, 13, core)]
        for n in range(1, 8):
            ref = block(n // 4, n % 4)
            self.core.append(remote(ref, ref, sems, 13, core))
        self.shared, self.shared_sem = some_of(out, kind, 8), rsem.at[13]

    def start(self):
        self.ring.start()
        self.core[0].start()
        self.local.start()

    def forward(self):
        self.ring.forward()

    def forward_y(self):
        self.own_y.wait_recv()
        self.far_ring.start()
        self.core[4].start()

    def share(self):
        self.ring.behind()
        self.core[3].start()
        self.ring.ahead()
        self.core[1].start()
        self.ring.far()
        self.core[2].start()

    def forward_far(self):
        self.far_ring.forward()

    def share_far(self):
        self.far_ring.behind()
        self.core[7].start()
        self.far_ring.ahead()
        self.core[5].start()
        self.far_ring.far()
        self.core[6].start()

    def finish(self):
        all_of(self.shared, self.shared_sem)
        self.local.wait()
        all_of(self.sent, self.ssem)


class ScatterDp:
    COPIES = 21

    @staticmethod
    def scratch(block):
        return (
            [pltpu.VMEM(block, BF16)]
            + RingReduce.scratch(*block) * 2
            + [DMA, DMA((8,))]
        )

    def __init__(self, part, kind, from_core, from_y, h0, f0, h1, f1, ssem, rsem):
        yh, x, c, yl, z = place()
        sems = (ssem, rsem)
        self.from_core, self.from_y = from_core, from_y
        self.sent, self.ssem = some_of(part, kind, 15), ssem
        block = lambda k, i, d: block_of(
            part, kind, lax.rem(yh + k, 2) * 8 + lax.rem(x + i, 4) * 2 + d
        )
        self.block = lambda k, i: block(k, i, c)
        self.core = [
            remote(block(n // 4, n % 4, 1 - c), from_core(n), sems, 0, dict(dc=1))
            for n in range(8)
        ]
        self.ring = RingReduce(lambda i: block(0, i, c), "dx", h0, f0, sems, 1)
        self.far_ring = RingReduce(lambda i: block(1, i, c), "dx", h1, f1, sems, 4)
        self.last = remote(block(1, 0, c), from_y, sems, 7, dict(dyh=1))
        self.shared, self.shared_sem = some_of(part, kind, 8), rsem.at[0]

    def start(self):
        for n in (6, 5, 7, 4, 2, 1, 3, 0):
            self.core[n].start()

    def add_core(self, n):
        ref = self.block(n // 4, n % 4)
        add_into(ref, ref, self.from_core(n))

    def along_x(self):
        all_of(self.shared, self.shared_sem)
        for n in (6, 5, 7):
            self.add_core(n)
        self.far_ring.start()
        for n in (2, 1, 3):
            self.add_core(n)
        self.ring.start()
        for n in (4, 0):
            self.add_core(n)

    def forward(self):
        self.far_ring.forward()
        self.ring.forward()

    def along_y(self):
        self.far_ring.arrive()
        add_into(self.far_ring.terms[0], *self.far_ring.terms)
        self.last.start()

    def finish(self, out):
        self.ring.arrive()
        self.last.wait_recv()
        add_into(out, *self.ring.terms, self.from_y)
        all_of(self.sent, self.ssem)


def params(cid):
    return pltpu.CompilerParams(
        collective_id=cid, has_side_effects=True, vmem_limit_bytes=65400 << 10
    )


def nn(a, b):
    return jnp.dot(a, b, preferred_element_type=F32)


def nt(a, b):
    return lax.dot_general(a, b, (((1,), (1,)), ((), ())), preferred_element_type=F32)


def tn(a, b):
    return lax.dot_general(a, b, (((0,), (0,)), ((), ())), preferred_element_type=F32)


def tiles(count, size):
    def run(body):
        @pl.loop(0, count // size)
        def _(i):
            body(pl.ds(pl.multiple_of(i * size, size), size))

    return run


def rope_table():
    frequency = THETA ** (-(np.arange(64, dtype=np.float32) * np.float32(2.0) / np.float32(HEAD_DIM)))
    angles = np.arange(1024, dtype=np.float32)[:, None] * frequency.astype(np.float32)[None, :]
    cosine, sine = np.cos(angles), np.sin(angles)
    return np.concatenate([cosine, sine], 1).astype(np.float32)


def cos_sin(table):
    turned = pltpu.roll(table, 64, 1)
    first = lax.broadcasted_iota(jnp.int32, table.shape, 1) < 64
    return jnp.where(first, table, turned), jnp.where(first, -turned, table)


class Exchange:
    PEERS = tuple(dict(dz=a, dyl=b) for b in range(2) for a in range(4) if a or b)

    def __init__(self, buf, ssem, rsem):
        yh, x, c, yl, z = place()
        self.buf, self.ssem = buf, ssem
        self.mine = buf.at[yl * 4 + z]
        self.copies = [
            remote(self.mine, self.mine, (ssem, rsem), i, peer)
            for i, peer in enumerate(self.PEERS)
        ]

    def start(self):
        for copy in self.copies:
            copy.start()

    def finish(self):
        for copy in self.copies:
            copy.wait_recv()
        all_of(self.buf.at[pl.ds(0, 7)], self.ssem)

    def sum(self):
        total = self.buf[0]
        for i in range(1, 8):
            total += self.buf[i]
        return total


def row_sums(values):
    return nt(jnp.ones((8, values.shape[1]), F32), values)


def spread(out, pair):
    row = lax.broadcasted_iota(jnp.int32, (8, 256), 0)
    column = lax.broadcasted_iota(jnp.int32, (8, 256), 1)
    for i in range(4):
        pick = jnp.where(row == column // 128 * 4 + i, 1.0, 0.0)
        out[pl.ds(256 * i, 256), :] = lax.dot_general(
            pair,
            pick,
            (((0,), (0,)), ((), ())),
            precision=lax.Precision.HIGHEST,
            preferred_element_type=F32,
        )


def note_sums(out, r, a, b):
    row = lax.broadcasted_iota(jnp.int32, (8, 256), 0)
    sums = jnp.where(row < 4, row_sums(a), row_sums(b))
    out[...] = jnp.where(lax.rem(row, 4) == r.start // 256, sums, out[...])


ALL_PEERS = Exchange.PEERS + DP_PEERS
SCALE = HEAD_DIM**-0.5


def diagonal_mask(scores, first, length):
    row = lax.broadcasted_iota(jnp.int32, scores.shape, 0)
    column = lax.broadcasted_iota(jnp.int32, scores.shape, 1)
    return jnp.where((column <= row) & (column + first < length), scores, -1e30)


class SumAll:
    def __init__(self, slots, hold, boxes, ssem, rsem):
        self.exchange = Exchange(slots, ssem.at[5], rsem)
        self.hold, self.boxes = hold, boxes
        self.copies = []
        for i, peer in enumerate(DP_PEERS):
            k = (1, 1, 1, 2, 0)[i]
            self.copies.append(remote(hold.at[k], boxes.at[i], (ssem.at[i], rsem), 7 + i, peer))

    def start(self):
        self.exchange.start()

    def core(self):
        self.exchange.finish()
        self.hold[0] = self.exchange.sum()
        self.copies[4].start()

    def along_x(self):
        self.copies[4].wait()
        self.hold[1] = self.hold[0] + self.boxes[4]
        for copy in self.copies[:3]:
            copy.start()

    def along_y(self):
        for copy in self.copies[:3]:
            copy.wait()
        self.hold[2] = self.hold[1] + self.boxes[0] + self.boxes[1] + self.boxes[2]
        self.copies[3].start()

    def finish(self, out):
        self.copies[3].wait()
        out[...] = self.hold[2] + self.boxes[3]


def whole_layer(tokens, lengths, cotangent, gains, weights, table):
    kinds = ("row", "row", "row", "col", "row", "row", "col")
    blocks = ((128, 256),) * 3 + ((256, 128), (128, 1024), (128, 1024), (1024, 128))

    def layer_step(
        lengths, q_gain_all, k_gain_all, attn_gain, mlp_gain, tokens, cotangent_in, table_in, i0, i1, i2, i3, i4, i5, i6,
        act, input_grad, o0, o1, o2, o3, o4, o5, o6,
        q_sum, k_sum, attn_sum, mlp_sum, x_kept, heads_kept, raw_kept,
        x, dd, wg, wu, wd, gate_factor, silu, inner, dg, du, part, residual, attn_part, mlp_part, q_line, k_line,
        wq, wk, wv, wo, stats, branch, cotangent, table, gain_lines, total, gate_out, up_out, do, dq, dk, dv, sums, gain_slots, gain_hold, gain_boxes,
        *rest,
    ):
        bufs, rest = rest[:8], rest[8:]
        dp_bufs, rest = [rest[7 * i : 7 * i + 7] for i in range(7)], rest[49:]
        scatter_sems, gather_sems, sum_sems, isems, wsems = [
            rest[2 * i : 2 * i + 2] for i in range(5)
        ]
        lsem, msem, ready = rest[10:]
        yh, xx, c, yl, z = place()
        me = yl * 4 + z
        length = lengths[0]
        own_columns = pl.ds(pl.multiple_of(me * 256, 256), 256)
        q_gain, k_gain = q_gain_all[:, own_columns], k_gain_all[:, own_columns]
        q_rot, k_rot, v_low, mixed = (dg.at[:, pl.ds(256 * i, 256)] for i in range(4))
        q_raw, k_raw, dvr = (du.at[:, pl.ds(256 * i, 256)] for i in range(3))
        dqr, dkr = q_raw, k_raw
        raw = du.at[:, pl.ds(0, 512)]
        load_heads = pltpu.make_async_copy(heads_kept, dg, msem.at[0])
        load_raw = pltpu.make_async_copy(raw_kept, raw, msem.at[2])
        reload = pltpu.make_async_copy(x_kept, x, msem.at[1])
        keep_x = pltpu.make_async_copy(dd, x_kept, msem.at[1])
        keep_heads = pltpu.make_async_copy(dg, heads_kept, msem.at[0])
        keep_raw = pltpu.make_async_copy(raw, raw_kept, msem.at[2])
        first = pltpu.make_async_copy(tokens, rows(dd, me), msem.at[3])
        first.start()
        load_table = pltpu.make_async_copy(table_in, table, msem.at[4])
        load_cotangent = pltpu.make_async_copy(cotangent_in, cotangent, msem.at[5])
        load_table.start()
        load_cotangent.start()
        greet(ALL_PEERS)
        shards = (i0, i1, i2, i3, i4, i5, i6)
        targets = (wq, wk, wv, wo, wg, wu, wd)
        spreads = [
            GatherDp(shards[i], targets[i], kinds[i], wsems[0].at[i], wsems[1].at[i], lsem.at[i])
            for i in range(7)
        ]
        small, large, down_weights = spreads[:4], spreads[4:6], spreads[6]
        for spread_item in small:
            spread_item.start()
            spread_item.own_y.start()
        first.wait()
        gather = GatherTensor(dd, *gather_sems, 384)
        gather.start()

        sums[me] = jnp.zeros((8, 256), F32)

        def forward_small():
            for spread_item in small:
                spread_item.forward()
                spread_item.forward_y()

        def spread_small(stage):
            for spread_item in small:
                if stage == 0:
                    spread_item.share()
                    spread_item.forward_far()
                elif stage == 1:
                    spread_item.share_far()
                else:
                    spread_item.finish()
            if stage == 1:
                down_weights.own_y.start()
            if stage == 2:
                for spread_item in large:
                    spread_item.start()
                large[0].own_y.start()

        def heads(i):
            r = pl.ds(pl.multiple_of(i * 256, 256), 256)
            q = nn(dd[r, :], wq[...])
            k = nn(dd[r, :], wk[...])
            dq[r, :] = q
            dk[r, :] = k
            du[r, 0:256] = q.astype(BF16)
            du[r, 256:512] = k.astype(BF16)
            v_low[r, :] = nn(dd[r, :], wv[...]).astype(BF16)
            note_sums(sums.at[me], r, q * q, k * k)

        gather.run(lambda slot: None, spread_small, heads, forward_small, 5)
        keep_x.start()
        exchange = Exchange(sums, *sum_sems)
        exchange.start()
        keep_raw.start()
        load_table.wait()
        load_cotangent.wait()
        exchange.finish()
        large[1].own_y.start()
        for spread_item in large:
            spread_item.forward()
        large[0].forward_y()
        spread(dv, lax.rsqrt(exchange.sum() * (1.0 / 2048) + EPS))
        narrow = lax.broadcasted_iota(jnp.int32, (1024, 128), 1) < 64
        stats[:, 128:256] = jnp.where(narrow, dv[:, 0:128], dv[:, 128:256])

        @tiles(1024, 256)
        def _(r):
            cos, sin = cos_sin(table[r, :])
            for source, gain, s, target, factor in (
                (dq, q_gain, 0, q_rot, SCALE),
                (dk, k_gain, 128, k_rot, 1.0),
            ):
                scale = dv[r, s : s + 128]
                for h in (0, 128):
                    v = source[r, h : h + 128] * scale * gain[:, h : h + 128]
                    v = v * cos + pltpu.roll(v, 64, 1) * sin
                    target[r, h : h + 128] = (v * factor).astype(BF16)

        def attend(wanted):
            for i in range(4):

                @pl.when(wanted == i)
                def _():
                    @pl.loop(0, 2)
                    def _(h):
                        cols = pl.ds(pl.multiple_of(h * 128, 128), 128)
                        mine = lax.broadcasted_iota(jnp.int32, (256, 128), 1) // 64 == h
                        low = i * 256
                        block = slice(low, low + 256)
                        q = q_rot[block, cols]
                        near = diagonal_mask(nt(q, k_rot[block, cols]), low, length)
                        peak = jnp.max(near, 1, keepdims=True)
                        if i:
                            past = nt(q, k_rot[0:low, cols])
                            peak = jnp.maximum(peak, jnp.max(past, 1, keepdims=True))
                        e1 = jnp.exp(near - peak)
                        denom = jnp.sum(e1, 1, keepdims=True)
                        out = nn(e1.astype(BF16), v_low[block, cols])
                        if i:
                            e0 = jnp.exp(past - peak)
                            denom += jnp.sum(e0, 1, keepdims=True)
                            out += nn(e0.astype(BF16), v_low[0:low, cols])
                        mixed[block, cols] = (out / denom).astype(BF16)
                        lse = peak + jnp.log(denom)
                        stats[block, 0:128] = jnp.where(mine, lse, stats[block, 0:128])

        def project(first_row):
            attend(first_row // 256)
            s = pl.ds(pl.multiple_of(first_row, 256), 256)

            @pl.loop(0, 2)
            def _(i):
                n = pl.ds(pl.multiple_of(i * 1024, 1024), 1024)
                part[s, n] = nn(mixed[s, :], wo[:, n]).astype(BF16)

        scatter = ScatterTensor(part, bufs, *scatter_sems)
        scatter.run(project)
        keep_heads.start()
        large[1].forward_y()
        scatter.step(0)
        for spread_item in large:
            spread_item.share()
        scatter.step(1)
        for spread_item in large:
            spread_item.forward_far()
        down_weights.start()
        down_weights.forward_y()
        scatter.step(2)
        scatter.step(3)
        for spread_item in large:
            spread_item.share_far()
        scatter.finish(branch)
        own = rows(x, me)
        own_tokens = rows(dd, me)
        for copy in (keep_x, keep_raw, keep_heads):
            copy.wait()

        def tell(i):
            pl.semaphore_signal(ready.at[i], 1, device_id=other(dc=1), device_id_type=MESH)

        @tiles(128, 32)
        def _(r):
            b = branch[r, :]
            scale = lax.rsqrt(jnp.mean(b * b, 1, keepdims=True) + EPS)
            value = own_tokens[r, :].astype(F32) + b * scale * attn_gain[...]
            residual[r, :] = value
            own[r, :] = value.astype(BF16)

        gather = GatherTensor(x, *gather_sems)
        gather.start()
        down_weights.forward()
        for spread_item in large:
            spread_item.finish()

        def gate_up(slot):
            s = pl.ds(pl.multiple_of(slot * 128, 128), 128)

            @tiles(1024, 512)
            def _(n):
                gate = nn(x[s, :], wg[:, n])
                up = nn(x[s, :], wu[:, n])
                sigmoid = jax.nn.sigmoid(gate)
                low = gate * sigmoid
                silu[s, n] = low.astype(BF16)
                gate_factor[s, n] = (up * (sigmoid + low * (1.0 - sigmoid))).astype(BF16)
                inner[s, n] = (low * up).astype(BF16)

        def spread_down(stage):
            if stage == 0:
                down_weights.share()
                down_weights.forward_far()
            elif stage == 1:
                down_weights.share_far()
        gather.run(gate_up, spread_down)
        down_weights.finish()

        def down(first_row):
            s = pl.ds(pl.multiple_of(first_row, 256), 256)

            @pl.loop(0, 2)
            def _(i):
                n = pl.ds(pl.multiple_of(i * 1024, 1024), 1024)
                part[s, n] = nn(inner[s, :], wd[:, n]).astype(BF16)

        scatter = ScatterTensor(part, bufs, *scatter_sems)
        scatter.run(down)
        for n in range(4):
            scatter.step(n)
        scatter.finish(total)
        mlp_part[...] = jnp.zeros_like(mlp_part)
        attn_part[...] = jnp.zeros_like(attn_part)
        own_d = rows(dd, me)

        @tiles(128, 32)
        def _(r):
            v = total[r, :]
            position = lax.broadcasted_iota(jnp.int32, (32, 1), 0) + (me * 128 + r.start)
            ok = position < length
            scale = lax.rsqrt(jnp.mean(v * v, 1, keepdims=True) + EPS)
            normal = v * scale
            part[r, :] = jnp.where(ok, residual[r, :] + normal * mlp_gain[...], 0.0).astype(BF16)
            grad = jnp.where(ok, cotangent[r, :].astype(F32), 0.0)
            residual[r, :] = grad
            mlp_part[...] += jnp.sum(grad * normal, 0, keepdims=True)
            weighted = mlp_gain[...] * grad
            mean = jnp.mean(v * weighted, 1, keepdims=True)
            own_d[r, :] = (scale * weighted - v * (scale * scale * scale * mean)).astype(BF16)

        gather = GatherTensor(dd, *gather_sems)
        gather.start()
        store_act = pltpu.make_async_copy(part.at[pl.ds(0, 128)], act, msem.at[1])
        store_act.start()

        def d_inner(slot):
            s = pl.ds(pl.multiple_of(slot * 128, 128), 128)

            @tiles(1024, 512)
            def _(n):
                d = nt(dd[s, :], wd[n, :])
                dg[s, n] = (d * gate_factor[s, n].astype(F32)).astype(BF16)
                du[s, n] = (d * silu[s, n].astype(F32)).astype(BF16)

        gather.run(d_inner)
        store_act.wait()
        tell(0)

        def d_input(first_row):
            s = pl.ds(pl.multiple_of(first_row, 256), 256)

            @pl.loop(0, 2)
            def _(i):
                n = pl.ds(pl.multiple_of(i * 1024, 1024), 1024)
                part[s, n] = (nt(dg[s, :], wg[n, :]) + nt(du[s, :], wu[n, :])).astype(BF16)

        scatter = ScatterTensor(part, bufs, *scatter_sems)
        scatter.run(d_input)
        scatter.step(0)

        def down_grad(i):
            m = pl.ds(i * 512, 512)

            @tiles(2048, 512)
            def _(n):
                wd[m, n] = tn(inner[:, m], dd[:, n]).astype(BF16)

        def gate_grad(first):
            @pl.loop(first, first + 2)
            def _(i):
                m = pl.ds(pl.multiple_of(i * 512, 512), 512)

                @tiles(1024, 512)
                def _(n):
                    wg[m, n] = tn(x[:, m], dg[:, n]).astype(BF16)

        down_grad(0)
        down_grad(1)
        scatter.step(1)
        tell(1)

        def by_rows(ref):
            return lambda n: ref.at[pl.ds(n * 128, 128)]

        def by_columns(ref):
            return lambda n: ref.at[:, pl.ds(n * 128, 128)]

        small_slots = [by_rows(gate_factor.at[:, pl.ds(256 * i, 256)]) for i in range(3)]
        small_slots.append(
            lambda n: gate_factor.at[
                pl.ds(n // 2 * 256, 256), pl.ds(768 + n % 2 * 128, 128)
            ]
        )
        slots = small_slots + [by_rows(silu), by_rows(inner), by_columns(gate_factor)]
        wholes = (wq, wk, silu, wo, wg, wu, wd)
        scatter_kinds = kinds[:2] + ("folded",) + kinds[3:]
        items = [ScatterDp(wholes[i], scatter_kinds[i], slots[i], *dp_bufs[i]) for i in range(7)]
        qk, value_item, out_item, gate_item, up_item, down_item = items[:2], *items[2:]
        pl.semaphore_wait(ready.at[0], 1)
        down_item.start()
        scatter.step(2)
        gate_grad(0)
        scatter.step(3)
        gate_grad(2)
        gate_item.start()
        load_heads.start()
        down_item.along_x()
        tell(2)
        scatter.finish(total)

        @tiles(128, 32)
        def _(r):
            grad = residual[r, :] + total[r, :]
            residual[r, :] = grad
            b = branch[r, :]
            scale = lax.rsqrt(jnp.mean(b * b, 1, keepdims=True) + EPS)
            attn_part[...] += jnp.sum(grad * b * scale, 0, keepdims=True)
            weighted = attn_gain[...] * grad
            mean = jnp.mean(b * weighted, 1, keepdims=True)
            own_d[r, :] = (scale * weighted - b * (scale * scale * scale * mean)).astype(BF16)

        gather = GatherTensor(dd, *gather_sems, 768)
        gather.start()


        @tiles(2048, 512)
        def _(m):
            @tiles(1024, 512)
            def _(n):
                wu[m, n] = tn(x[:, m], du[:, n]).astype(BF16)

        reload.start()
        load_raw.start()
        gate_item.along_x()
        pl.semaphore_wait(ready.at[1], 1)
        up_item.start()
        dk[...] = jnp.zeros_like(dk)
        dv[...] = jnp.zeros_like(dv)

        def attend_back(wanted):
            for i in range(4):

                @pl.when(wanted == i)
                def _():
                    @pl.loop(0, 2)
                    def _(h):
                        cols = pl.ds(pl.multiple_of(h * 128, 128), 128)
                        low = i * 256
                        block = slice(low, low + 256)
                        q, d = q_rot[block, cols], do[block, cols]
                        peak = jnp.where(h == 0, stats[block, 0:1], stats[block, 64:65])
                        k1, v1 = k_rot[block, cols], v_low[block, cols]
                        p1 = jnp.exp(diagonal_mask(nt(q, k1), low, length) - peak)
                        dp1 = nt(d, v1)
                        delta = jnp.sum(p1 * dp1, 1, keepdims=True)
                        if i:
                            k0, v0 = k_rot[0:low, cols], v_low[0:low, cols]
                            p0 = jnp.exp(nt(q, k0) - peak)
                            dp0 = nt(d, v0)
                            delta += jnp.sum(p0 * dp0, 1, keepdims=True)
                        ds1 = (p1 * (dp1 - delta)).astype(BF16)
                        dq_block = nn(ds1, k1)
                        dk[block, cols] += tn(ds1, q)
                        dv[block, cols] += tn(p1.astype(BF16), d)
                        if i:
                            ds0 = (p0 * (dp0 - delta)).astype(BF16)
                            dq_block += nn(ds0, k0)
                            dk[0:low, cols] += tn(ds0, q)
                            dv[0:low, cols] += tn(p0.astype(BF16), d)
                        dq[block, cols] = dq_block

        def d_mixed(slot):
            s = pl.ds(pl.multiple_of(slot * 128, 128), 128)
            do[s, :] = nt(dd[s, :], wo[...]).astype(BF16)

        def beside(stage):
            if stage == 0:
                down_item.forward()
                load_heads.wait()
            elif stage == 1:
                gate_item.forward()
                up_item.along_x()
            else:
                down_item.along_y()

        gather.run(d_mixed, beside, attend_back)
        load_raw.wait()

        q_line[...] = jnp.zeros_like(q_line)
        k_line[...] = jnp.zeros_like(k_line)
        sums[me] = jnp.zeros((8, 256), F32)

        @tiles(1024, 256)
        def _(r):
            cos, sin = cos_sin(table[r, :])
            for source, rawer, gain, s, factor, line in (
                (dq, q_raw, q_gain, 128, SCALE, q_line),
                (dk, k_raw, k_gain, 192, 1.0, k_line),
            ):
                scale = stats[r, s : s + 1]
                for h in (0, 128):
                    v = source[r, h : h + 128] * factor
                    v = v * cos - pltpu.roll(v, 64, 1) * sin
                    w = v * rawer[r, h : h + 128].astype(F32)
                    line[:, h : h + 128] += jnp.sum(w * scale, 0, keepdims=True)
                    source[r, h : h + 128] = v * gain[:, h : h + 128]
            note_sums(
                sums.at[me],
                r,
                dq[r, :] * q_raw[r, :].astype(F32),
                dk[r, :] * k_raw[r, :].astype(F32),
            )
            dvr[r, :] = dv[r, :].astype(BF16)

        exchange = Exchange(sums, *sum_sems)
        exchange.start()
        reload.wait()
        row = lax.broadcasted_iota(jnp.int32, (8, 1024), 0)
        column = lax.broadcasted_iota(jnp.int32, (8, 1024), 1)
        message = jnp.zeros((8, 1024), F32)
        for k, line in enumerate((attn_part, attn_part, mlp_part, mlp_part)):
            line = line[:, 1024 * (k % 2) : 1024 * (k % 2) + 1024]
            message = jnp.where(row == 4 + k, line, message)
        for first_row, line in ((0, q_line), (2, k_line)):
            line = jnp.concatenate([line[...]] * 4, 1)
            message += jnp.where((row == first_row + yl) & (column // 256 == z), line, 0.0)
        gain_slots[me] = message
        total_gain = SumAll(gain_slots, gain_hold, gain_boxes, *isems)

        @pl.loop(0, 4)
        def _(i):
            m = pl.ds(pl.multiple_of(i * 512, 512), 512)
            r = pl.ds(pl.multiple_of(lax.rem(i, 2) * 512, 512), 512)
            columns = pl.ds(pl.multiple_of(i // 2 * 256, 256), 256)
            silu[r, columns] = tn(x[:, m], dvr[...]).astype(BF16)

        pl.semaphore_wait(ready.at[2], 1)
        value_item.start()
        exchange.finish()
        total_gain.start()
        gate_item.along_y()
        spread(dv, exchange.sum() * (1.0 / 2048))

        @tiles(1024, 256)
        def _(r):
            for source, rawer, s, target in ((dq, q_raw, 0, dqr), (dk, k_raw, 128, dkr)):
                scale = stats[r, 128 + s // 2 : 129 + s // 2]
                factor = scale * scale * scale * dv[r, s : s + 128]
                for h in (0, 128):
                    target[r, h : h + 128] = (
                        scale * source[r, h : h + 128]
                        - rawer[r, h : h + 128].astype(F32) * factor
                    ).astype(BF16)

        def d_tokens(first_row):
            s = pl.ds(pl.multiple_of(first_row, 256), 256)

            @pl.loop(0, 2)
            def _(i):
                n = pl.ds(pl.multiple_of(i * 1024, 1024), 1024)
                terms = nt(dqr[s, :], wq[n, :]) + nt(dkr[s, :], wk[n, :]) + nt(dvr[s, :], wv[n, :])
                part[s, n] = terms.astype(BF16)

        scatter = ScatterTensor(part, bufs, *scatter_sems, 640)
        scatter.run(d_tokens)
        up_item.forward()

        @tiles(2048, 512)
        def _(m):
            xt = x[:, m].T
            wq[m, :] = nn(xt, dqr[...]).astype(BF16)
            wk[m, :] = nn(xt, dkr[...]).astype(BF16)

        for item in qk:
            item.start()
        scatter.step(0)
        value_item.along_x()
        total_gain.core()

        @tiles(2048, 512)
        def _(n):
            wo[:, n] = tn(mixed[...], dd[:, n]).astype(BF16)

        out_item.start()
        scatter.step(2)
        value_item.forward()
        for item in qk:
            item.along_x()
        scatter.step(1)
        total_gain.along_x()
        out_item.along_x()
        up_item.along_y()
        scatter.step(3)
        for item in qk:
            item.forward()
        out_item.forward()
        value_item.along_y()
        total_gain.along_y()
        stores = []

        def store(item, source, target):
            item.finish(source)
            stores.append(pltpu.make_async_copy(source, target, lsem.at[len(stores)]))
            stores[-1].start()

        store(down_item, dv.at[:, pl.ds(0, 128)], o6)
        store(gate_item, gate_out, o4)
        for item in qk:
            item.along_y()
        out_item.along_y()
        scatter.finish(total)

        @tiles(128, 32)
        def _(r):
            total[r, :] += residual[r, :]

        stores.append(pltpu.make_async_copy(total, input_grad, lsem.at[len(stores)]))
        stores[-1].start()
        store(up_item, up_out, o5)
        total_gain.finish(gain_slots.at[0])
        for i, out in enumerate((q_sum, k_sum, attn_sum, mlp_sum)):
            gain_lines[i, :, 0:1024] = gain_slots[0, 2 * i : 2 * i + 1, :]
            gain_lines[i, :, 1024:2048] = gain_slots[0, 2 * i + 1 : 2 * i + 2, :]
            stores.append(pltpu.make_async_copy(gain_lines.at[i], out, lsem.at[len(stores)]))
            stores[-1].start()
        store(value_item, dk.at[pl.ds(256, 128)], o2)
        for i, out in enumerate((o0, o1)):
            store(qk[i], dk.at[pl.ds(128 * i, 128)], out)
        store(out_item, dv.at[pl.ds(0, 256), pl.ds(128, 128)], o3)
        for copy in stores:
            copy.wait()

    S = jax.ShapeDtypeStruct
    W = pltpu.VMEM
    scratch = [W((1024, 2048), BF16)] * 2 + [W((2048, 1024), BF16)] * 2 + [W((1024, 2048), BF16)]
    scratch += [W((1024, 1024), BF16)] * 5 + [W((1024, 2048), BF16)]
    scratch += [W((128, 2048), F32)] + [W((1, 2048), F32)] * 2 + [W((1, 256), F32)] * 2
    scratch += [W((2048, 256), BF16)] * 3 + [W((256, 2048), BF16)]
    scratch += [W((1024, 256), F32), W((128, 2048), F32), W((128, 2048), BF16)]
    scratch += [W((1024, 128), F32), W((4, 1, 2048), F32), W((128, 2048), F32)]
    scratch += [W((128, 1024), F32)] * 2 + [W((1024, 256), BF16)]
    scratch += [W((1024, 256), F32)] * 3
    scratch += [W((8, 8, 256), F32), W((8, 8, 1024), F32)] + [W((3, 8, 1024), F32), W((5, 8, 1024), F32)]
    scratch += ScatterTensor.scratch(640, CUT)
    for b in blocks:
        scratch += ScatterDp.scratch(b)
    scratch += [DMA, DMA((14,)), DMA, DMA((21,)), DMA, DMA((7,)), DMA((6,)), DMA((12,))]
    scratch += [DMA((7,)), DMA((7, 14))]
    scratch += [DMA((12,)), DMA((6,)), pltpu.SemaphoreType.REGULAR((3,))]
    return pl.pallas_call(
        layer_step,
        out_shape=[S((128, 2048), BF16), S((128, 2048), F32)]
        + [S(b, F32) for b in blocks]
        + [S((1, 2048), F32)] * 4
        + [S((1024, 2048), BF16), S((1024, 1024), BF16), S((1024, 512), BF16)],
        in_specs=[SMEM] + [VM] * 4 + [ANY] * 10,
        out_specs=[ANY] * 16,
        scratch_shapes=scratch,
        compiler_params=params(1),
        name="layer_step",
    )(lengths, *gains, tokens, cotangent, table, *weights)[:13]


def hand_over(*arrays):
    n = len(arrays)

    def hand_over_step(*refs):
        held, (lsem, ssem) = refs[2 * n : 3 * n], refs[3 * n :]
        loads = [pltpu.make_async_copy(refs[i], held[i], lsem.at[i]) for i in range(n)]
        stores = [pltpu.make_async_copy(held[i], refs[n + i], ssem.at[i]) for i in range(n)]
        for copy in loads:
            copy.start()
        for load, store in zip(loads, stores):
            load.wait()
            store.start()
        for copy in stores:
            copy.wait()

    return pl.pallas_call(
        hand_over_step,
        out_shape=[jax.ShapeDtypeStruct(a.shape, a.dtype) for a in arrays],
        in_specs=[ANY] * n,
        out_specs=[ANY] * n,
        scratch_shapes=[pltpu.VMEM(a.shape, a.dtype) for a in arrays] + [DMA((n,))] * 2,
        compiler_params=pltpu.CompilerParams(vmem_limit_bytes=63 << 20),
        name="hand_over_step",
    )(*arrays)


def local(
    tokens, lengths, w_query, w_key, w_value, w_out, w_gate, w_up, w_down,
    q_gain, k_gain, attn_gain, mlp_gain, cotangent,
):
    weights = (w_query, w_key, w_value, w_out, w_gate, w_up, w_down)
    gains = (q_gain[None], k_gain[None], attn_gain[None], mlp_gain[None])
    results = whole_layer(tokens[0], lengths, cotangent[0], gains, weights, rope_table())
    act, input_grad, *grads = hand_over(*results)
    return (act[None], input_grad[None], *grads[:7], *(g.reshape(2048) for g in grads[7:]))


def solution(mesh):
    return jax.shard_map(
        local,
        mesh=mesh,
        in_specs=(
            P("dp", "tensor", None),
            P("dp"),
            P("dp", "tensor"),
            P("dp", "tensor"),
            P("dp", "tensor"),
            P("tensor", "dp"),
            P("dp", "tensor"),
            P("dp", "tensor"),
            P("tensor", "dp"),
            P(),
            P(),
            P(),
            P(),
            P("dp", "tensor", None),
        ),
        out_specs=(
            P("dp", "tensor", None),
            P("dp", "tensor", None),
            P("dp", "tensor"),
            P("dp", "tensor"),
            P("dp", "tensor"),
            P("tensor", "dp"),
            P("dp", "tensor"),
            P("dp", "tensor"),
            P("tensor", "dp"),
            P(),
            P(),
            P(),
            P(),
        ),
        check_vma=False,
    )
```

```python
import jax
import jax.numpy as jnp
import numpy as np
from jax import lax
from jax.experimental import pallas as pl
from jax.experimental.pallas import tpu as pltpu
from jax.sharding import PartitionSpec as P

HEAD_DIM = 128
EPS = 1e-06
THETA = 500000.0
MESH = pl.DeviceIdType.MESH
BF16 = jnp.bfloat16
F32 = jnp.float32
ANY = pl.BlockSpec(memory_space=pl.ANY)
VM = pl.BlockSpec(memory_space=pltpu.VMEM)
DMA = pltpu.SemaphoreType.DMA
CUT = 896
WIDTH = 2048


def place():
    d = lax.axis_index("dp")
    t = lax.axis_index("tensor")
    return d // 8, lax.rem(d // 2, 4), lax.rem(d, 2), t // 4, lax.rem(t, 4)


def other(dyh=0, dx=0, dc=0, dyl=0, dz=0):
    yh, x, c, yl, z = place()
    return (
        lax.rem(yh + dyh, 2) * 8 + lax.rem(x + dx, 4) * 2 + lax.rem(c + dc, 2),
        lax.rem(yl + dyl, 2) * 4 + lax.rem(z + dz, 4),
    )


TENSOR_PEERS = (dict(dz=1), dict(dz=3), dict(dyl=1))
DP_PEERS = (dict(dx=1), dict(dx=2), dict(dx=3), dict(dyh=1), dict(dc=1))
SMEM = pl.BlockSpec(memory_space=pltpu.SMEM)


def greet(peers):
    barrier = pltpu.get_barrier_semaphore()
    for peer in peers:
        pl.semaphore_signal(barrier, 1, device_id=other(**peer), device_id_type=MESH)
    pl.semaphore_wait(barrier, len(peers))


def remote(src, dst, sems, index, peer):
    ssem, rsem = sems
    return pltpu.make_async_remote_copy(
        src_ref=src,
        dst_ref=dst,
        send_sem=ssem,
        recv_sem=rsem.at[index],
        device_id=other(**peer),
        device_id_type=MESH,
    )


def all_of(bytes_of, sem):
    pltpu.make_async_copy(bytes_of, bytes_of, sem).wait()


def rows(ref, slot):
    return ref.at[pl.ds(pl.multiple_of(slot * 128, 128), 128)]


def halves(ref):
    half = ref.shape[0] // 2
    return ref.at[pl.ds(0, half)], ref.at[pl.ds(half, half)]


def add_into(out, *terms):
    step = min(out.shape[0], 32 if out.shape[1] > 1024 else 64 if out.shape[1] > 128 else 128)

    @pl.loop(0, out.shape[0] // step)
    def _(i):
        r = pl.ds(pl.multiple_of(i * step, step), step)
        if len(terms) == 2 and out.dtype == BF16:
            out[r, :] = terms[0][r, :] + terms[1][r, :]
        else:
            total = terms[0][r, :].astype(F32)
            for term in terms[1:]:
                total += term[r, :].astype(F32)
            out[r, :] = total.astype(out.dtype)


class RingGather:
    COPIES = 6

    def __init__(self, block, axis, sems, base, source=None):
        up, down = {axis: 1}, {axis: 3}
        src = halves(block(0) if source is None else source)
        own, behind, ahead = halves(block(0)), halves(block(3)), halves(block(1))
        self.copies = [
            remote(src[0], own[0], sems, base, up),
            remote(src[1], own[1], sems, base + 1, down),
            remote(src[1], own[1], sems, base + 2, up),
            remote(src[0], own[0], sems, base + 3, down),
            remote(behind[0], behind[0], sems, base + 4, up),
            remote(ahead[1], ahead[1], sems, base + 5, down),
        ]

    def start(self):
        for copy in self.copies[:4]:
            copy.start()

    def forward(self):
        for i in range(2):
            self.copies[i].wait_recv()
            self.copies[4 + i].start()

    def behind(self):
        self.copies[2].wait_recv()

    def ahead(self):
        self.copies[3].wait_recv()

    def far(self):
        for copy in self.copies[4:]:
            copy.wait_recv()


class RingReduce:
    COPIES = 6

    @staticmethod
    def scratch(n, m):
        return [pltpu.VMEM((2, n // 2, m), BF16), pltpu.VMEM((2, n, m), BF16)]

    def __init__(self, block, axis, part, full, sems, base):
        up, down = {axis: 1}, {axis: 3}
        one, two, three = halves(block(1)), halves(block(2)), halves(block(3))
        from_behind, from_ahead = halves(full.at[0]), halves(full.at[1])
        self.adds = ((one[0], part.at[0]), (three[1], part.at[1]))
        self.terms = (block(0), full.at[0], full.at[1])
        self.full, self.full_sem = full, sems[1].at[base + 2]
        self.copies = [
            remote(two[0], part.at[0], sems, base, up),
            remote(two[1], part.at[1], sems, base + 1, down),
            remote(one[1], from_behind[1], sems, base + 2, up),
            remote(three[0], from_ahead[0], sems, base + 2, down),
            remote(one[0], from_behind[0], sems, base + 2, up),
            remote(three[1], from_ahead[1], sems, base + 2, down),
        ]

    def start(self):
        for copy in self.copies[:4]:
            copy.start()

    def forward(self):
        for i in range(2):
            self.copies[i].wait_recv()
            add_into(self.adds[i][0], *self.adds[i])
            self.copies[4 + i].start()

    def arrive(self):
        all_of(self.full, self.full_sem)


class GatherTensor:
    COPIES = 21

    def __init__(self, buf, ssem, rsem, cut=CUT):
        yh, x, c, yl, z = place()
        self.yl, self.z = yl, z
        self.sent, self.ssem = buf.at[pl.ds(0, 896)], ssem
        sems = (ssem, rsem)
        slot = lambda k, i: rows(buf, lax.rem(yl + k, 2) * 4 + lax.rem(z + i, 4))
        low = lambda ref: ref.at[:, pl.ds(0, cut)]
        high = lambda ref: ref.at[:, pl.ds(cut, WIDTH - cut)]
        self.ring = RingGather(lambda i: slot(0, i), "dz", sems, 0)
        self.pair_ring = RingGather(lambda i: high(slot(1, i)), "dz", sems, 6)
        own = slot(0, 0)
        pair = dict(dyl=1)
        self.high = remote(high(own), high(own), sems, 12, pair)
        self.low = []
        for n, i in enumerate((0, 3, 1, 2)):
            for half in halves(low(slot(0, i))):
                self.low.append(remote(half, half, sems, 13 + len(self.low), pair))

    def start(self):
        self.high.start()
        self.ring.start()
        self.low[0].start()
        self.low[1].start()

    def run(self, process, spare=None, by_block=None, early=None, first=3):
        yl, z = self.yl, self.z

        @pl.loop(0, 2)
        def _(k):
            @pl.when(k == 1)
            def _():
                self.ring.forward()
                self.low[2].start()
                self.low[5].start()
                if early is not None:
                    early()
                self.high.wait_recv()
                self.pair_ring.start()
                self.ring.behind()
                self.low[3].start()
                self.ring.ahead()
                self.low[4].start()
                self.low[0].wait_recv()
                self.low[1].wait_recv()

            process(lax.rem(yl + k, 2) * 4 + z)

        if spare is not None:
            spare(0)

        @pl.loop(0, 6 if by_block is None else 7)
        def _(j):
            if spare is not None:
                for stage, at in ((1, 3), (2, 5)):

                    @pl.when(j == at)
                    def _():
                        spare(stage)

            if by_block is not None:
                last = j // 6
                rest = 2 - 2 * yl + last * (1 - z // 2) + (1 - last) * (z // 2)

                @pl.when((j >= 5) | (j == first))
                def _():
                    @pl.loop(0, 3)
                    def _(t):
                        third = t // 2

                        @pl.when(((t < 2) & (j == first)) | ((t == 2) & (j >= 5)))
                        def _():
                            by_block((1 - third) * (2 * yl + t) + third * rest)

            @pl.when(j == 2)
            def _():
                self.ring.far()
                self.low[6].start()
                self.low[7].start()
                self.pair_ring.forward()

            @pl.when(j == 3)
            def _():
                self.pair_ring.behind()
                self.low[2].wait_recv()
                self.low[3].wait_recv()

            @pl.when(j == 4)
            def _():
                self.pair_ring.ahead()
                self.low[4].wait_recv()
                self.low[5].wait_recv()

            @pl.when(j == 5)
            def _():
                self.pair_ring.far()
                self.low[6].wait_recv()
                self.low[7].wait_recv()

            i = lax.rem(j, 3)
            step = (3 * i * i - 7 * i + 6) // 2

            @pl.when(j < 6)
            def _():
                process(lax.rem(yl + j // 3, 2) * 4 + lax.rem(z + step, 4))

        all_of(self.sent, self.ssem)


class ScatterTensor:
    COPIES = 23

    @staticmethod
    def scratch(least, most):
        return (
            [pltpu.VMEM((4, 128, most), BF16), pltpu.VMEM((128, WIDTH - least), BF16)]
            + RingReduce.scratch(128, most)
            + RingReduce.scratch(128, WIDTH - least) * 2
        )

    def __init__(self, part, bufs, ssem, rsem, cut=CUT):
        yh, x, c, yl, z = place()
        self.z = z
        narrow = lambda ref, n: ref.at[:, :, pl.ds(0, n)]
        wide = WIDTH - cut
        bufs = [
            narrow(bufs[0], cut),
            bufs[1].at[:, pl.ds(0, wide)],
            *(narrow(ref, cut) for ref in bufs[2:4]),
            *(narrow(ref, wide) for ref in bufs[4:]),
        ]
        self.yl = yl
        self.from_pair, self.last = bufs[0], bufs[1]
        self.sent, self.ssem = part.at[pl.ds(0, 896)], ssem
        sems = (ssem, rsem)
        slot = lambda k, i: rows(part, lax.rem(yl + k, 2) * 4 + lax.rem(z + i, 4))
        low = lambda k, i: slot(k, i).at[:, pl.ds(0, cut)]
        high = lambda k, i: slot(k, i).at[:, pl.ds(cut, wide)]
        self.cut = cut
        pair = dict(dyl=1)
        self.low = lambda i: low(0, i)
        self.low_ring = RingReduce(lambda i: low(0, i), "dz", bufs[2], bufs[3], sems, 0)
        self.pair_ring = RingReduce(lambda i: high(1, i), "dz", bufs[4], bufs[5], sems, 3)
        self.own_ring = RingReduce(lambda i: high(0, i), "dz", bufs[6], bufs[7], sems, 6)
        self.first = lambda i: remote(low(1, i), bufs[0].at[i], sems, 9 + i, pair)
        self.second = remote(high(1, 0), bufs[1], sems, 13, pair)

    def run(self, process):
        yl, z = self.yl, self.z

        @pl.loop(0, 4)
        def _(k):
            half = lax.rem(yl + 1 + k // 2, 2)
            process(half * 512 + lax.rem((z + 2) // 2 + k, 2) * 256)
            beside = 3 - 2 * lax.rem(z, 2)

            @pl.when(k == 0)
            def _():
                self.first(2).start()
                self.pair_ring.copies[0].start()
                self.pair_ring.copies[1].start()
                self.first(beside).start()

            @pl.when(k == 1)
            def _():
                self.first(4 - beside).start()
                self.pair_ring.copies[2].start()
                self.pair_ring.copies[3].start()
                self.first(0).start()

    def add_first(self, i):
        self.first(i).wait_recv()
        add_into(self.low(i), self.low(i), self.from_pair.at[i])

    def add_low(self, i):
        self.add_first(i)
        for k in (1, 3):

            @pl.when(i == k)
            def _():
                self.low_ring.copies[2 + k // 3].start()

    def step(self, n):
        beside = 3 - 2 * lax.rem(self.z, 2)
        if n == 0:
            self.pair_ring.forward()
            self.own_ring.start()
            self.add_first(2)
            self.low_ring.copies[0].start()
            self.low_ring.copies[1].start()
        if n == 1:
            self.own_ring.forward()
            self.add_low(beside)
        if n == 2:
            self.pair_ring.arrive()
            add_into(self.pair_ring.terms[0], *self.pair_ring.terms)
            self.second.start()
            self.add_low(4 - beside)
        if n == 3:
            self.low_ring.forward()
            self.add_first(0)

    def finish(self, out):
        self.own_ring.arrive()
        self.second.wait_recv()
        add_into(out.at[:, pl.ds(self.cut, WIDTH - self.cut)], *self.own_ring.terms, self.last)
        self.low_ring.arrive()
        add_into(out.at[:, pl.ds(0, self.cut)], *self.low_ring.terms)
        all_of(self.sent, self.ssem)


def block_of(ref, kind, slot):
    if kind == "row":
        size = ref.shape[0] // 16
        return ref.at[pl.ds(pl.multiple_of(slot * size, size), size)]
    if kind == "folded":
        return ref.at[
            pl.ds(pl.multiple_of(lax.rem(slot, 8) * 128, 128), 128),
            pl.ds(pl.multiple_of(slot // 8 * 256, 256), 256),
        ]
    size = ref.shape[1] // 16
    return ref.at[:, pl.ds(pl.multiple_of(slot * size, size), size)]


def some_of(ref, kind, count):
    if kind == "row":
        return ref.at[pl.ds(0, ref.shape[0] // 16 * count)]
    if kind == "folded":
        return ref.at[pl.ds(0, 64 * count), pl.ds(0, 512)]
    return ref.at[:, pl.ds(0, ref.shape[1] // 16 * count)]


class GatherDp:
    COPIES = 21

    def __init__(self, shard, out, kind, ssem, rsem, lsem):
        yh, x, c, yl, z = place()
        sems = (ssem, rsem)
        block = lambda k, i: block_of(
            out, kind, lax.rem(yh + k, 2) * 8 + lax.rem(x + i, 4) * 2 + c
        )
        self.sent, self.ssem = some_of(out, kind, 15), ssem
        self.local = pltpu.make_async_copy(shard, block(0, 0), lsem)
        self.ring = RingGather(lambda i: block(0, i), "dx", sems, 0, shard)
        self.far_ring = RingGather(lambda i: block(1, i), "dx", sems, 6)
        self.own_y = remote(shard, block(0, 0), sems, 12, dict(dyh=1))
        core = dict(dc=1)
        self.core = [remote(shard, block(0, 0), sems, 13, core)]
        for n in range(1, 8):
            ref = block(n // 4, n % 4)
            self.core.append(remote(ref, ref, sems, 13, core))
        self.shared, self.shared_sem = some_of(out, kind, 8), rsem.at[13]

    def start(self):
        self.ring.start()
        self.core[0].start()
        self.local.start()

    def forward(self):
        self.ring.forward()

    def forward_y(self):
        self.own_y.wait_recv()
        self.far_ring.start()
        self.core[4].start()

    def share(self):
        self.ring.behind()
        self.core[3].start()
        self.ring.ahead()
        self.core[1].start()
        self.ring.far()
        self.core[2].start()

    def forward_far(self):
        self.far_ring.forward()

    def share_far(self):
        self.far_ring.behind()
        self.core[7].start()
        self.far_ring.ahead()
        self.core[5].start()
        self.far_ring.far()
        self.core[6].start()

    def finish(self):
        all_of(self.shared, self.shared_sem)
        self.local.wait()
        all_of(self.sent, self.ssem)


class ScatterDp:
    COPIES = 21

    @staticmethod
    def scratch(block):
        return (
            [pltpu.VMEM(block, BF16)]
            + RingReduce.scratch(*block) * 2
            + [DMA, DMA((8,))]
        )

    def __init__(self, part, kind, from_core, from_y, h0, f0, h1, f1, ssem, rsem):
        yh, x, c, yl, z = place()
        sems = (ssem, rsem)
        self.from_core, self.from_y = from_core, from_y
        self.sent, self.ssem = some_of(part, kind, 15), ssem
        block = lambda k, i, d: block_of(
            part, kind, lax.rem(yh + k, 2) * 8 + lax.rem(x + i, 4) * 2 + d
        )
        self.block = lambda k, i: block(k, i, c)
        self.core = [
            remote(block(n // 4, n % 4, 1 - c), from_core(n), sems, 0, dict(dc=1))
            for n in range(8)
        ]
        self.ring = RingReduce(lambda i: block(0, i, c), "dx", h0, f0, sems, 1)
        self.far_ring = RingReduce(lambda i: block(1, i, c), "dx", h1, f1, sems, 4)
        self.last = remote(block(1, 0, c), from_y, sems, 7, dict(dyh=1))
        self.shared, self.shared_sem = some_of(part, kind, 8), rsem.at[0]

    def start(self):
        for n in (6, 5, 7, 4, 2, 1, 3, 0):
            self.core[n].start()

    def add_core(self, n):
        ref = self.block(n // 4, n % 4)
        add_into(ref, ref, self.from_core(n))

    def along_x(self):
        all_of(self.shared, self.shared_sem)
        for n in (6, 5, 7):
            self.add_core(n)
        self.far_ring.start()
        for n in (2, 1, 3):
            self.add_core(n)
        self.ring.start()
        for n in (4, 0):
            self.add_core(n)

    def forward(self):
        self.far_ring.forward()
        self.ring.forward()

    def along_y(self):
        self.far_ring.arrive()
        add_into(self.far_ring.terms[0], *self.far_ring.terms)
        self.last.start()

    def finish(self, out):
        self.ring.arrive()
        self.last.wait_recv()
        add_into(out, *self.ring.terms, self.from_y)
        all_of(self.sent, self.ssem)


def params(cid):
    return pltpu.CompilerParams(
        collective_id=cid, has_side_effects=True, vmem_limit_bytes=65400 << 10
    )


def nn(a, b):
    return jnp.dot(a, b, preferred_element_type=F32)


def nt(a, b):
    return lax.dot_general(a, b, (((1,), (1,)), ((), ())), preferred_element_type=F32)


def tn(a, b):
    return lax.dot_general(a, b, (((0,), (0,)), ((), ())), preferred_element_type=F32)


def tiles(count, size):
    def run(body):
        @pl.loop(0, count // size)
        def _(i):
            body(pl.ds(pl.multiple_of(i * size, size), size))

    return run


def rope_table():
    frequency = THETA ** (-(np.arange(64, dtype=np.float32) * np.float32(2.0) / np.float32(HEAD_DIM)))
    angles = np.arange(1024, dtype=np.float32)[:, None] * frequency.astype(np.float32)[None, :]
    cosine, sine = np.cos(angles), np.sin(angles)
    return np.concatenate([cosine, sine], 1).astype(np.float32)


def cos_sin(table):
    turned = pltpu.roll(table, 64, 1)
    first = lax.broadcasted_iota(jnp.int32, table.shape, 1) < 64
    return jnp.where(first, table, turned), jnp.where(first, -turned, table)


class Exchange:
    PEERS = tuple(dict(dz=a, dyl=b) for b in range(2) for a in range(4) if a or b)

    def __init__(self, buf, ssem, rsem):
        yh, x, c, yl, z = place()
        self.buf, self.ssem = buf, ssem
        self.mine = buf.at[yl * 4 + z]
        self.copies = [
            remote(self.mine, self.mine, (ssem, rsem), i, peer)
            for i, peer in enumerate(self.PEERS)
        ]

    def start(self):
        for copy in self.copies:
            copy.start()

    def finish(self):
        for copy in self.copies:
            copy.wait_recv()
        all_of(self.buf.at[pl.ds(0, 7)], self.ssem)

    def sum(self):
        total = self.buf[0]
        for i in range(1, 8):
            total += self.buf[i]
        return total


def row_sums(values):
    return nt(jnp.ones((8, values.shape[1]), F32), values)


def spread(out, pair):
    row = lax.broadcasted_iota(jnp.int32, (8, 256), 0)
    column = lax.broadcasted_iota(jnp.int32, (8, 256), 1)
    for i in range(4):
        pick = jnp.where(row == column // 128 * 4 + i, 1.0, 0.0)
        out[pl.ds(256 * i, 256), :] = lax.dot_general(
            pair,
            pick,
            (((0,), (0,)), ((), ())),
            precision=lax.Precision.HIGHEST,
            preferred_element_type=F32,
        )


def note_sums(out, r, a, b):
    row = lax.broadcasted_iota(jnp.int32, (8, 256), 0)
    sums = jnp.where(row < 4, row_sums(a), row_sums(b))
    out[...] = jnp.where(lax.rem(row, 4) == r.start // 256, sums, out[...])


ALL_PEERS = Exchange.PEERS + DP_PEERS
SCALE = HEAD_DIM**-0.5


def diagonal_mask(scores, first, length):
    row = lax.broadcasted_iota(jnp.int32, scores.shape, 0)
    column = lax.broadcasted_iota(jnp.int32, scores.shape, 1)
    return jnp.where((column <= row) & (column + first < length), scores, -1e30)


class SumAll:
    def __init__(self, slots, hold, boxes, ssem, rsem):
        self.exchange = Exchange(slots, ssem.at[5], rsem)
        self.hold, self.boxes = hold, boxes
        self.copies = []
        for i, peer in enumerate(DP_PEERS):
            k = (1, 1, 1, 2, 0)[i]
            self.copies.append(remote(hold.at[k], boxes.at[i], (ssem.at[i], rsem), 7 + i, peer))

    def start(self):
        self.exchange.start()

    def core(self):
        self.exchange.finish()
        self.hold[0] = self.exchange.sum()
        self.copies[4].start()

    def along_x(self):
        self.copies[4].wait()
        self.hold[1] = self.hold[0] + self.boxes[4]
        for copy in self.copies[:3]:
            copy.start()

    def along_y(self):
        for copy in self.copies[:3]:
            copy.wait()
        self.hold[2] = self.hold[1] + self.boxes[0] + self.boxes[1] + self.boxes[2]
        self.copies[3].start()

    def finish(self, out):
        self.copies[3].wait()
        out[...] = self.hold[2] + self.boxes[3]


def whole_layer(tokens, lengths, cotangent, gains, weights, table):
    kinds = ("row", "row", "row", "col", "row", "row", "col")
    blocks = ((128, 256),) * 3 + ((256, 128), (128, 1024), (128, 1024), (1024, 128))

    def layer_step(
        lengths, q_gain_all, k_gain_all, attn_gain, mlp_gain, tokens, cotangent_in, table_in, i0, i1, i2, i3, i4, i5, i6,
        act, input_grad, o0, o1, o2, o3, o4, o5, o6,
        q_sum, k_sum, attn_sum, mlp_sum, x_kept, heads_kept, raw_kept,
        x, dd, wg, wu, wd, gate_factor, silu, inner, dg, du, part, residual, attn_part, mlp_part, q_line, k_line,
        wq, wk, wv, wo, stats, branch, cotangent, table, gain_lines, total, gate_out, up_out, do, dq, dk, dv, sums, gain_slots, gain_hold, gain_boxes,
        *rest,
    ):
        bufs, rest = rest[:8], rest[8:]
        dp_bufs, rest = [rest[7 * i : 7 * i + 7] for i in range(7)], rest[49:]
        scatter_sems, gather_sems, sum_sems, isems, wsems = [
            rest[2 * i : 2 * i + 2] for i in range(5)
        ]
        lsem, msem, ready = rest[10:]
        yh, xx, c, yl, z = place()
        me = yl * 4 + z
        length = lengths[0]
        own_columns = pl.ds(pl.multiple_of(me * 256, 256), 256)
        q_gain, k_gain = q_gain_all[:, own_columns], k_gain_all[:, own_columns]
        q_rot, k_rot, v_low, mixed = (dg.at[:, pl.ds(256 * i, 256)] for i in range(4))
        q_raw, k_raw, dvr = (du.at[:, pl.ds(256 * i, 256)] for i in range(3))
        dqr, dkr = q_raw, k_raw
        raw = du.at[:, pl.ds(0, 512)]
        load_heads = pltpu.make_async_copy(heads_kept, dg, msem.at[0])
        load_raw = pltpu.make_async_copy(raw_kept, raw, msem.at[2])
        reload = pltpu.make_async_copy(x_kept, x, msem.at[1])
        keep_x = pltpu.make_async_copy(dd, x_kept, msem.at[1])
        keep_heads = pltpu.make_async_copy(dg, heads_kept, msem.at[0])
        keep_raw = pltpu.make_async_copy(raw, raw_kept, msem.at[2])
        first = pltpu.make_async_copy(tokens, rows(dd, me), msem.at[3])
        first.start()
        load_table = pltpu.make_async_copy(table_in, table, msem.at[4])
        load_cotangent = pltpu.make_async_copy(cotangent_in, cotangent, msem.at[5])
        load_table.start()
        load_cotangent.start()
        greet(ALL_PEERS)
        shards = (i0, i1, i2, i3, i4, i5, i6)
        targets = (wq, wk, wv, wo, wg, wu, wd)
        spreads = [
            GatherDp(shards[i], targets[i], kinds[i], wsems[0].at[i], wsems[1].at[i], lsem.at[i])
            for i in range(7)
        ]
        small, large, down_weights = spreads[:4], spreads[4:6], spreads[6]
        for spread_item in small:
            spread_item.start()
            spread_item.own_y.start()
        first.wait()
        gather = GatherTensor(dd, *gather_sems, 384)
        gather.start()

        sums[me] = jnp.zeros((8, 256), F32)

        def forward_small():
            for spread_item in small:
                spread_item.forward()
                spread_item.forward_y()

        def spread_small(stage):
            for spread_item in small:
                if stage == 0:
                    spread_item.share()
                    spread_item.forward_far()
                elif stage == 1:
                    spread_item.share_far()
                else:
                    spread_item.finish()
            if stage == 1:
                down_weights.own_y.start()
            if stage == 2:
                for spread_item in large:
                    spread_item.start()
                large[0].own_y.start()

        def heads(i):
            r = pl.ds(pl.multiple_of(i * 256, 256), 256)
            q = nn(dd[r, :], wq[...])
            k = nn(dd[r, :], wk[...])
            dq[r, :] = q
            dk[r, :] = k
            du[r, 0:256] = q.astype(BF16)
            du[r, 256:512] = k.astype(BF16)
            v_low[r, :] = nn(dd[r, :], wv[...]).astype(BF16)
            note_sums(sums.at[me], r, q * q, k * k)

        gather.run(lambda slot: None, spread_small, heads, forward_small, 5)
        keep_x.start()
        exchange = Exchange(sums, *sum_sems)
        exchange.start()
        keep_raw.start()
        load_table.wait()
        load_cotangent.wait()
        exchange.finish()
        large[1].own_y.start()
        for spread_item in large:
            spread_item.forward()
        large[0].forward_y()
        spread(dv, lax.rsqrt(exchange.sum() * (1.0 / 2048) + EPS))
        narrow = lax.broadcasted_iota(jnp.int32, (1024, 128), 1) < 64
        stats[:, 128:256] = jnp.where(narrow, dv[:, 0:128], dv[:, 128:256])

        @tiles(1024, 256)
        def _(r):
            cos, sin = cos_sin(table[r, :])
            for source, gain, s, target, factor in (
                (dq, q_gain, 0, q_rot, SCALE),
                (dk, k_gain, 128, k_rot, 1.0),
            ):
                scale = dv[r, s : s + 128]
                for h in (0, 128):
                    v = source[r, h : h + 128] * scale * gain[:, h : h + 128]
                    v = v * cos + pltpu.roll(v, 64, 1) * sin
                    target[r, h : h + 128] = (v * factor).astype(BF16)

        def attend(wanted):
            for i in range(4):

                @pl.when(wanted == i)
                def _():
                    @pl.loop(0, 2)
                    def _(h):
                        cols = pl.ds(pl.multiple_of(h * 128, 128), 128)
                        mine = lax.broadcasted_iota(jnp.int32, (256, 128), 1) // 64 == h
                        low = i * 256
                        block = slice(low, low + 256)
                        q = q_rot[block, cols]
                        near = diagonal_mask(nt(q, k_rot[block, cols]), low, length)
                        peak = jnp.max(near, 1, keepdims=True)
                        if i:
                            past = nt(q, k_rot[0:low, cols])
                            peak = jnp.maximum(peak, jnp.max(past, 1, keepdims=True))
                        e1 = jnp.exp(near - peak)
                        denom = jnp.sum(e1, 1, keepdims=True)
                        out = nn(e1.astype(BF16), v_low[block, cols])
                        if i:
                            e0 = jnp.exp(past - peak)
                            denom += jnp.sum(e0, 1, keepdims=True)
                            out += nn(e0.astype(BF16), v_low[0:low, cols])
                        mixed[block, cols] = (out / denom).astype(BF16)
                        lse = peak + jnp.log(denom)
                        stats[block, 0:128] = jnp.where(mine, lse, stats[block, 0:128])

        def project(first_row):
            attend(first_row // 256)
            s = pl.ds(pl.multiple_of(first_row, 256), 256)

            @pl.loop(0, 2)
            def _(i):
                n = pl.ds(pl.multiple_of(i * 1024, 1024), 1024)
                part[s, n] = nn(mixed[s, :], wo[:, n]).astype(BF16)

        scatter = ScatterTensor(part, bufs, *scatter_sems)
        scatter.run(project)
        keep_heads.start()
        large[1].forward_y()
        scatter.step(0)
        for spread_item in large:
            spread_item.share()
        scatter.step(1)
        for spread_item in large:
            spread_item.forward_far()
        down_weights.start()
        down_weights.forward_y()
        scatter.step(2)
        scatter.step(3)
        for spread_item in large:
            spread_item.share_far()
        scatter.finish(branch)
        own = rows(x, me)
        own_tokens = rows(dd, me)
        for copy in (keep_x, keep_raw, keep_heads):
            copy.wait()

        def tell(i):
            pl.semaphore_signal(ready.at[i], 1, device_id=other(dc=1), device_id_type=MESH)

        @tiles(128, 32)
        def _(r):
            b = branch[r, :]
            scale = lax.rsqrt(jnp.mean(b * b, 1, keepdims=True) + EPS)
            value = own_tokens[r, :].astype(F32) + b * scale * attn_gain[...]
            residual[r, :] = value
            own[r, :] = value.astype(BF16)

        gather = GatherTensor(x, *gather_sems)
        gather.start()
        down_weights.forward()
        for spread_item in large:
            spread_item.finish()

        def gate_up(slot):
            s = pl.ds(pl.multiple_of(slot * 128, 128), 128)

            @tiles(1024, 512)
            def _(n):
                gate = nn(x[s, :], wg[:, n])
                up = nn(x[s, :], wu[:, n])
                sigmoid = jax.nn.sigmoid(gate)
                low = gate * sigmoid
                silu[s, n] = low.astype(BF16)
                gate_factor[s, n] = (up * (sigmoid + low * (1.0 - sigmoid))).astype(BF16)
                inner[s, n] = (low * up).astype(BF16)

        def spread_down(stage):
            if stage == 0:
                down_weights.share()
                down_weights.forward_far()
            elif stage == 1:
                down_weights.share_far()
        gather.run(gate_up, spread_down)
        down_weights.finish()

        def down(first_row):
            s = pl.ds(pl.multiple_of(first_row, 256), 256)

            @pl.loop(0, 2)
            def _(i):
                n = pl.ds(pl.multiple_of(i * 1024, 1024), 1024)
                part[s, n] = nn(inner[s, :], wd[:, n]).astype(BF16)

        scatter = ScatterTensor(part, bufs, *scatter_sems)
        scatter.run(down)
        scatter.step(0)

        @pl.loop(0, 2)
        def _(h):
            near = pl.ds(pl.multiple_of(h * 1024, 1024), 512)
            far = pl.ds(pl.multiple_of(h * 1024 + 512, 512), 512)
            wd[0:512, near] = wd[0:512, near].T
            wd[512:1024, far] = wd[512:1024, far].T
            corner = wd[0:512, far].T
            wd[0:512, far] = wd[512:1024, near].T
            wd[512:1024, near] = corner

        for n in range(1, 4):
            scatter.step(n)
        scatter.finish(total)
        mlp_part[...] = jnp.zeros_like(mlp_part)
        attn_part[...] = jnp.zeros_like(attn_part)
        own_d = rows(dd, me)

        @tiles(128, 32)
        def _(r):
            v = total[r, :]
            position = lax.broadcasted_iota(jnp.int32, (32, 1), 0) + (me * 128 + r.start)
            ok = position < length
            scale = lax.rsqrt(jnp.mean(v * v, 1, keepdims=True) + EPS)
            normal = v * scale
            part[r, :] = jnp.where(ok, residual[r, :] + normal * mlp_gain[...], 0.0).astype(BF16)
            grad = jnp.where(ok, cotangent[r, :].astype(F32), 0.0)
            residual[r, :] = grad
            mlp_part[...] += jnp.sum(grad * normal, 0, keepdims=True)
            weighted = mlp_gain[...] * grad
            mean = jnp.mean(v * weighted, 1, keepdims=True)
            own_d[r, :] = (scale * weighted - v * (scale * scale * scale * mean)).astype(BF16)

        gather = GatherTensor(dd, *gather_sems)
        gather.start()
        store_act = pltpu.make_async_copy(part.at[pl.ds(0, 128)], act, msem.at[1])
        store_act.start()

        def d_inner(slot):
            s = pl.ds(pl.multiple_of(slot * 128, 128), 128)

            @pl.loop(0, 2)
            def _(i):
                n = pl.ds(pl.multiple_of(i * 512, 512), 512)
                beyond = pl.ds(pl.multiple_of(1024 + i * 512, 512), 512)
                d = nn(dd[s, 0:1024], wd[:, n]) + nn(dd[s, 1024:2048], wd[:, beyond])
                dg[s, n] = (d * gate_factor[s, n].astype(F32)).astype(BF16)
                du[s, n] = (d * silu[s, n].astype(F32)).astype(BF16)

        gather.run(d_inner)
        store_act.wait()
        tell(0)

        def d_input(first_row):
            s = pl.ds(pl.multiple_of(first_row, 256), 256)

            @pl.loop(0, 2)
            def _(i):
                n = pl.ds(pl.multiple_of(i * 1024, 1024), 1024)
                part[s, n] = (nt(dg[s, :], wg[n, :]) + nt(du[s, :], wu[n, :])).astype(BF16)

        scatter = ScatterTensor(part, bufs, *scatter_sems)
        scatter.run(d_input)
        scatter.step(0)

        def down_grad(i):
            m = pl.ds(i * 512, 512)

            @tiles(2048, 512)
            def _(n):
                wd[m, n] = tn(inner[:, m], dd[:, n]).astype(BF16)

        def gate_grad(first):
            @pl.loop(first, first + 2)
            def _(i):
                m = pl.ds(pl.multiple_of(i * 512, 512), 512)

                @tiles(1024, 512)
                def _(n):
                    wg[m, n] = tn(x[:, m], dg[:, n]).astype(BF16)

        down_grad(0)
        down_grad(1)
        scatter.step(1)
        tell(1)

        def by_rows(ref):
            return lambda n: ref.at[pl.ds(n * 128, 128)]

        def by_columns(ref):
            return lambda n: ref.at[:, pl.ds(n * 128, 128)]

        small_slots = [by_rows(gate_factor.at[:, pl.ds(256 * i, 256)]) for i in range(3)]
        small_slots.append(
            lambda n: gate_factor.at[
                pl.ds(n // 2 * 256, 256), pl.ds(768 + n % 2 * 128, 128)
            ]
        )
        slots = small_slots + [by_rows(silu), by_rows(inner), by_columns(gate_factor)]
        wholes = (wq, wk, silu, wo, wg, wu, wd)
        scatter_kinds = kinds[:2] + ("folded",) + kinds[3:]
        items = [ScatterDp(wholes[i], scatter_kinds[i], slots[i], *dp_bufs[i]) for i in range(7)]
        qk, value_item, out_item, gate_item, up_item, down_item = items[:2], *items[2:]
        pl.semaphore_wait(ready.at[0], 1)
        down_item.start()
        scatter.step(2)
        gate_grad(0)
        scatter.step(3)
        gate_grad(2)
        gate_item.start()
        load_heads.start()
        down_item.along_x()
        tell(2)
        scatter.finish(total)

        @tiles(128, 32)
        def _(r):
            grad = residual[r, :] + total[r, :]
            residual[r, :] = grad
            b = branch[r, :]
            scale = lax.rsqrt(jnp.mean(b * b, 1, keepdims=True) + EPS)
            attn_part[...] += jnp.sum(grad * b * scale, 0, keepdims=True)
            weighted = attn_gain[...] * grad
            mean = jnp.mean(b * weighted, 1, keepdims=True)
            own_d[r, :] = (scale * weighted - b * (scale * scale * scale * mean)).astype(BF16)

        gather = GatherTensor(dd, *gather_sems, 768)
        gather.start()


        @tiles(2048, 512)
        def _(m):
            @tiles(1024, 512)
            def _(n):
                wu[m, n] = tn(x[:, m], du[:, n]).astype(BF16)

        reload.start()
        load_raw.start()
        gate_item.along_x()
        pl.semaphore_wait(ready.at[1], 1)
        up_item.start()
        dk[...] = jnp.zeros_like(dk)
        dv[...] = jnp.zeros_like(dv)

        def attend_back(wanted):
            for i in range(4):

                @pl.when(wanted == i)
                def _():
                    @pl.loop(0, 2)
                    def _(h):
                        cols = pl.ds(pl.multiple_of(h * 128, 128), 128)
                        low = i * 256
                        block = slice(low, low + 256)
                        q, d = q_rot[block, cols], do[block, cols]
                        peak = jnp.where(h == 0, stats[block, 0:1], stats[block, 64:65])
                        k1, v1 = k_rot[block, cols], v_low[block, cols]
                        p1 = jnp.exp(diagonal_mask(nt(q, k1), low, length) - peak)
                        dp1 = nt(d, v1)
                        delta = jnp.sum(p1 * dp1, 1, keepdims=True)
                        if i:
                            k0, v0 = k_rot[0:low, cols], v_low[0:low, cols]
                            p0 = jnp.exp(nt(q, k0) - peak)
                            dp0 = nt(d, v0)
                            delta += jnp.sum(p0 * dp0, 1, keepdims=True)
                        ds1 = (p1 * (dp1 - delta)).astype(BF16)
                        dq_block = nn(ds1, k1)
                        dk[block, cols] += tn(ds1, q)
                        dv[block, cols] += tn(p1.astype(BF16), d)
                        if i:
                            ds0 = (p0 * (dp0 - delta)).astype(BF16)
                            dq_block += nn(ds0, k0)
                            dk[0:low, cols] += tn(ds0, q)
                            dv[0:low, cols] += tn(p0.astype(BF16), d)
                        dq[block, cols] = dq_block

        def d_mixed(slot):
            s = pl.ds(pl.multiple_of(slot * 128, 128), 128)
            do[s, :] = nt(dd[s, :], wo[...]).astype(BF16)

        def beside(stage):
            if stage == 0:
                down_item.forward()
                load_heads.wait()
            elif stage == 1:
                gate_item.forward()
                up_item.along_x()
            else:
                down_item.along_y()

        gather.run(d_mixed, beside, attend_back)
        load_raw.wait()

        q_line[...] = jnp.zeros_like(q_line)
        k_line[...] = jnp.zeros_like(k_line)
        sums[me] = jnp.zeros((8, 256), F32)

        @tiles(1024, 256)
        def _(r):
            cos, sin = cos_sin(table[r, :])
            for source, rawer, gain, s, factor, line in (
                (dq, q_raw, q_gain, 128, SCALE, q_line),
                (dk, k_raw, k_gain, 192, 1.0, k_line),
            ):
                scale = stats[r, s : s + 1]
                for h in (0, 128):
                    v = source[r, h : h + 128] * factor
                    v = v * cos - pltpu.roll(v, 64, 1) * sin
                    w = v * rawer[r, h : h + 128].astype(F32)
                    line[:, h : h + 128] += jnp.sum(w * scale, 0, keepdims=True)
                    source[r, h : h + 128] = v * gain[:, h : h + 128]
            note_sums(
                sums.at[me],
                r,
                dq[r, :] * q_raw[r, :].astype(F32),
                dk[r, :] * k_raw[r, :].astype(F32),
            )
            dvr[r, :] = dv[r, :].astype(BF16)

        exchange = Exchange(sums, *sum_sems)
        exchange.start()
        reload.wait()
        row = lax.broadcasted_iota(jnp.int32, (8, 1024), 0)
        column = lax.broadcasted_iota(jnp.int32, (8, 1024), 1)
        message = jnp.zeros((8, 1024), F32)
        for k, line in enumerate((attn_part, attn_part, mlp_part, mlp_part)):
            line = line[:, 1024 * (k % 2) : 1024 * (k % 2) + 1024]
            message = jnp.where(row == 4 + k, line, message)
        for first_row, line in ((0, q_line), (2, k_line)):
            line = jnp.concatenate([line[...]] * 4, 1)
            message += jnp.where((row == first_row + yl) & (column // 256 == z), line, 0.0)
        gain_slots[me] = message
        total_gain = SumAll(gain_slots, gain_hold, gain_boxes, *isems)

        @pl.loop(0, 4)
        def _(i):
            m = pl.ds(pl.multiple_of(i * 512, 512), 512)
            r = pl.ds(pl.multiple_of(lax.rem(i, 2) * 512, 512), 512)
            columns = pl.ds(pl.multiple_of(i // 2 * 256, 256), 256)
            silu[r, columns] = tn(x[:, m], dvr[...]).astype(BF16)

        pl.semaphore_wait(ready.at[2], 1)
        value_item.start()
        exchange.finish()
        total_gain.start()
        gate_item.along_y()
        spread(dv, exchange.sum() * (1.0 / 2048))

        def d_tokens(first_row):
            s = pl.ds(pl.multiple_of(first_row, 256), 256)
            for source, rawer, k, target in ((dq, q_raw, 0, dqr), (dk, k_raw, 128, dkr)):
                scale = stats[s, 128 + k // 2 : 129 + k // 2]
                factor = scale * scale * scale * dv[s, k : k + 128]
                for h in (0, 128):
                    target[s, h : h + 128] = (
                        scale * source[s, h : h + 128]
                        - rawer[s, h : h + 128].astype(F32) * factor
                    ).astype(BF16)

            @pl.loop(0, 2)
            def _(i):
                n = pl.ds(pl.multiple_of(i * 1024, 1024), 1024)
                terms = nt(dqr[s, :], wq[n, :]) + nt(dkr[s, :], wk[n, :]) + nt(dvr[s, :], wv[n, :])
                part[s, n] = terms.astype(BF16)

        scatter = ScatterTensor(part, bufs, *scatter_sems, 640)
        scatter.run(d_tokens)
        up_item.forward()

        @tiles(2048, 512)
        def _(m):
            xt = x[:, m].T
            wq[m, :] = nn(xt, dqr[...]).astype(BF16)
            wk[m, :] = nn(xt, dkr[...]).astype(BF16)

        for item in qk:
            item.start()
        scatter.step(0)
        value_item.along_x()
        total_gain.core()

        @tiles(2048, 512)
        def _(n):
            wo[:, n] = tn(mixed[...], dd[:, n]).astype(BF16)

        out_item.start()
        scatter.step(2)
        value_item.forward()
        for item in qk:
            item.along_x()
        scatter.step(1)
        total_gain.along_x()
        out_item.along_x()
        up_item.along_y()
        scatter.step(3)
        for item in qk:
            item.forward()
        out_item.forward()
        value_item.along_y()
        total_gain.along_y()
        stores = []

        def store(item, source, target):
            item.finish(source)
            stores.append(pltpu.make_async_copy(source, target, lsem.at[len(stores)]))
            stores[-1].start()

        store(down_item, dv.at[:, pl.ds(0, 128)], o6)
        store(gate_item, gate_out, o4)
        for item in qk:
            item.along_y()
        out_item.along_y()
        scatter.finish(total)

        @tiles(128, 32)
        def _(r):
            total[r, :] += residual[r, :]

        stores.append(pltpu.make_async_copy(total, input_grad, lsem.at[len(stores)]))
        stores[-1].start()
        store(up_item, up_out, o5)
        total_gain.finish(gain_slots.at[0])
        for i, out in enumerate((q_sum, k_sum, attn_sum, mlp_sum)):
            gain_lines[i, :, 0:1024] = gain_slots[0, 2 * i : 2 * i + 1, :]
            gain_lines[i, :, 1024:2048] = gain_slots[0, 2 * i + 1 : 2 * i + 2, :]
            stores.append(pltpu.make_async_copy(gain_lines.at[i], out, lsem.at[len(stores)]))
            stores[-1].start()
        store(value_item, dk.at[pl.ds(256, 128)], o2)
        for i, out in enumerate((o0, o1)):
            store(qk[i], dk.at[pl.ds(128 * i, 128)], out)
        store(out_item, dv.at[pl.ds(0, 256), pl.ds(128, 128)], o3)
        for copy in stores:
            copy.wait()

    S = jax.ShapeDtypeStruct
    W = pltpu.VMEM
    scratch = [W((1024, 2048), BF16)] * 2 + [W((2048, 1024), BF16)] * 2 + [W((1024, 2048), BF16)]
    scratch += [W((1024, 1024), BF16)] * 5 + [W((1024, 2048), BF16)]
    scratch += [W((128, 2048), F32)] + [W((1, 2048), F32)] * 2 + [W((1, 256), F32)] * 2
    scratch += [W((2048, 256), BF16)] * 3 + [W((256, 2048), BF16)]
    scratch += [W((1024, 256), F32), W((128, 2048), F32), W((128, 2048), BF16)]
    scratch += [W((1024, 128), F32), W((4, 1, 2048), F32), W((128, 2048), F32)]
    scratch += [W((128, 1024), F32)] * 2 + [W((1024, 256), BF16)]
    scratch += [W((1024, 256), F32)] * 3
    scratch += [W((8, 8, 256), F32), W((8, 8, 1024), F32)] + [W((3, 8, 1024), F32), W((5, 8, 1024), F32)]
    scratch += ScatterTensor.scratch(640, CUT)
    for b in blocks:
        scratch += ScatterDp.scratch(b)
    scratch += [DMA, DMA((14,)), DMA, DMA((21,)), DMA, DMA((7,)), DMA((6,)), DMA((12,))]
    scratch += [DMA((7,)), DMA((7, 14))]
    scratch += [DMA((12,)), DMA((6,)), pltpu.SemaphoreType.REGULAR((3,))]
    return pl.pallas_call(
        layer_step,
        out_shape=[S((128, 2048), BF16), S((128, 2048), F32)]
        + [S(b, F32) for b in blocks]
        + [S((1, 2048), F32)] * 4
        + [S((1024, 2048), BF16), S((1024, 1024), BF16), S((1024, 512), BF16)],
        in_specs=[SMEM] + [VM] * 4 + [ANY] * 10,
        out_specs=[ANY] * 16,
        scratch_shapes=scratch,
        compiler_params=params(1),
        name="layer_step",
    )(lengths, *gains, tokens, cotangent, table, *weights)[:13]


def hand_over(*arrays):
    n = len(arrays)

    def hand_over_step(*refs):
        held, (lsem, ssem) = refs[2 * n : 3 * n], refs[3 * n :]
        loads = [pltpu.make_async_copy(refs[i], held[i], lsem.at[i]) for i in range(n)]
        stores = [pltpu.make_async_copy(held[i], refs[n + i], ssem.at[i]) for i in range(n)]
        for copy in loads:
            copy.start()
        for load, store in zip(loads, stores):
            load.wait()
            store.start()
        for copy in stores:
            copy.wait()

    return pl.pallas_call(
        hand_over_step,
        out_shape=[jax.ShapeDtypeStruct(a.shape, a.dtype) for a in arrays],
        in_specs=[ANY] * n,
        out_specs=[ANY] * n,
        scratch_shapes=[pltpu.VMEM(a.shape, a.dtype) for a in arrays] + [DMA((n,))] * 2,
        compiler_params=pltpu.CompilerParams(vmem_limit_bytes=63 << 20),
        name="hand_over_step",
    )(*arrays)


def local(
    tokens, lengths, w_query, w_key, w_value, w_out, w_gate, w_up, w_down,
    q_gain, k_gain, attn_gain, mlp_gain, cotangent,
):
    weights = (w_query, w_key, w_value, w_out, w_gate, w_up, w_down)
    gains = (q_gain[None], k_gain[None], attn_gain[None], mlp_gain[None])
    results = whole_layer(tokens[0], lengths, cotangent[0], gains, weights, rope_table())
    act, input_grad, *grads = hand_over(*results)
    return (act[None], input_grad[None], *grads[:7], *(g.reshape(2048) for g in grads[7:]))


def solution(mesh):
    return jax.shard_map(
        local,
        mesh=mesh,
        in_specs=(
            P("dp", "tensor", None),
            P("dp"),
            P("dp", "tensor"),
            P("dp", "tensor"),
            P("dp", "tensor"),
            P("tensor", "dp"),
            P("dp", "tensor"),
            P("dp", "tensor"),
            P("tensor", "dp"),
            P(),
            P(),
            P(),
            P(),
            P("dp", "tensor", None),
        ),
        out_specs=(
            P("dp", "tensor", None),
            P("dp", "tensor", None),
            P("dp", "tensor"),
            P("dp", "tensor"),
            P("dp", "tensor"),
            P("tensor", "dp"),
            P("dp", "tensor"),
            P("dp", "tensor"),
            P("tensor", "dp"),
            P(),
            P(),
            P(),
            P(),
        ),
        check_vma=False,
    )
```

```python
import jax
import jax.numpy as jnp
import numpy as np
from jax import lax
from jax.experimental import pallas as pl
from jax.experimental.pallas import tpu as pltpu
from jax.sharding import PartitionSpec as P

HEAD_DIM = 128
EPS = 1e-06
THETA = 500000.0
MESH = pl.DeviceIdType.MESH
BF16 = jnp.bfloat16
F32 = jnp.float32
ANY = pl.BlockSpec(memory_space=pl.ANY)
VM = pl.BlockSpec(memory_space=pltpu.VMEM)
DMA = pltpu.SemaphoreType.DMA
CUT = 896
WIDTH = 2048


def place():
    d = lax.axis_index("dp")
    t = lax.axis_index("tensor")
    return d // 8, lax.rem(d // 2, 4), lax.rem(d, 2), t // 4, lax.rem(t, 4)


def other(dyh=0, dx=0, dc=0, dyl=0, dz=0):
    yh, x, c, yl, z = place()
    return (
        lax.rem(yh + dyh, 2) * 8 + lax.rem(x + dx, 4) * 2 + lax.rem(c + dc, 2),
        lax.rem(yl + dyl, 2) * 4 + lax.rem(z + dz, 4),
    )


TENSOR_PEERS = (dict(dz=1), dict(dz=3), dict(dyl=1))
DP_PEERS = (dict(dx=1), dict(dx=2), dict(dx=3), dict(dyh=1), dict(dc=1))
SMEM = pl.BlockSpec(memory_space=pltpu.SMEM)


def greet(peers):
    barrier = pltpu.get_barrier_semaphore()
    for peer in peers:
        pl.semaphore_signal(barrier, 1, device_id=other(**peer), device_id_type=MESH)
    pl.semaphore_wait(barrier, len(peers))


def remote(src, dst, sems, index, peer):
    ssem, rsem = sems
    return pltpu.make_async_remote_copy(
        src_ref=src,
        dst_ref=dst,
        send_sem=ssem,
        recv_sem=rsem.at[index],
        device_id=other(**peer),
        device_id_type=MESH,
    )


def all_of(bytes_of, sem):
    pltpu.make_async_copy(bytes_of, bytes_of, sem).wait()


def rows(ref, slot):
    return ref.at[pl.ds(pl.multiple_of(slot * 128, 128), 128)]


def halves(ref):
    half = ref.shape[0] // 2
    return ref.at[pl.ds(0, half)], ref.at[pl.ds(half, half)]


def add_into(out, *terms):
    step = min(out.shape[0], 32 if out.shape[1] > 1024 else 64 if out.shape[1] > 128 else 128)

    @pl.loop(0, out.shape[0] // step)
    def _(i):
        r = pl.ds(pl.multiple_of(i * step, step), step)
        if len(terms) == 2 and out.dtype == BF16:
            out[r, :] = terms[0][r, :] + terms[1][r, :]
        else:
            total = terms[0][r, :].astype(F32)
            for term in terms[1:]:
                total += term[r, :].astype(F32)
            out[r, :] = total.astype(out.dtype)


class RingGather:
    COPIES = 6

    def __init__(self, block, axis, sems, base, source=None):
        up, down = {axis: 1}, {axis: 3}
        src = halves(block(0) if source is None else source)
        own, behind, ahead = halves(block(0)), halves(block(3)), halves(block(1))
        self.copies = [
            remote(src[0], own[0], sems, base, up),
            remote(src[1], own[1], sems, base + 1, down),
            remote(src[1], own[1], sems, base + 2, up),
            remote(src[0], own[0], sems, base + 3, down),
            remote(behind[0], behind[0], sems, base + 4, up),
            remote(ahead[1], ahead[1], sems, base + 4, down),
        ]
        self.furthest, self.far_sem = block(2), sems[1].at[base + 4]

    def start(self):
        for copy in self.copies[:4]:
            copy.start()

    def forward(self):
        for i in range(2):
            self.copies[i].wait_recv()
            self.copies[4 + i].start()

    def behind(self):
        self.copies[2].wait_recv()

    def ahead(self):
        self.copies[3].wait_recv()

    def far(self):
        all_of(self.furthest, self.far_sem)


class RingReduce:
    COPIES = 6

    @staticmethod
    def scratch(n, m):
        return [pltpu.VMEM((2, n // 2, m), BF16), pltpu.VMEM((2, n, m), BF16)]

    def __init__(self, block, axis, part, full, sems, base):
        up, down = {axis: 1}, {axis: 3}
        one, two, three = halves(block(1)), halves(block(2)), halves(block(3))
        from_behind, from_ahead = halves(full.at[0]), halves(full.at[1])
        self.adds = ((one[0], part.at[0]), (three[1], part.at[1]))
        self.terms = (block(0), full.at[0], full.at[1])
        self.full, self.full_sem = full, sems[1].at[base + 2]
        self.copies = [
            remote(two[0], part.at[0], sems, base, up),
            remote(two[1], part.at[1], sems, base + 1, down),
            remote(one[1], from_behind[1], sems, base + 2, up),
            remote(three[0], from_ahead[0], sems, base + 2, down),
            remote(one[0], from_behind[0], sems, base + 2, up),
            remote(three[1], from_ahead[1], sems, base + 2, down),
        ]

    def start(self):
        for copy in self.copies[:4]:
            copy.start()

    def forward(self):
        for i in range(2):
            self.copies[i].wait_recv()
            add_into(self.adds[i][0], *self.adds[i])
            self.copies[4 + i].start()

    def arrive(self):
        all_of(self.full, self.full_sem)


class GatherTensor:
    COPIES = 21

    def __init__(self, buf, ssem, rsem, cut=CUT):
        yh, x, c, yl, z = place()
        self.yl, self.z = yl, z
        self.sent, self.ssem = buf.at[pl.ds(0, 896)], ssem
        sems = (ssem, rsem)
        slot = lambda k, i: rows(buf, lax.rem(yl + k, 2) * 4 + lax.rem(z + i, 4))
        low = lambda ref: ref.at[:, pl.ds(0, cut)]
        high = lambda ref: ref.at[:, pl.ds(cut, WIDTH - cut)]
        self.ring = RingGather(lambda i: slot(0, i), "dz", sems, 0)
        self.pair_ring = RingGather(lambda i: high(slot(1, i)), "dz", sems, 6)
        own = slot(0, 0)
        pair = dict(dyl=1)
        self.high = remote(high(own), high(own), sems, 12, pair)
        self.low = []
        for n, i in enumerate((0, 3, 1, 2)):
            for half in halves(low(slot(0, i))):
                self.low.append(remote(half, half, sems, 13 + len(self.low), pair))

    def start(self):
        self.high.start()
        self.ring.start()
        self.low[0].start()
        self.low[1].start()

    def run(self, process, spare=None, by_block=None, early=None, first=3):
        yl, z = self.yl, self.z

        @pl.loop(0, 2)
        def _(k):
            @pl.when(k == 1)
            def _():
                self.ring.forward()
                self.low[2].start()
                self.low[5].start()
                if early is not None:
                    early()
                self.high.wait_recv()
                self.pair_ring.start()
                self.ring.behind()
                self.low[3].start()
                self.ring.ahead()
                self.low[4].start()
                self.low[0].wait_recv()
                self.low[1].wait_recv()

            process(lax.rem(yl + k, 2) * 4 + z)

        if spare is not None:
            spare(0)

        @pl.loop(0, 6 if by_block is None else 7)
        def _(j):
            if spare is not None:
                for stage, at in ((1, 3), (2, 5)):

                    @pl.when(j == at)
                    def _():
                        spare(stage)

            if by_block is not None:
                last = j // 6
                rest = 2 - 2 * yl + last * (1 - z // 2) + (1 - last) * (z // 2)

                @pl.when((j >= 5) | (j == first))
                def _():
                    @pl.loop(0, 3)
                    def _(t):
                        third = t // 2

                        @pl.when(((t < 2) & (j == first)) | ((t == 2) & (j >= 5)))
                        def _():
                            by_block((1 - third) * (2 * yl + t) + third * rest)

            @pl.when(j == 2)
            def _():
                self.ring.far()
                self.low[6].start()
                self.low[7].start()
                self.pair_ring.forward()

            @pl.when(j == 3)
            def _():
                self.pair_ring.behind()
                self.low[2].wait_recv()
                self.low[3].wait_recv()

            @pl.when(j == 4)
            def _():
                self.pair_ring.ahead()
                self.low[4].wait_recv()
                self.low[5].wait_recv()

            @pl.when(j == 5)
            def _():
                self.pair_ring.far()
                self.low[6].wait_recv()
                self.low[7].wait_recv()

            i = lax.rem(j, 3)
            step = (3 * i * i - 7 * i + 6) // 2

            @pl.when(j < 6)
            def _():
                process(lax.rem(yl + j // 3, 2) * 4 + lax.rem(z + step, 4))

        all_of(self.sent, self.ssem)


class ScatterTensor:
    COPIES = 23

    @staticmethod
    def scratch(least, most):
        return (
            [pltpu.VMEM((4, 128, most), BF16), pltpu.VMEM((128, WIDTH - least), BF16)]
            + RingReduce.scratch(128, most)
            + RingReduce.scratch(128, WIDTH - least) * 2
        )

    def __init__(self, part, bufs, ssem, rsem, cut=CUT):
        yh, x, c, yl, z = place()
        self.z = z
        narrow = lambda ref, n: ref.at[:, :, pl.ds(0, n)]
        wide = WIDTH - cut
        bufs = [
            narrow(bufs[0], cut),
            bufs[1].at[:, pl.ds(0, wide)],
            *(narrow(ref, cut) for ref in bufs[2:4]),
            *(narrow(ref, wide) for ref in bufs[4:]),
        ]
        self.yl = yl
        self.from_pair, self.last = bufs[0], bufs[1]
        self.sent, self.ssem = part.at[pl.ds(0, 896)], ssem
        sems = (ssem, rsem)
        slot = lambda k, i: rows(part, lax.rem(yl + k, 2) * 4 + lax.rem(z + i, 4))
        low = lambda k, i: slot(k, i).at[:, pl.ds(0, cut)]
        high = lambda k, i: slot(k, i).at[:, pl.ds(cut, wide)]
        self.cut = cut
        pair = dict(dyl=1)
        self.low = lambda i: low(0, i)
        self.low_ring = RingReduce(lambda i: low(0, i), "dz", bufs[2], bufs[3], sems, 0)
        self.pair_ring = RingReduce(lambda i: high(1, i), "dz", bufs[4], bufs[5], sems, 3)
        self.own_ring = RingReduce(lambda i: high(0, i), "dz", bufs[6], bufs[7], sems, 6)
        self.first = lambda i: remote(low(1, i), bufs[0].at[i], sems, 9 + i, pair)
        self.second = remote(high(1, 0), bufs[1], sems, 13, pair)

    def run(self, process):
        yl, z = self.yl, self.z

        @pl.loop(0, 4)
        def _(k):
            half = lax.rem(yl + 1 + k // 2, 2)
            process(half * 512 + lax.rem((z + 2) // 2 + k, 2) * 256)
            beside = 3 - 2 * lax.rem(z, 2)

            @pl.when(k == 0)
            def _():
                self.first(2).start()
                self.pair_ring.copies[0].start()
                self.pair_ring.copies[1].start()
                self.first(beside).start()

            @pl.when(k == 1)
            def _():
                self.first(4 - beside).start()
                self.pair_ring.copies[2].start()
                self.pair_ring.copies[3].start()
                self.first(0).start()

    def add_first(self, i):
        self.first(i).wait_recv()
        add_into(self.low(i), self.low(i), self.from_pair.at[i])

    def add_low(self, i):
        self.add_first(i)
        for k in (1, 3):

            @pl.when(i == k)
            def _():
                self.low_ring.copies[2 + k // 3].start()

    def step(self, n):
        beside = 3 - 2 * lax.rem(self.z, 2)
        if n == 0:
            self.pair_ring.forward()
            self.own_ring.start()
            self.add_first(2)
            self.low_ring.copies[0].start()
            self.low_ring.copies[1].start()
        if n == 1:
            self.own_ring.forward()
            self.add_low(beside)
        if n == 2:
            self.pair_ring.arrive()
            add_into(self.pair_ring.terms[0], *self.pair_ring.terms)
            self.second.start()
            self.add_low(4 - beside)
        if n == 3:
            self.low_ring.forward()
            self.add_first(0)

    def finish(self, out):
        self.own_ring.arrive()
        self.second.wait_recv()
        add_into(out.at[:, pl.ds(self.cut, WIDTH - self.cut)], *self.own_ring.terms, self.last)
        self.low_ring.arrive()
        add_into(out.at[:, pl.ds(0, self.cut)], *self.low_ring.terms)
        all_of(self.sent, self.ssem)


def block_of(ref, kind, slot):
    if kind == "row":
        size = ref.shape[0] // 16
        return ref.at[pl.ds(pl.multiple_of(slot * size, size), size)]
    if kind == "folded":
        return ref.at[
            pl.ds(pl.multiple_of(lax.rem(slot, 8) * 128, 128), 128),
            pl.ds(pl.multiple_of(slot // 8 * 256, 256), 256),
        ]
    size = ref.shape[1] // 16
    return ref.at[:, pl.ds(pl.multiple_of(slot * size, size), size)]


def some_of(ref, kind, count):
    if kind == "row":
        return ref.at[pl.ds(0, ref.shape[0] // 16 * count)]
    if kind == "folded":
        return ref.at[pl.ds(0, 64 * count), pl.ds(0, 512)]
    return ref.at[:, pl.ds(0, ref.shape[1] // 16 * count)]


class GatherDp:
    COPIES = 21

    def __init__(self, shard, out, kind, ssem, rsem, lsem):
        yh, x, c, yl, z = place()
        sems = (ssem, rsem)
        block = lambda k, i: block_of(
            out, kind, lax.rem(yh + k, 2) * 8 + lax.rem(x + i, 4) * 2 + c
        )
        self.sent, self.ssem = some_of(out, kind, 15), ssem
        self.local = pltpu.make_async_copy(shard, block(0, 0), lsem)
        self.ring = RingGather(lambda i: block(0, i), "dx", sems, 0, shard)
        self.far_ring = RingGather(lambda i: block(1, i), "dx", sems, 5)
        self.own_y = remote(shard, block(0, 0), sems, 10, dict(dyh=1))
        core = dict(dc=1)
        self.core = [remote(shard, block(0, 0), sems, 11, core)]
        for n in range(1, 8):
            ref = block(n // 4, n % 4)
            self.core.append(remote(ref, ref, sems, 11, core))
        self.shared, self.shared_sem = some_of(out, kind, 8), rsem.at[11]

    def start(self):
        self.ring.start()
        self.core[0].start()
        self.local.start()

    def forward(self):
        self.ring.forward()

    def forward_y(self):
        self.own_y.wait_recv()
        self.far_ring.start()
        self.core[4].start()

    def share(self):
        self.ring.behind()
        self.core[3].start()
        self.ring.ahead()
        self.core[1].start()
        self.ring.far()
        self.core[2].start()

    def forward_far(self):
        self.far_ring.forward()

    def share_far(self):
        self.far_ring.behind()
        self.core[7].start()
        self.far_ring.ahead()
        self.core[5].start()
        self.far_ring.far()
        self.core[6].start()

    def finish(self):
        all_of(self.shared, self.shared_sem)
        self.local.wait()
        all_of(self.sent, self.ssem)


class ScatterDp:
    COPIES = 21

    @staticmethod
    def scratch(block):
        return (
            [pltpu.VMEM(block, BF16)]
            + RingReduce.scratch(*block) * 2
            + [DMA, DMA((8,))]
        )

    def __init__(self, part, kind, from_core, from_y, h0, f0, h1, f1, ssem, rsem):
        yh, x, c, yl, z = place()
        sems = (ssem, rsem)
        self.from_core, self.from_y = from_core, from_y
        self.sent, self.ssem = some_of(part, kind, 15), ssem
        block = lambda k, i, d: block_of(
            part, kind, lax.rem(yh + k, 2) * 8 + lax.rem(x + i, 4) * 2 + d
        )
        self.block = lambda k, i: block(k, i, c)
        self.core = [
            remote(block(n // 4, n % 4, 1 - c), from_core(n), sems, 0, dict(dc=1))
            for n in range(8)
        ]
        self.ring = RingReduce(lambda i: block(0, i, c), "dx", h0, f0, sems, 1)
        self.far_ring = RingReduce(lambda i: block(1, i, c), "dx", h1, f1, sems, 4)
        self.last = remote(block(1, 0, c), from_y, sems, 7, dict(dyh=1))
        self.shared, self.shared_sem = some_of(part, kind, 8), rsem.at[0]

    def start(self):
        for n in (6, 5, 7, 4, 2, 1, 3, 0):
            self.core[n].start()

    def add_core(self, n):
        ref = self.block(n // 4, n % 4)
        add_into(ref, ref, self.from_core(n))

    def along_x(self):
        all_of(self.shared, self.shared_sem)
        for n in (6, 5, 7):
            self.add_core(n)
        self.far_ring.start()
        for n in (2, 1, 3):
            self.add_core(n)
        self.ring.start()
        for n in (4, 0):
            self.add_core(n)

    def forward(self):
        self.far_ring.forward()
        self.ring.forward()

    def along_y(self):
        self.far_ring.arrive()
        add_into(self.far_ring.terms[0], *self.far_ring.terms)
        self.last.start()

    def finish(self, out):
        self.ring.arrive()
        self.last.wait_recv()
        add_into(out, *self.ring.terms, self.from_y)
        all_of(self.sent, self.ssem)


def params(cid):
    return pltpu.CompilerParams(
        collective_id=cid, has_side_effects=True, vmem_limit_bytes=65400 << 10
    )


def nn(a, b):
    return jnp.dot(a, b, preferred_element_type=F32)


def nt(a, b):
    return lax.dot_general(a, b, (((1,), (1,)), ((), ())), preferred_element_type=F32)


def tn(a, b):
    return lax.dot_general(a, b, (((0,), (0,)), ((), ())), preferred_element_type=F32)


def tiles(count, size):
    def run(body):
        @pl.loop(0, count // size)
        def _(i):
            body(pl.ds(pl.multiple_of(i * size, size), size))

    return run


def rope_table():
    frequency = THETA ** (-(np.arange(64, dtype=np.float32) * np.float32(2.0) / np.float32(HEAD_DIM)))
    angles = np.arange(1024, dtype=np.float32)[:, None] * frequency.astype(np.float32)[None, :]
    cosine, sine = np.cos(angles), np.sin(angles)
    return np.concatenate([cosine, sine], 1).astype(np.float32)


def cos_sin(table):
    turned = pltpu.roll(table, 64, 1)
    first = lax.broadcasted_iota(jnp.int32, table.shape, 1) < 64
    return jnp.where(first, table, turned), jnp.where(first, -turned, table)


class Exchange:
    PEERS = tuple(dict(dz=a, dyl=b) for b in range(2) for a in range(4) if a or b)

    def __init__(self, buf, ssem, rsem):
        yh, x, c, yl, z = place()
        self.buf, self.ssem = buf, ssem
        self.mine = buf.at[yl * 4 + z]
        self.copies = [
            remote(self.mine, self.mine, (ssem, rsem), i, peer)
            for i, peer in enumerate(self.PEERS)
        ]

    def start(self):
        for copy in self.copies:
            copy.start()

    def finish(self):
        for copy in self.copies:
            copy.wait_recv()
        all_of(self.buf.at[pl.ds(0, 7)], self.ssem)

    def sum(self):
        total = self.buf[0]
        for i in range(1, 8):
            total += self.buf[i]
        return total


def row_sums(values):
    return nt(jnp.ones((8, values.shape[1]), F32), values)


def spread(out, pair):
    row = lax.broadcasted_iota(jnp.int32, (8, 256), 0)
    column = lax.broadcasted_iota(jnp.int32, (8, 256), 1)
    for i in range(4):
        pick = jnp.where(row == column // 128 * 4 + i, 1.0, 0.0)
        out[pl.ds(256 * i, 256), :] = lax.dot_general(
            pair,
            pick,
            (((0,), (0,)), ((), ())),
            precision=lax.Precision.HIGHEST,
            preferred_element_type=F32,
        )


def note_sums(out, r, a, b):
    row = lax.broadcasted_iota(jnp.int32, (8, 256), 0)
    sums = jnp.where(row < 4, row_sums(a), row_sums(b))
    out[...] = jnp.where(lax.rem(row, 4) == r.start // 256, sums, out[...])


ALL_PEERS = Exchange.PEERS + DP_PEERS
SCALE = HEAD_DIM**-0.5


def diagonal_mask(scores, first, length):
    row = lax.broadcasted_iota(jnp.int32, scores.shape, 0)
    column = lax.broadcasted_iota(jnp.int32, scores.shape, 1)
    return jnp.where((column <= row) & (column + first < length), scores, -1e30)


class SumAll:
    def __init__(self, slots, hold, boxes, ssem, rsem):
        self.exchange = Exchange(slots, ssem.at[5], rsem)
        self.hold, self.boxes = hold, boxes
        self.copies = []
        for i, peer in enumerate(DP_PEERS):
            k = (1, 1, 1, 2, 0)[i]
            self.copies.append(remote(hold.at[k], boxes.at[i], (ssem.at[i], rsem), 7 + i, peer))

    def start(self):
        self.exchange.start()

    def core(self):
        self.exchange.finish()
        self.hold[0] = self.exchange.sum()
        self.copies[4].start()

    def along_x(self):
        self.copies[4].wait()
        self.hold[1] = self.hold[0] + self.boxes[4]
        for copy in self.copies[:3]:
            copy.start()

    def along_y(self):
        for copy in self.copies[:3]:
            copy.wait()
        self.hold[2] = self.hold[1] + self.boxes[0] + self.boxes[1] + self.boxes[2]
        self.copies[3].start()

    def finish(self, out):
        self.copies[3].wait()
        out[...] = self.hold[2] + self.boxes[3]


def whole_layer(tokens, lengths, cotangent, gains, weights, table):
    kinds = ("row", "row", "row", "col", "row", "row", "col")
    blocks = ((128, 256),) * 3 + ((256, 128), (128, 1024), (128, 1024), (1024, 128))

    def layer_step(
        lengths, q_gain_all, k_gain_all, attn_gain, mlp_gain, tokens, cotangent_in, table_in, i0, i1, i2, i3, i4, i5, i6,
        act, input_grad, o0, o1, o2, o3, o4, o5, o6,
        q_sum, k_sum, attn_sum, mlp_sum, x_kept, heads_kept, raw_kept,
        x, dd, wg, wu, wd, gate_factor, silu, inner, dg, du, part, residual, attn_part, mlp_part, q_line, k_line,
        wq, wk, wv, wo, stats, branch, cotangent, table, gain_lines, total, gate_out, up_out, do, dq, dk, dv, sums, gain_slots, gain_hold, gain_boxes,
        *rest,
    ):
        bufs, rest = rest[:8], rest[8:]
        dp_bufs, rest = [rest[7 * i : 7 * i + 7] for i in range(7)], rest[49:]
        scatter_sems, gather_sems, sum_sems, isems, wsems = [
            rest[2 * i : 2 * i + 2] for i in range(5)
        ]
        lsem, msem, ready = rest[10:]
        yh, xx, c, yl, z = place()
        me = yl * 4 + z
        length = lengths[0]
        own_columns = pl.ds(pl.multiple_of(me * 256, 256), 256)
        q_gain, k_gain = q_gain_all[:, own_columns], k_gain_all[:, own_columns]
        q_rot, k_rot, v_low, mixed = (dg.at[:, pl.ds(256 * i, 256)] for i in range(4))
        q_raw, k_raw, dvr = (du.at[:, pl.ds(256 * i, 256)] for i in range(3))
        dqr, dkr = q_raw, k_raw
        raw = du.at[:, pl.ds(0, 512)]
        load_heads = pltpu.make_async_copy(heads_kept, dg, msem.at[0])
        load_raw = pltpu.make_async_copy(raw_kept, raw, msem.at[2])
        reload = pltpu.make_async_copy(x_kept, x, msem.at[1])
        keep_x = pltpu.make_async_copy(dd, x_kept, msem.at[1])
        keep_heads = pltpu.make_async_copy(dg, heads_kept, msem.at[0])
        keep_raw = pltpu.make_async_copy(raw, raw_kept, msem.at[2])
        first = pltpu.make_async_copy(tokens, rows(dd, me), msem.at[3])
        first.start()
        load_table = pltpu.make_async_copy(table_in, table, msem.at[4])
        load_cotangent = pltpu.make_async_copy(cotangent_in, cotangent, msem.at[5])
        load_table.start()
        load_cotangent.start()
        greet(ALL_PEERS)
        shards = (i0, i1, i2, i3, i4, i5, i6)
        targets = (wq, wk, wv, wo, wg, wu, wd)
        spreads = [
            GatherDp(shards[i], targets[i], kinds[i], wsems[0].at[i], wsems[1].at[i], lsem.at[i])
            for i in range(7)
        ]
        small, large, down_weights = spreads[:4], spreads[4:6], spreads[6]
        for spread_item in small:
            spread_item.start()
            spread_item.own_y.start()
        first.wait()
        gather = GatherTensor(dd, *gather_sems, 384)
        gather.start()

        sums[me] = jnp.zeros((8, 256), F32)

        def forward_small():
            for spread_item in small:
                spread_item.forward()
                spread_item.forward_y()

        def spread_small(stage):
            for spread_item in small:
                if stage == 0:
                    spread_item.share()
                    spread_item.forward_far()
                elif stage == 1:
                    spread_item.share_far()
                else:
                    spread_item.finish()
            if stage == 1:
                down_weights.own_y.start()
            if stage == 2:
                for spread_item in large:
                    spread_item.start()
                large[0].own_y.start()

        def heads(i):
            r = pl.ds(pl.multiple_of(i * 256, 256), 256)
            q = nn(dd[r, :], wq[...])
            k = nn(dd[r, :], wk[...])
            dq[r, :] = q
            dk[r, :] = k
            du[r, 0:256] = q.astype(BF16)
            du[r, 256:512] = k.astype(BF16)
            v_low[r, :] = nn(dd[r, :], wv[...]).astype(BF16)
            note_sums(sums.at[me], r, q * q, k * k)

        gather.run(lambda slot: None, spread_small, heads, forward_small, 5)
        keep_x.start()
        exchange = Exchange(sums, *sum_sems)
        exchange.start()
        keep_raw.start()
        load_table.wait()
        load_cotangent.wait()
        exchange.finish()
        large[1].own_y.start()
        for spread_item in large:
            spread_item.forward()
        large[0].forward_y()
        spread(dv, lax.rsqrt(exchange.sum() * (1.0 / 2048) + EPS))
        narrow = lax.broadcasted_iota(jnp.int32, (1024, 128), 1) < 64
        stats[:, 128:256] = jnp.where(narrow, dv[:, 0:128], dv[:, 128:256])

        @tiles(1024, 256)
        def _(r):
            cos, sin = cos_sin(table[r, :])
            for source, gain, s, target, factor in (
                (dq, q_gain, 0, q_rot, SCALE),
                (dk, k_gain, 128, k_rot, 1.0),
            ):
                scale = dv[r, s : s + 128]
                for h in (0, 128):
                    v = source[r, h : h + 128] * scale * gain[:, h : h + 128]
                    v = v * cos + pltpu.roll(v, 64, 1) * sin
                    target[r, h : h + 128] = (v * factor).astype(BF16)

        def attend(wanted):
            for i in range(4):

                @pl.when(wanted == i)
                def _():
                    @pl.loop(0, 2)
                    def _(h):
                        cols = pl.ds(pl.multiple_of(h * 128, 128), 128)
                        mine = lax.broadcasted_iota(jnp.int32, (256, 128), 1) // 64 == h
                        low = i * 256
                        block = slice(low, low + 256)
                        q = q_rot[block, cols]
                        near = diagonal_mask(nt(q, k_rot[block, cols]), low, length)
                        peak = jnp.max(near, 1, keepdims=True)
                        if i:
                            past = nt(q, k_rot[0:low, cols])
                            peak = jnp.maximum(peak, jnp.max(past, 1, keepdims=True))
                        e1 = jnp.exp(near - peak)
                        denom = jnp.sum(e1, 1, keepdims=True)
                        out = nn(e1.astype(BF16), v_low[block, cols])
                        if i:
                            e0 = jnp.exp(past - peak)
                            denom += jnp.sum(e0, 1, keepdims=True)
                            out += nn(e0.astype(BF16), v_low[0:low, cols])
                        mixed[block, cols] = (out / denom).astype(BF16)
                        lse = peak + jnp.log(denom)
                        stats[block, 0:128] = jnp.where(mine, lse, stats[block, 0:128])

        def project(first_row):
            attend(first_row // 256)
            s = pl.ds(pl.multiple_of(first_row, 256), 256)

            @pl.loop(0, 2)
            def _(i):
                n = pl.ds(pl.multiple_of(i * 1024, 1024), 1024)
                part[s, n] = nn(mixed[s, :], wo[:, n]).astype(BF16)

        scatter = ScatterTensor(part, bufs, *scatter_sems)
        scatter.run(project)
        keep_heads.start()
        large[1].forward_y()
        scatter.step(0)
        for spread_item in large:
            spread_item.share()
        scatter.step(1)
        for spread_item in large:
            spread_item.forward_far()
        down_weights.start()
        down_weights.forward_y()
        scatter.step(2)
        scatter.step(3)
        for spread_item in large:
            spread_item.share_far()
        scatter.finish(branch)
        own = rows(x, me)
        own_tokens = rows(dd, me)
        for copy in (keep_x, keep_raw, keep_heads):
            copy.wait()

        def tell(i):
            pl.semaphore_signal(ready.at[i], 1, device_id=other(dc=1), device_id_type=MESH)

        @tiles(128, 32)
        def _(r):
            b = branch[r, :]
            scale = lax.rsqrt(jnp.mean(b * b, 1, keepdims=True) + EPS)
            value = own_tokens[r, :].astype(F32) + b * scale * attn_gain[...]
            residual[r, :] = value
            own[r, :] = value.astype(BF16)

        gather = GatherTensor(x, *gather_sems)
        gather.start()
        down_weights.forward()
        for spread_item in large:
            spread_item.finish()

        def gate_up(slot):
            s = pl.ds(pl.multiple_of(slot * 128, 128), 128)

            @tiles(1024, 512)
            def _(n):
                gate = nn(x[s, :], wg[:, n])
                up = nn(x[s, :], wu[:, n])
                sigmoid = jax.nn.sigmoid(gate)
                low = gate * sigmoid
                silu[s, n] = low.astype(BF16)
                gate_factor[s, n] = (up * (sigmoid + low * (1.0 - sigmoid))).astype(BF16)
                inner[s, n] = (low * up).astype(BF16)

        def spread_down(stage):
            if stage == 0:
                down_weights.share()
                down_weights.forward_far()
            elif stage == 1:
                down_weights.share_far()
        gather.run(gate_up, spread_down)
        down_weights.finish()

        def down(first_row):
            s = pl.ds(pl.multiple_of(first_row, 256), 256)

            @pl.loop(0, 2)
            def _(i):
                n = pl.ds(pl.multiple_of(i * 1024, 1024), 1024)
                part[s, n] = nn(inner[s, :], wd[:, n]).astype(BF16)

        scatter = ScatterTensor(part, bufs, *scatter_sems)
        scatter.run(down)
        scatter.step(0)

        @pl.loop(0, 2)
        def _(h):
            near = pl.ds(pl.multiple_of(h * 1024, 1024), 512)
            far = pl.ds(pl.multiple_of(h * 1024 + 512, 512), 512)
            wd[0:512, near] = wd[0:512, near].T
            wd[512:1024, far] = wd[512:1024, far].T
            corner = wd[0:512, far].T
            wd[0:512, far] = wd[512:1024, near].T
            wd[512:1024, near] = corner

        for n in range(1, 4):
            scatter.step(n)
        scatter.finish(total)
        mlp_part[...] = jnp.zeros_like(mlp_part)
        attn_part[...] = jnp.zeros_like(attn_part)
        own_d = rows(dd, me)

        @tiles(128, 32)
        def _(r):
            v = total[r, :]
            position = lax.broadcasted_iota(jnp.int32, (32, 1), 0) + (me * 128 + r.start)
            ok = position < length
            scale = lax.rsqrt(jnp.mean(v * v, 1, keepdims=True) + EPS)
            normal = v * scale
            part[r, :] = jnp.where(ok, residual[r, :] + normal * mlp_gain[...], 0.0).astype(BF16)
            grad = jnp.where(ok, cotangent[r, :].astype(F32), 0.0)
            residual[r, :] = grad
            mlp_part[...] += jnp.sum(grad * normal, 0, keepdims=True)
            weighted = mlp_gain[...] * grad
            mean = jnp.mean(v * weighted, 1, keepdims=True)
            own_d[r, :] = (scale * weighted - v * (scale * scale * scale * mean)).astype(BF16)

        gather = GatherTensor(dd, *gather_sems)
        gather.start()
        store_act = pltpu.make_async_copy(part.at[pl.ds(0, 128)], act, msem.at[1])
        store_act.start()

        def d_inner(slot):
            s = pl.ds(pl.multiple_of(slot * 128, 128), 128)

            @pl.loop(0, 2)
            def _(i):
                n = pl.ds(pl.multiple_of(i * 512, 512), 512)
                beyond = pl.ds(pl.multiple_of(1024 + i * 512, 512), 512)
                d = nn(dd[s, 0:1024], wd[:, n]) + nn(dd[s, 1024:2048], wd[:, beyond])
                dg[s, n] = (d * gate_factor[s, n].astype(F32)).astype(BF16)
                du[s, n] = (d * silu[s, n].astype(F32)).astype(BF16)

        gather.run(d_inner)
        store_act.wait()
        tell(0)

        def d_input(first_row):
            s = pl.ds(pl.multiple_of(first_row, 256), 256)

            @pl.loop(0, 2)
            def _(i):
                n = pl.ds(pl.multiple_of(i * 1024, 1024), 1024)
                part[s, n] = (nt(dg[s, :], wg[n, :]) + nt(du[s, :], wu[n, :])).astype(BF16)

        scatter = ScatterTensor(part, bufs, *scatter_sems)
        scatter.run(d_input)
        scatter.step(0)

        def down_grad(i):
            m = pl.ds(i * 512, 512)

            @tiles(2048, 1024)
            def _(n):
                wd[m, n] = tn(inner[:, m], dd[:, n]).astype(BF16)

        def gate_grad(first):
            @pl.loop(first, first + 2)
            def _(i):
                m = pl.ds(pl.multiple_of(i * 512, 512), 512)
                wg[m, :] = tn(x[:, m], dg[...]).astype(BF16)

        down_grad(0)
        down_grad(1)
        scatter.step(1)
        tell(1)

        def by_rows(ref):
            return lambda n: ref.at[pl.ds(n * 128, 128)]

        def by_columns(ref):
            return lambda n: ref.at[:, pl.ds(n * 128, 128)]

        small_slots = [by_rows(gate_factor.at[:, pl.ds(256 * i, 256)]) for i in range(3)]
        small_slots.append(
            lambda n: gate_factor.at[
                pl.ds(n // 2 * 256, 256), pl.ds(768 + n % 2 * 128, 128)
            ]
        )
        slots = small_slots + [by_rows(silu), by_rows(inner), by_columns(gate_factor)]
        wholes = (wq, wk, silu, wo, wg, wu, wd)
        scatter_kinds = kinds[:2] + ("folded",) + kinds[3:]
        items = [ScatterDp(wholes[i], scatter_kinds[i], slots[i], *dp_bufs[i]) for i in range(7)]
        qk, value_item, out_item, gate_item, up_item, down_item = items[:2], *items[2:]
        pl.semaphore_wait(ready.at[0], 1)
        down_item.start()
        scatter.step(2)
        gate_grad(0)
        scatter.step(3)
        gate_grad(2)
        gate_item.start()
        load_heads.start()
        down_item.along_x()
        tell(2)
        scatter.finish(total)

        @tiles(128, 32)
        def _(r):
            grad = residual[r, :] + total[r, :]
            residual[r, :] = grad
            b = branch[r, :]
            scale = lax.rsqrt(jnp.mean(b * b, 1, keepdims=True) + EPS)
            attn_part[...] += jnp.sum(grad * b * scale, 0, keepdims=True)
            weighted = attn_gain[...] * grad
            mean = jnp.mean(b * weighted, 1, keepdims=True)
            own_d[r, :] = (scale * weighted - b * (scale * scale * scale * mean)).astype(BF16)

        gather = GatherTensor(dd, *gather_sems, 768)
        gather.start()


        @tiles(2048, 512)
        def _(m):
            wu[m, :] = tn(x[:, m], du[...]).astype(BF16)

        reload.start()
        load_raw.start()
        gate_item.along_x()
        pl.semaphore_wait(ready.at[1], 1)
        up_item.start()
        dk[...] = jnp.zeros_like(dk)
        dv[...] = jnp.zeros_like(dv)

        def attend_back(wanted):
            for i in range(4):

                @pl.when(wanted == i)
                def _():
                    @pl.loop(0, 2)
                    def _(h):
                        cols = pl.ds(pl.multiple_of(h * 128, 128), 128)
                        low = i * 256
                        block = slice(low, low + 256)
                        q, d = q_rot[block, cols], do[block, cols]
                        peak = jnp.where(h == 0, stats[block, 0:1], stats[block, 64:65])
                        k1, v1 = k_rot[block, cols], v_low[block, cols]
                        p1 = jnp.exp(diagonal_mask(nt(q, k1), low, length) - peak)
                        dp1 = nt(d, v1)
                        delta = jnp.sum(p1 * dp1, 1, keepdims=True)
                        if i:
                            k0, v0 = k_rot[0:low, cols], v_low[0:low, cols]
                            p0 = jnp.exp(nt(q, k0) - peak)
                            dp0 = nt(d, v0)
                            delta += jnp.sum(p0 * dp0, 1, keepdims=True)
                        ds1 = (p1 * (dp1 - delta)).astype(BF16)
                        dq_block = nn(ds1, k1)
                        dk[block, cols] += tn(ds1, q)
                        dv[block, cols] += tn(p1.astype(BF16), d)
                        if i:
                            ds0 = (p0 * (dp0 - delta)).astype(BF16)
                            dq_block += nn(ds0, k0)
                            dk[0:low, cols] += tn(ds0, q)
                            dv[0:low, cols] += tn(p0.astype(BF16), d)
                        dq[block, cols] = dq_block

        def d_mixed(slot):
            s = pl.ds(pl.multiple_of(slot * 128, 128), 128)
            do[s, :] = nt(dd[s, :], wo[...]).astype(BF16)

        def beside(stage):
            if stage == 0:
                down_item.forward()
                load_heads.wait()
            elif stage == 1:
                gate_item.forward()
                up_item.along_x()
            else:
                down_item.along_y()

        gather.run(d_mixed, beside, attend_back)
        load_raw.wait()

        q_line[...] = jnp.zeros_like(q_line)
        k_line[...] = jnp.zeros_like(k_line)
        sums[me] = jnp.zeros((8, 256), F32)

        @tiles(1024, 256)
        def _(r):
            cos, sin = cos_sin(table[r, :])
            for source, rawer, gain, s, factor, line in (
                (dq, q_raw, q_gain, 128, SCALE, q_line),
                (dk, k_raw, k_gain, 192, 1.0, k_line),
            ):
                scale = stats[r, s : s + 1]
                for h in (0, 128):
                    v = source[r, h : h + 128] * factor
                    v = v * cos - pltpu.roll(v, 64, 1) * sin
                    w = v * rawer[r, h : h + 128].astype(F32)
                    line[:, h : h + 128] += jnp.sum(w * scale, 0, keepdims=True)
                    source[r, h : h + 128] = v * gain[:, h : h + 128]
            note_sums(
                sums.at[me],
                r,
                dq[r, :] * q_raw[r, :].astype(F32),
                dk[r, :] * k_raw[r, :].astype(F32),
            )
            dvr[r, :] = dv[r, :].astype(BF16)

        exchange = Exchange(sums, *sum_sems)
        exchange.start()
        reload.wait()
        row = lax.broadcasted_iota(jnp.int32, (8, 1024), 0)
        column = lax.broadcasted_iota(jnp.int32, (8, 1024), 1)
        message = jnp.zeros((8, 1024), F32)
        for k, line in enumerate((attn_part, attn_part, mlp_part, mlp_part)):
            line = line[:, 1024 * (k % 2) : 1024 * (k % 2) + 1024]
            message = jnp.where(row == 4 + k, line, message)
        for first_row, line in ((0, q_line), (2, k_line)):
            line = jnp.concatenate([line[...]] * 4, 1)
            message += jnp.where((row == first_row + yl) & (column // 256 == z), line, 0.0)
        gain_slots[me] = message
        total_gain = SumAll(gain_slots, gain_hold, gain_boxes, *isems)

        @pl.loop(0, 4)
        def _(i):
            m = pl.ds(pl.multiple_of(i * 512, 512), 512)
            r = pl.ds(pl.multiple_of(lax.rem(i, 2) * 512, 512), 512)
            columns = pl.ds(pl.multiple_of(i // 2 * 256, 256), 256)
            silu[r, columns] = tn(x[:, m], dvr[...]).astype(BF16)

        pl.semaphore_wait(ready.at[2], 1)
        value_item.start()
        exchange.finish()
        total_gain.start()
        gate_item.along_y()
        spread(dv, exchange.sum() * (1.0 / 2048))

        def d_tokens(first_row):
            s = pl.ds(pl.multiple_of(first_row, 256), 256)
            for source, rawer, k, target in ((dq, q_raw, 0, dqr), (dk, k_raw, 128, dkr)):
                scale = stats[s, 128 + k // 2 : 129 + k // 2]
                factor = scale * scale * scale * dv[s, k : k + 128]
                for h in (0, 128):
                    target[s, h : h + 128] = (
                        scale * source[s, h : h + 128]
                        - rawer[s, h : h + 128].astype(F32) * factor
                    ).astype(BF16)

            @pl.loop(0, 2)
            def _(i):
                n = pl.ds(pl.multiple_of(i * 1024, 1024), 1024)
                terms = nt(dqr[s, :], wq[n, :]) + nt(dkr[s, :], wk[n, :]) + nt(dvr[s, :], wv[n, :])
                part[s, n] = terms.astype(BF16)

        scatter = ScatterTensor(part, bufs, *scatter_sems, 640)
        scatter.run(d_tokens)
        up_item.forward()

        @tiles(2048, 512)
        def _(m):
            xt = x[:, m].T
            wq[m, :] = nn(xt, dqr[...]).astype(BF16)
            wk[m, :] = nn(xt, dkr[...]).astype(BF16)

        for item in qk:
            item.start()
        scatter.step(0)
        value_item.along_x()
        total_gain.core()

        @tiles(2048, 512)
        def _(n):
            wo[:, n] = tn(mixed[...], dd[:, n]).astype(BF16)

        out_item.start()
        scatter.step(2)
        value_item.forward()
        for item in qk:
            item.along_x()
        scatter.step(1)
        total_gain.along_x()
        out_item.along_x()
        up_item.along_y()
        scatter.step(3)
        for item in qk:
            item.forward()
        out_item.forward()
        value_item.along_y()
        total_gain.along_y()
        stores = []

        def store(item, source, target):
            item.finish(source)
            stores.append(pltpu.make_async_copy(source, target, lsem.at[len(stores)]))
            stores[-1].start()

        store(down_item, dv.at[:, pl.ds(0, 128)], o6)
        store(gate_item, gate_out, o4)
        for item in qk:
            item.along_y()
        out_item.along_y()
        scatter.finish(total)

        @tiles(128, 32)
        def _(r):
            total[r, :] += residual[r, :]

        stores.append(pltpu.make_async_copy(total, input_grad, lsem.at[len(stores)]))
        stores[-1].start()
        store(up_item, up_out, o5)
        total_gain.finish(gain_slots.at[0])
        for i, out in enumerate((q_sum, k_sum, attn_sum, mlp_sum)):
            gain_lines[i, :, 0:1024] = gain_slots[0, 2 * i : 2 * i + 1, :]
            gain_lines[i, :, 1024:2048] = gain_slots[0, 2 * i + 1 : 2 * i + 2, :]
            stores.append(pltpu.make_async_copy(gain_lines.at[i], out, lsem.at[len(stores)]))
            stores[-1].start()
        store(value_item, dk.at[pl.ds(256, 128)], o2)
        for i, out in enumerate((o0, o1)):
            store(qk[i], dk.at[pl.ds(128 * i, 128)], out)
        store(out_item, dv.at[pl.ds(0, 256), pl.ds(128, 128)], o3)
        for copy in stores:
            copy.wait()

    S = jax.ShapeDtypeStruct
    W = pltpu.VMEM
    scratch = [W((1024, 2048), BF16)] * 2 + [W((2048, 1024), BF16)] * 2 + [W((1024, 2048), BF16)]
    scratch += [W((1024, 1024), BF16)] * 5 + [W((1024, 2048), BF16)]
    scratch += [W((128, 2048), F32)] + [W((1, 2048), F32)] * 2 + [W((1, 256), F32)] * 2
    scratch += [W((2048, 256), BF16)] * 3 + [W((256, 2048), BF16)]
    scratch += [W((1024, 256), F32), W((128, 2048), F32), W((128, 2048), BF16)]
    scratch += [W((1024, 128), F32), W((4, 1, 2048), F32), W((128, 2048), F32)]
    scratch += [W((128, 1024), F32)] * 2 + [W((1024, 256), BF16)]
    scratch += [W((1024, 256), F32)] * 3
    scratch += [W((8, 8, 256), F32), W((8, 8, 1024), F32)] + [W((3, 8, 1024), F32), W((5, 8, 1024), F32)]
    scratch += ScatterTensor.scratch(640, CUT)
    for b in blocks:
        scratch += ScatterDp.scratch(b)
    scratch += [DMA, DMA((14,)), DMA, DMA((21,)), DMA, DMA((7,)), DMA((6,)), DMA((12,))]
    scratch += [DMA((7,)), DMA((7, 12))]
    scratch += [DMA((12,)), DMA((6,)), pltpu.SemaphoreType.REGULAR((3,))]
    return pl.pallas_call(
        layer_step,
        out_shape=[S((128, 2048), BF16), S((128, 2048), F32)]
        + [S(b, F32) for b in blocks]
        + [S((1, 2048), F32)] * 4
        + [S((1024, 2048), BF16), S((1024, 1024), BF16), S((1024, 512), BF16)],
        in_specs=[SMEM] + [VM] * 4 + [ANY] * 10,
        out_specs=[ANY] * 16,
        scratch_shapes=scratch,
        compiler_params=params(1),
        name="layer_step",
    )(lengths, *gains, tokens, cotangent, table, *weights)[:13]


def hand_over(*arrays):
    n = len(arrays)

    def hand_over_step(*refs):
        held, (lsem, ssem) = refs[2 * n : 3 * n], refs[3 * n :]
        loads = [pltpu.make_async_copy(refs[i], held[i], lsem.at[i]) for i in range(n)]
        stores = [pltpu.make_async_copy(held[i], refs[n + i], ssem.at[i]) for i in range(n)]
        for copy in loads:
            copy.start()
        for load, store in zip(loads, stores):
            load.wait()
            store.start()
        for copy in stores:
            copy.wait()

    return pl.pallas_call(
        hand_over_step,
        out_shape=[jax.ShapeDtypeStruct(a.shape, a.dtype) for a in arrays],
        in_specs=[ANY] * n,
        out_specs=[ANY] * n,
        scratch_shapes=[pltpu.VMEM(a.shape, a.dtype) for a in arrays] + [DMA((n,))] * 2,
        compiler_params=pltpu.CompilerParams(vmem_limit_bytes=63 << 20),
        name="hand_over_step",
    )(*arrays)


def local(
    tokens, lengths, w_query, w_key, w_value, w_out, w_gate, w_up, w_down,
    q_gain, k_gain, attn_gain, mlp_gain, cotangent,
):
    weights = (w_query, w_key, w_value, w_out, w_gate, w_up, w_down)
    gains = (q_gain[None], k_gain[None], attn_gain[None], mlp_gain[None])
    results = whole_layer(tokens[0], lengths, cotangent[0], gains, weights, rope_table())
    act, input_grad, *grads = hand_over(*results)
    return (act[None], input_grad[None], *grads[:7], *(g.reshape(2048) for g in grads[7:]))


def solution(mesh):
    return jax.shard_map(
        local,
        mesh=mesh,
        in_specs=(
            P("dp", "tensor", None),
            P("dp"),
            P("dp", "tensor"),
            P("dp", "tensor"),
            P("dp", "tensor"),
            P("tensor", "dp"),
            P("dp", "tensor"),
            P("dp", "tensor"),
            P("tensor", "dp"),
            P(),
            P(),
            P(),
            P(),
            P("dp", "tensor", None),
        ),
        out_specs=(
            P("dp", "tensor", None),
            P("dp", "tensor", None),
            P("dp", "tensor"),
            P("dp", "tensor"),
            P("dp", "tensor"),
            P("tensor", "dp"),
            P("dp", "tensor"),
            P("dp", "tensor"),
            P("tensor", "dp"),
            P(),
            P(),
            P(),
            P(),
        ),
        check_vma=False,
    )
```
